32 devices in a mesh: grp: 2 (over y), side: 4 (over z), shard: 4 (over x, core).
Axes of the slice: x: 2, y: 2, z: 4, core: 2. Of those that a mesh axis runs over, the one named last changes fastest.
Arguments:
- queries: bfloat16 [480, 8192], P(('grp', 'side', 'shard')), parts along dimension 0, may hold values from -6.5 to 6.5
- new_kv: bfloat16 [480, 2048], P(('grp', 'side', 'shard')), parts along dimension 0, may hold values from -4.5 to 4.5
- kv_pool: bfloat16 [3584, 16, 2048], P(('grp', 'side', 'shard')), parts along dimension 0, may hold values from -4.5 to 4.5
- page_table: int32 [480, 16], P(('grp', 'side', 'shard')), parts along dimension 0, may hold values from 0 to 111, as said below
- ctx_len: int32 [480], P(('grp', 'side', 'shard')), parts along dimension 0, may hold values from 0 to 256, as said below
- residual_in: bfloat16 [480, 8192], P(('grp', 'side', 'shard')), parts along dimension 0, may hold values from -6 to 6
- norm_gain: bfloat16 [8192], replicated, may hold values from 0.5 to 1.5
- w_up: bfloat16 [8192, 16384], P('side', 'shard'), may hold values from -0.0625 to 0.0625
- w_down: bfloat16 [16384, 8192], P('shard', 'side'), may hold values from -0.046875 to 0.046875
Outputs:
- layer_out: bfloat16 [480, 8192], P(('grp', 'side', 'shard')), parts along dimension 0
The draws below stay inside these ranges and needn't reach their ends.
There are 2 independent parts, one for each index of `grp`. The reference program is written for one: setup_inputs(seed, part) draws one part's arguments, and reference() takes and returns one part's arrays. A program takes and returns all parts, laid end to end along the dimension named above; an argument that names none is the same for every part. Nothing has to cross between parts.
Inputs may be any that keep to these rules, and one draw needn't show every extreme that they name: `ctx_len`: on one device's 15 slots, 3 to 12 have a nonzero length, exactly 12 on some device; a live slot's pages together hold at most 112 pages on its device; every device has a slot of length 256. `page_table`: the first ceil(ctx_len / 16) entries of a live slot name distinct pages, and no page is named by two live slots of one device; other entries name valid pages.
All inputs are finite; a program needn't handle non-finite values.
Results may differ from the reference program's by a relative error of at most 0.009.
Values may be sent and summed in bfloat16 or wider, within the bound.
No kernel may reach another device: no remote copies, remote signals or barrier semaphores. Data moves between devices by JAX's collectives and lax.ppermute only.
A program may use at most 128 MiB of HBM per device.

```python
import math
import jax
import jax.numpy as jnp
from jax import lax

D = 8192
FF = 16384
HEADS = 64
KV_HEADS = 8
HEAD = 128
PAGE = 16
MAXP = 16
POOL = 112
LIVE_CAP = 12
SLOT_DEV = 15
GROUP = 8
ATT_DEVS = 16
SLOTS = 240
POOLS = 1792


def layout(key):
    local_key = jax.random.fold_in(key, 501)
    device_total = SLOTS // SLOT_DEV
    chosen = jax.random.randint(jax.random.fold_in(local_key, 1), (), 0, device_total, dtype=jnp.int32)
    device_keys = jax.random.split(jax.random.fold_in(local_key, 2), device_total)

    def one_device(device_key, device_id):
        key_count, key_rank, key_want, key_tail, key_pages = jax.random.split(device_key, 5)
        live_count = jax.random.randint(key_count, (), LIVE_CAP // 4, LIVE_CAP + 1, dtype=jnp.int32)
        live_count = jnp.where(device_id == chosen, LIVE_CAP, live_count).astype(jnp.int32)
        shuffled = jax.random.permutation(key_rank, SLOT_DEV).astype(jnp.int32)
        slot_rank = jnp.argsort(shuffled).astype(jnp.int32)
        rank_slot = jnp.argsort(slot_rank).astype(jnp.int32)
        wanted = jax.random.randint(key_want, (SLOT_DEV,), 1, MAXP + 1, dtype=jnp.int32)
        tails = jax.random.randint(key_tail, (SLOT_DEV,), 1, PAGE + 1, dtype=jnp.int32)
        page_order = jax.random.permutation(key_pages, POOL).astype(jnp.int32)

        def place(used, position):
            slot_here = rank_slot[position]
            want_here = jnp.where(position == 0, MAXP, wanted[slot_here]).astype(jnp.int32)
            room_left = (POOL - used - (live_count - 1 - position)).astype(jnp.int32)
            taken = jnp.where(position < live_count, jnp.minimum(want_here, room_left), 0).astype(jnp.int32)
            return ((used + taken).astype(jnp.int32), (used, taken))
        unused, placed = lax.scan(place, jnp.int32(0), jnp.arange(SLOT_DEV, dtype=jnp.int32))
        starts_rank, taken_rank = placed
        tail_rank = jnp.where(jnp.arange(SLOT_DEV, dtype=jnp.int32) == 0, PAGE, tails[rank_slot]).astype(jnp.int32)
        length_rank = jnp.where(taken_rank > 0, (taken_rank - 1) * PAGE + tail_rank, 0).astype(jnp.int32)
        lengths = length_rank[slot_rank]
        starts = starts_rank[slot_rank]
        entry = (starts[:, None] + jnp.arange(MAXP, dtype=jnp.int32)[None, :]) % POOL
        return (lengths, page_order[entry])
    lengths, tables = jax.vmap(one_device)(device_keys, jnp.arange(device_total, dtype=jnp.int32))
    return (lengths.reshape(SLOTS).astype(jnp.int32), tables.reshape(SLOTS, MAXP).astype(jnp.int32))


def draw_ctx_len(key, part):
    return layout(key)[0]


def draw_page_table(key, part):
    return layout(key)[1]


def draw_queries(key, part):
    own_key = jax.random.fold_in(key, 11)
    return jax.random.truncated_normal(own_key, -4.5, 4.5, (SLOTS, HEADS * HEAD), jnp.float32).astype(jnp.bfloat16)


def draw_new_kv(key, part):
    own_key = jax.random.fold_in(key, 12)
    return jax.random.truncated_normal(own_key, -4.5, 4.5, (SLOTS, 2 * KV_HEADS * HEAD), jnp.float32).astype(jnp.bfloat16)


def draw_kv_pool(key, part):
    own_key = jax.random.fold_in(key, 13)
    return jax.random.truncated_normal(own_key, -4.5, 4.5, (POOLS, PAGE, 2 * KV_HEADS * HEAD), jnp.float32).astype(jnp.bfloat16)


def steps_of(stream_key, shape, shards, smallest, high):
    def one(axis_at, parts):
        heights = jax.random.uniform(jax.random.fold_in(jax.random.fold_in(stream_key, 6), axis_at), (parts,), jnp.float32, smallest / len(shards), high / len(shards))
        return jnp.repeat(jnp.exp(heights), shape[axis_at] // parts).reshape((-1,) + (1,) * (len(shape) - axis_at - 1))

    loudness = one(*shards[0])
    for cut in shards[1:]:
        loudness = loudness * one(*cut)
    return loudness


def bell_draw(key, extent, deviation, bound, cuts=(), kind=jnp.bfloat16):
    loudness = steps_of(key, extent, cuts, -0.22, 0.18) if cuts else 1.0
    drawn = jax.random.normal(key, extent, jnp.float32) * deviation * loudness
    return jnp.minimum(jnp.maximum(drawn, -bound), bound).astype(kind)


def setup_inputs(seed: int = 0, part: int = 0) -> dict:
    arg_keys = jax.random.split(jax.random.key(seed), 10)
    part_keys = jax.random.split(jax.random.fold_in(arg_keys[9], part), 10)
    queries = draw_queries(jax.random.fold_in(jax.random.fold_in(arg_keys[9], part), 71), part)
    new_kv = draw_new_kv(jax.random.fold_in(jax.random.fold_in(arg_keys[9], part), 71), part)
    kv_pool = draw_kv_pool(jax.random.fold_in(jax.random.fold_in(arg_keys[9], part), 71), part)
    page_table = draw_page_table(jax.random.fold_in(jax.random.fold_in(arg_keys[9], part), 71), part)
    ctx_len = draw_ctx_len(jax.random.fold_in(jax.random.fold_in(arg_keys[9], part), 71), part)
    residual_in = bell_draw(part_keys[5], (SLOTS, D), 1.0, 6.0, ((0, 16),))
    norm_gain = jnp.clip(1.0 + 0.1 * jax.random.normal(arg_keys[6], (D,), jnp.float32), 0.5, 1.5).astype(jnp.bfloat16)
    w_up = bell_draw(arg_keys[7], (D, FF), D ** -0.5, 0.0625, ((0, 4), (1, 4)))
    w_down = bell_draw(arg_keys[8], (FF, D), FF ** -0.5, 0.046875, ((0, 4), (1, 4)))
    return dict(queries=queries, new_kv=new_kv, kv_pool=kv_pool, page_table=page_table, ctx_len=ctx_len, residual_in=residual_in, norm_gain=norm_gain, w_up=w_up, w_down=w_down)


epsilon = 1e-05

def attend_slots(queries, new_kv, pool_pages, page_rows, lengths):
    slot_count = queries.shape[0]
    positions = page_rows.shape[1] * pool_pages.shape[1]
    fetched = pool_pages[page_rows].reshape(slot_count, positions, 2, KV_HEADS, HEAD).astype(jnp.float32)
    fresh_kv = new_kv.reshape(slot_count, 2, KV_HEADS, HEAD).astype(jnp.float32)
    query_heads = queries.reshape(slot_count, KV_HEADS, GROUP, HEAD).astype(jnp.float32)
    score_scale = 1.0 / math.sqrt(HEAD)
    scores = jnp.einsum('sgqd,slgd->sgql', query_heads, fetched[:, :, 0]) * score_scale
    own_score = jnp.einsum('sgqd,sgd->sgq', query_heads, fresh_kv[:, 0]) * score_scale
    visible = (jnp.arange(positions, dtype=jnp.int32)[None, :] < lengths[:, None])[:, None, None, :]
    scores = jnp.where(visible, scores, -1e+30)
    highest = jnp.maximum(lax.optimization_barrier(jnp.max(scores, axis=-1)), own_score)
    weights = jnp.where(visible, jnp.exp(scores - highest[..., None]), 0.0)
    own_weight = jnp.exp(own_score - highest)
    denominator = lax.optimization_barrier(jnp.sum(weights, axis=-1)) + own_weight
    rounded = lax.optimization_barrier(((weights / denominator[..., None]).astype(jnp.bfloat16), (own_weight / denominator).astype(jnp.bfloat16)))
    probabilities = rounded[0].astype(jnp.float32)
    own_prob = rounded[1].astype(jnp.float32)
    attended = jnp.einsum('sgql,slgd->sgqd', probabilities, fetched[:, :, 1])
    attended = attended + own_prob[..., None] * fresh_kv[:, 1][:, :, None, :]
    return attended.reshape(slot_count, HEADS * HEAD)

def per_device(values):
    return values.reshape((ATT_DEVS, -1) + values.shape[1:])

def attend_device(operands):
    return attend_slots(operands[0], operands[1], operands[2], operands[3], operands[4])

def reference(queries, new_kv, kv_pool, page_table, ctx_len, residual_in, norm_gain, w_up, w_down):
    pools = kv_pool.reshape(ATT_DEVS, POOL, PAGE, 2 * KV_HEADS * HEAD)
    attended = lax.map(attend_device, (per_device(queries), per_device(new_kv), pools, per_device(page_table), per_device(ctx_len)))
    attended = attended.reshape(SLOTS, HEADS * HEAD)
    mixed_rows = residual_in.astype(jnp.float32) + attended
    mean_square = lax.optimization_barrier(jnp.mean(mixed_rows * mixed_rows, axis=-1, keepdims=True))
    normed = (mixed_rows * lax.rsqrt(mean_square + epsilon) * norm_gain.astype(jnp.float32)).astype(jnp.bfloat16)
    lifted = jnp.dot(normed, w_up, preferred_element_type=jnp.float32)
    clipped = jnp.maximum(lifted, 0.0)
    active = (clipped * clipped).astype(jnp.bfloat16)
    ffn_out = jnp.dot(active, w_down, preferred_element_type=jnp.float32)
    live_mask = (ctx_len > 0)[:, None]
    return (mixed_rows + jnp.where(live_mask, ffn_out, 0.0)).astype(jnp.bfloat16)
```

```python
import functools
import math

import jax
import jax.numpy as jnp
from jax import lax
from jax.experimental import pallas as pl
from jax.experimental.pallas import tpu as pltpu
from jax.sharding import PartitionSpec as P

KV_HEADS = 8
HEAD = 128
GROUP = 8
LIVE_CAP = 12
PAD = 16

epsilon = 1e-05
bf16, f32, i32 = jnp.bfloat16, jnp.float32, jnp.int32
VMEM_MB = 1 << 20


def params(mb, **more):
    return pltpu.CompilerParams(vmem_limit_bytes=mb * VMEM_MB, **more)


def cost(flops, bytes_accessed):
    return pl.CostEstimate(flops=int(flops), bytes_accessed=int(bytes_accessed), transcendentals=0)


def pad_rows(x):
    rows = x.shape[0]
    if rows == PAD:
        return x
    return jnp.concatenate([x, jnp.zeros((PAD - rows,) + x.shape[1:], x.dtype)], axis=0)


def live_ranks(lengths, slots):
    live, rank, count = [], [], jnp.int32(0)
    for slot in range(slots):
        alive = lengths[slot] > 0
        live.append(alive)
        rank.append(count)
        count = count + alive.astype(i32)
    return live, rank


def attend_kernel(
    lengths, where_side, q_ref, nk_ref, nv_ref, k_ref, v_ref, table_ref, res_ref, gain_ref, *rest
):
    sides = len(rest) - 3
    mixed_ref, sends, bias_ref, square_ref = rest[0], rest[1 : 1 + sides], rest[-2], rest[-1]
    head = pl.program_id(0)
    slots = q_ref.shape[0]
    pages, page = k_ref.shape[0], k_ref.shape[1]
    tokens = pages * page
    width = mixed_ref.shape[1]
    scale = math.log2(math.e) / math.sqrt(HEAD)

    @pl.when(head == 0)
    def _():
        lanes = 128 * ((pages + 127) // 128)
        row = lax.broadcasted_iota(i32, (PAD, lanes), 0)
        column = lax.broadcasted_iota(i32, (PAD, lanes), 1)
        reach = jnp.zeros((PAD, lanes), i32)
        for slot in range(slots):
            reach = jnp.where(row == slot, lengths[slot], reach)
        table = pad_rows(table_ref[...])
        seen = jnp.zeros((PAD, lanes), i32)
        for entry in range(table.shape[1]):
            here = jnp.minimum(jnp.maximum(reach - entry * page, 0), page)
            seen = seen + jnp.where(table[:, entry : entry + 1] == column, here, 0)
        spread = (
            lax.broadcasted_iota(i32, (lanes, tokens), 1) // page
            == lax.broadcasted_iota(i32, (lanes, tokens), 0)
        )
        seen_tokens = jnp.dot(
            seen.astype(f32).astype(bf16),
            spread.astype(f32).astype(bf16),
            preferred_element_type=f32,
        )
        place = (lax.broadcasted_iota(i32, (PAD, tokens), 1) % page).astype(f32)
        bias_ref[...] = jnp.where(place < seen_tokens, 0.0, -1e30)
        square_ref[...] = jnp.zeros_like(square_ref)

    q = jnp.concatenate(
        [pad_rows(q_ref[:, g * HEAD : (g + 1) * HEAD]) for g in range(GROUP)], axis=0
    )
    keys = k_ref[...].reshape(tokens, HEAD)
    values = v_ref[...].reshape(tokens, HEAD)
    new_key = pad_rows(nk_ref[...]).astype(f32)
    new_value = pad_rows(nv_ref[...]).astype(f32)
    scores = lax.dot_general(q, keys, (((1,), (1,)), ((), ())), preferred_element_type=f32)
    scores = scores.reshape(GROUP, PAD, tokens) * scale + bias_ref[...][None]
    own = jnp.sum(q.astype(f32).reshape(GROUP, PAD, HEAD) * new_key[None], axis=-1, keepdims=True)
    own = own * scale
    highest = jnp.maximum(jnp.max(scores, axis=-1, keepdims=True), own)
    weights = jnp.exp2(scores - highest)
    own_weight = jnp.exp2(own - highest)
    total = jnp.sum(weights, axis=-1, keepdims=True) + own_weight
    summed = jnp.dot(
        weights.astype(bf16).reshape(GROUP * PAD, tokens), values, preferred_element_type=f32
    ).reshape(GROUP, PAD, HEAD)
    attended = (summed + own_weight * new_value[None]) / total
    squares = jnp.zeros((slots, HEAD), f32)
    base = pl.multiple_of(head * (GROUP * HEAD), GROUP * HEAD)
    for g in range(GROUP):
        mixed = res_ref[:, g * HEAD : (g + 1) * HEAD].astype(f32) + attended[g][:slots]
        mixed_ref[:, pl.ds(base + g * HEAD, HEAD)] = mixed
        squares = squares + mixed * mixed
    square_ref[...] += squares

    @pl.when(head == KV_HEADS - 1)
    def _():
        live, rank = live_ranks(lengths, slots)
        row = lax.broadcasted_iota(i32, (PAD, PAD), 0)
        column = lax.broadcasted_iota(i32, (PAD, PAD), 1)
        pick = jnp.zeros((PAD, PAD), f32)
        for slot in range(slots):
            chosen = jnp.logical_and(row == rank[slot], column == slot)
            pick = jnp.where(jnp.logical_and(chosen, live[slot]), 1.0, pick)
        pick = pick.astype(bf16)
        root = lax.rsqrt(jnp.sum(square_ref[...], axis=-1, keepdims=True) / width + epsilon)
        step = width // sides
        for shift in range(sides):
            at = pl.multiple_of(lax.rem(where_side[0] + shift, sides) * step, step)
            normed = mixed_ref[:, pl.ds(at, step)] * root * gain_ref[:, pl.ds(at, step)].astype(f32)
            normed = pad_rows(normed.astype(bf16))
            sends[shift][...] = jnp.dot(pick, normed, preferred_element_type=f32).astype(bf16)


def attend(queries, new_kv, kv_pool, page_table, ctx_len, residual_in, norm_gain, side, sides):
    slots, width = queries.shape
    pages, page, _ = kv_pool.shape
    tokens = pages * page
    step = width // sides
    head_block = lambda g, *_: (0, g)
    fixed = lambda g, *_: (0, 0)
    return pl.pallas_call(
        attend_kernel,
        grid_spec=pltpu.PrefetchScalarGridSpec(
            num_scalar_prefetch=2,
            grid=(KV_HEADS,),
            in_specs=[
                pl.BlockSpec((slots, GROUP * HEAD), head_block),
                pl.BlockSpec((slots, HEAD), head_block),
                pl.BlockSpec((slots, HEAD), lambda g, *_: (0, KV_HEADS + g)),
                pl.BlockSpec((pages, page, HEAD), lambda g, *_: (0, 0, g)),
                pl.BlockSpec((pages, page, HEAD), lambda g, *_: (0, 0, KV_HEADS + g)),
                pl.BlockSpec(page_table.shape, fixed),
                pl.BlockSpec((slots, GROUP * HEAD), head_block),
                pl.BlockSpec((1, width), fixed),
            ],
            out_specs=[pl.BlockSpec((slots, width), fixed)]
            + [pl.BlockSpec((PAD, step), fixed)] * sides,
            scratch_shapes=[pltpu.VMEM((PAD, tokens), f32), pltpu.VMEM((slots, HEAD), f32)],
        ),
        out_shape=[jax.ShapeDtypeStruct((slots, width), f32)]
        + [jax.ShapeDtypeStruct((PAD, step), bf16)] * sides,
        compiler_params=params(24),
        cost_estimate=cost(4 * 8 * 128 * 128 * tokens, kv_pool.size * 2),
        name="attend",
    )(
        ctx_len, side, queries, new_kv, new_kv, kv_pool, kv_pool, page_table, residual_in,
        norm_gain.reshape(1, width),
    )


def pack_up_kernel(meta, *refs, parts):
    gathered, w_ref, packed_ref, out_ref = refs[:parts], refs[parts], refs[-2], refs[-1]
    rows = packed_ref.shape[0]

    @pl.when(pl.program_id(0) == 0)
    def _():
        per = gathered[0].shape[0]
        pieces = per // PAD
        total = jnp.zeros(packed_ref.shape, f32)
        for part in range(parts):
            lane = lax.broadcasted_iota(i32, (rows, per), 1)
            row = lax.broadcasted_iota(i32, (rows, per), 0)
            target = jnp.full((rows, per), -1, i32)
            for piece in range(pieces):
                base = meta[1 + part * pieces + piece]
                count = meta[1 + parts * pieces + part * pieces + piece]
                inside = lane - piece * PAD
                mine = jnp.logical_and(inside >= 0, inside < count)
                target = jnp.where(mine, base + inside, target)
            pick = (target == row).astype(f32).astype(bf16)
            total = total + jnp.dot(pick, gathered[part][...], preferred_element_type=f32)
        packed_ref[...] = total.astype(bf16)

    out_ref[...] = jnp.dot(packed_ref[...], w_ref[...], preferred_element_type=f32).astype(out_ref.dtype)


def up_kernel(meta, x_ref, w_ref, out_ref):
    out_ref[...] = jnp.dot(x_ref[...], w_ref[...], preferred_element_type=f32).astype(out_ref.dtype)


TILE = 256


def pack_up(meta, gathered, w_up, rows, block_width):
    depth = w_up.shape[0]
    tiles = block_width // TILE
    fixed = lambda t, *_: (0, 0)
    return pl.pallas_call(
        functools.partial(pack_up_kernel, parts=len(gathered)),
        grid_spec=pltpu.PrefetchScalarGridSpec(
            num_scalar_prefetch=1,
            grid=(tiles,),
            in_specs=[pl.BlockSpec(g.shape, fixed) for g in gathered]
            + [pl.BlockSpec((depth, TILE), lambda t, meta: (0, meta[0] * tiles + t))],
            out_specs=[
                pl.BlockSpec((rows, depth), fixed),
                pl.BlockSpec((rows, TILE), lambda t, *_: (0, t)),
            ],
        ),
        out_shape=[
            jax.ShapeDtypeStruct((rows, depth), bf16),
            jax.ShapeDtypeStruct((rows, block_width), bf16),
        ],
        compiler_params=params(24),
        cost_estimate=cost(2 * rows * depth * block_width, depth * block_width * 2),
        name="pack_up",
    )(meta, *gathered, w_up)


def up(meta, packed, w_up, block_width, dtype):
    rows, depth = packed.shape
    tiles = block_width // TILE
    return pl.pallas_call(
        up_kernel,
        grid_spec=pltpu.PrefetchScalarGridSpec(
            num_scalar_prefetch=1,
            grid=(tiles,),
            in_specs=[
                pl.BlockSpec((rows, depth), lambda t, *_: (0, 0)),
                pl.BlockSpec((depth, TILE), lambda t, meta: (0, meta[0] * tiles + t)),
            ],
            out_specs=pl.BlockSpec((rows, TILE), lambda t, *_: (0, t)),
        ),
        out_shape=jax.ShapeDtypeStruct((rows, block_width), dtype),
        compiler_params=params(16),
        cost_estimate=cost(2 * rows * depth * block_width, depth * block_width * 2),
        name="up",
    )(meta, packed, w_up)


def down_kernel(meta, *refs, first):
    a_ref, w_ref = refs[0], refs[1]
    out_ref = refs[-1]
    part = jnp.dot(a_ref[...], w_ref[...], preferred_element_type=f32)
    out_ref[...] = part if first else refs[2][...] + part


def down(meta, active, w_down, before):
    rows, depth = active.shape
    width = w_down.shape[1]
    tile = 512
    sums = pl.BlockSpec((rows, tile), lambda t, *_: (0, t))
    return pl.pallas_call(
        functools.partial(down_kernel, first=before is None),
        grid_spec=pltpu.PrefetchScalarGridSpec(
            num_scalar_prefetch=1,
            grid=(width // tile,),
            in_specs=[
                pl.BlockSpec((rows, depth), lambda t, *_: (0, 0)),
                pl.BlockSpec((depth, tile), lambda t, meta: (meta[0], t)),
            ]
            + ([] if before is None else [sums]),
            out_specs=sums,
        ),
        out_shape=jax.ShapeDtypeStruct((rows, width), f32),
        compiler_params=params(16),
        cost_estimate=cost(2 * rows * depth * width, depth * width * 2),
        name="down",
    )(meta, active, w_down, *([] if before is None else [before]))


def down_unpack_kernel(meta, a_ref, w_ref, before_ref, *outs):
    parts = len(outs)
    rows = a_ref.shape[0]
    pieces = outs[0].shape[0] // PAD
    share = before_ref[...] + jnp.dot(a_ref[...], w_ref[...], preferred_element_type=f32)
    share = share.astype(bf16)
    row = lax.broadcasted_iota(i32, (PAD, rows), 0)
    column = lax.broadcasted_iota(i32, (PAD, rows), 1)
    for part in range(parts):
        picks = []
        for piece in range(pieces):
            base = meta[1 + part * pieces + piece]
            count = meta[1 + parts * pieces + part * pieces + piece]
            picks.append(jnp.logical_and(column - row == base, row < count).astype(f32))
        pick = jnp.concatenate(picks, axis=0).astype(bf16)
        outs[part][...] = jnp.dot(pick, share, preferred_element_type=f32).astype(bf16)


def down_unpack(meta, active, w_down, before, parts, per):
    rows, depth = active.shape
    width = w_down.shape[1]
    tile = 512
    return pl.pallas_call(
        down_unpack_kernel,
        grid_spec=pltpu.PrefetchScalarGridSpec(
            num_scalar_prefetch=1,
            grid=(width // tile,),
            in_specs=[
                pl.BlockSpec((rows, depth), lambda t, *_: (0, 0)),
                pl.BlockSpec((depth, tile), lambda t, meta: (meta[0], t)),
                pl.BlockSpec((rows, tile), lambda t, *_: (0, t)),
            ],
            out_specs=[pl.BlockSpec((per, tile), lambda t, *_: (0, t))] * parts,
        ),
        out_shape=[jax.ShapeDtypeStruct((per, width), bf16)] * parts,
        compiler_params=params(16),
        cost_estimate=cost(2 * rows * depth * width, depth * width * 2),
        name="down_unpack",
    )(meta, active, w_down, before)


def finish_kernel(lengths, where_side, mixed_ref, *refs):
    blocks, out_ref = refs[:-1], refs[-1]
    sides = len(blocks)
    slots, width = out_ref.shape
    step = width // sides
    live, rank = live_ranks(lengths, slots)
    row = lax.broadcasted_iota(i32, (PAD, PAD), 0)
    column = lax.broadcasted_iota(i32, (PAD, PAD), 1)
    pick = jnp.zeros((PAD, PAD), f32)
    for slot in range(slots):
        chosen = jnp.logical_and(column == rank[slot], row == slot)
        pick = jnp.where(jnp.logical_and(chosen, live[slot]), 1.0, pick)
    pick = pick.astype(bf16)
    for shift in range(sides):
        at = pl.multiple_of(lax.rem(where_side[0] + shift, sides) * step, step)
        back = jnp.dot(pick, blocks[shift][...], preferred_element_type=f32)[:slots]
        out_ref[:, pl.ds(at, step)] = (mixed_ref[:, pl.ds(at, step)] + back).astype(bf16)


def finish(ctx_len, side, mixed, blocks):
    whole = pl.BlockSpec(memory_space=pltpu.VMEM)
    scalars = pl.BlockSpec(memory_space=pltpu.SMEM)
    return pl.pallas_call(
        finish_kernel,
        in_specs=[scalars, scalars, whole] + [whole] * len(blocks),
        out_specs=whole,
        out_shape=jax.ShapeDtypeStruct(mixed.shape, bf16),
        compiler_params=params(16),
        cost_estimate=cost(mixed.size * 32, mixed.size * 8),
        name="finish",
    )(ctx_len, side, mixed, *blocks)


def swap(x, axis, count, mask):
    return lax.ppermute(x, axis, [(j, j ^ mask) for j in range(count)])


def shifted(x, axis, count, shift):
    return lax.ppermute(x, axis, [(j, (j + shift) % count) for j in range(count)])


def added(a, b):
    return (a.astype(f32) + b.astype(f32)).astype(bf16)


def tie(x, *others):
    return lax.optimization_barrier((x, *others))[0]


def feed_forward(rows, meta_of, gathered, w_up, w_down):
    width = w_up.shape[1] // 4
    packed, far_partner = pack_up(meta_of(3), gathered, w_up, rows, width)
    met = swap(far_partner, "side", 4, 1)
    near = up(meta_of(1), packed, w_up, width, bf16)
    far = up(meta_of(2), packed, w_up, width, bf16)
    own = up(meta_of(0), packed, w_up, width, f32)
    pair_sum = added(far, met)
    crossed = swap(pair_sum, "side", 4, 2)
    near = swap(tie(near, met), "side", 4, 1)
    lifted = own + near.astype(f32) + crossed.astype(f32)
    clipped = jnp.maximum(lifted, 0.0)
    active = (clipped * clipped).astype(bf16)
    across = swap(active, "side", 4, 2)
    beside = swap(active, "side", 4, 1)
    forwarded = swap(across, "side", 4, 1)
    total = down(meta_of(0), active, w_down, None)
    total = down(meta_of(1), beside, w_down, total)
    total = down(meta_of(2), across, w_down, total)
    return down_unpack(meta_of(3), forwarded, w_down, total, len(gathered), gathered[0].shape[0])


def line_shards(
    queries, new_kv, kv_pool, page_table, ctx_len, residual_in, norm_gain, w_up, w_down
):
    i, s = lax.axis_index("side"), lax.axis_index("shard")
    side = i.reshape(1)
    count = jnp.sum((ctx_len > 0).astype(i32))
    counts = lax.all_gather(count.reshape(1), ("side", "shard"), axis=0, tiled=True)
    mixed, *sends = attend(
        queries, new_kv, kv_pool, page_table, ctx_len, residual_in, norm_gain, side, 4
    )
    arrived = {shift: shifted(sends[shift], "side", 4, shift) for shift in (2, 1, 3)}
    arrived[0] = sends[0]
    here = jnp.concatenate([arrived[shift] for shift in range(4)], axis=0)
    by_x = swap(here, "shard", 4, 2)
    by_core = swap(here, "shard", 4, 1)
    by_both = swap(by_x, "shard", 4, 1)
    gathered = [here, by_core, by_x, by_both]

    starts = jnp.cumsum(counts) - counts
    order = jnp.stack([((i - shift) % 4) * 4 + (s ^ q) for q in range(4) for shift in range(4)])
    layout = jnp.concatenate([starts[order], counts[order]])

    def meta_of(mask):
        return jnp.concatenate([(i ^ mask).reshape(1), layout]).astype(i32)

    rows = 4 * 4 * LIVE_CAP
    mine, for_core, for_x, for_both = feed_forward(rows, meta_of, gathered, w_up, w_down)
    back = swap(jnp.concatenate([for_core, for_both], axis=0), "shard", 4, 1)
    half = back.shape[0] // 2
    to_x = added(for_x, back[half:])
    kept = added(mine, back[:half])
    home = added(kept, swap(to_x, "shard", 4, 2)).reshape(4, PAD, -1)
    blocks = [home[0]] + [shifted(home[shift], "side", 4, -shift) for shift in (1, 2, 3)]
    return finish(ctx_len, side, mixed, blocks)


def attend_slots(queries, new_kv, pool_pages, page_rows, lengths):
    slot_count = queries.shape[0]
    positions = page_rows.shape[1] * pool_pages.shape[1]
    fetched = pool_pages[page_rows].reshape(slot_count, positions, 2, KV_HEADS, HEAD)
    fresh_kv = new_kv.reshape(slot_count, 2, KV_HEADS, HEAD)
    query_heads = queries.reshape(slot_count, KV_HEADS, GROUP, HEAD)
    score_scale = 1.0 / math.sqrt(HEAD)
    scores = (
        jnp.einsum("sgqd,slgd->sgql", query_heads, fetched[:, :, 0], preferred_element_type=f32)
        * score_scale
    )
    own_score = (
        jnp.einsum("sgqd,sgd->sgq", query_heads, fresh_kv[:, 0], preferred_element_type=f32)
        * score_scale
    )
    visible = (jnp.arange(positions, dtype=i32)[None, :] < lengths[:, None])[:, None, None, :]
    scores = jnp.where(visible, scores, -1e30)
    highest = jnp.maximum(jnp.max(scores, axis=-1), own_score)
    weights = jnp.where(visible, jnp.exp(scores - highest[..., None]), 0.0)
    own_weight = jnp.exp(own_score - highest)
    denominator = jnp.sum(weights, axis=-1) + own_weight
    probabilities = (weights / denominator[..., None]).astype(bf16)
    own_prob = (own_weight / denominator).astype(bf16).astype(f32)
    attended = jnp.einsum(
        "sgql,slgd->sgqd", probabilities, fetched[:, :, 1], preferred_element_type=f32
    )
    attended = attended + own_prob[..., None] * fresh_kv[:, 1].astype(f32)[:, :, None, :]
    return attended.reshape(slot_count, -1)


def any_shards(queries, new_kv, kv_pool, page_table, ctx_len, residual_in, norm_gain, w_up, w_down):
    attended = attend_slots(queries, new_kv, kv_pool, page_table, ctx_len)
    mixed_rows = residual_in.astype(f32) + attended
    mean_square = jnp.mean(mixed_rows * mixed_rows, axis=-1, keepdims=True)
    normed = (mixed_rows * lax.rsqrt(mean_square + epsilon) * norm_gain.astype(f32)).astype(bf16)
    live_mask = ctx_len > 0
    spread = lax.all_to_all(normed, "side", split_axis=1, concat_axis=0, tiled=True)
    up_partial = jnp.dot(
        lax.all_gather(spread, "shard", axis=0, tiled=True), w_up, preferred_element_type=f32
    )
    lifted = lax.psum(up_partial, "side")
    clipped = jnp.maximum(lifted, 0.0)
    active = (clipped * clipped).astype(bf16)
    down_share = lax.psum_scatter(
        jnp.dot(active, w_down, preferred_element_type=f32).astype(bf16),
        "shard",
        scatter_dimension=0,
        tiled=True,
    )
    returned = lax.all_to_all(down_share, "side", split_axis=0, concat_axis=1, tiled=True)
    returned = jnp.where(live_mask[:, None], returned.astype(f32), 0.0)
    return (mixed_rows + returned).astype(bf16)


def solution(mesh):
    rows = ("grp", "side", "shard")
    placed = (
        P(rows, None),
        P(rows, None),
        P(rows, None, None),
        P(rows, None),
        P(rows),
        P(rows, None),
        P(),
        P("side", "shard"),
        P("shard", "side"),
    )
    square = mesh.shape["side"] == 4 and mesh.shape["shard"] == 4
    return jax.shard_map(
        line_shards if square else any_shards,
        mesh=mesh,
        in_specs=placed,
        out_specs=P(rows, None),
        check_vma=False,
    )
```

```python
import functools
import math

import jax
import jax.numpy as jnp
from jax import lax
from jax.experimental import pallas as pl
from jax.experimental.pallas import tpu as pltpu
from jax.sharding import PartitionSpec as P

KV_HEADS = 8
HEAD = 128
GROUP = 8
LIVE_CAP = 12
PAD = 16

epsilon = 1e-05
bf16, f32, i32 = jnp.bfloat16, jnp.float32, jnp.int32
VMEM_MB = 1 << 20


def params(mb, **more):
    return pltpu.CompilerParams(vmem_limit_bytes=mb * VMEM_MB, **more)


def cost(flops, bytes_accessed):
    return pl.CostEstimate(flops=int(flops), bytes_accessed=int(bytes_accessed), transcendentals=0)


def pad_rows(x):
    rows = x.shape[0]
    if rows == PAD:
        return x
    return jnp.concatenate([x, jnp.zeros((PAD - rows,) + x.shape[1:], x.dtype)], axis=0)


def live_ranks(lengths, slots):
    live, rank, count = [], [], jnp.int32(0)
    for slot in range(slots):
        alive = lengths[slot] > 0
        live.append(alive)
        rank.append(count)
        count = count + alive.astype(i32)
    return live, rank


def attend_kernel(
    lengths, where_side, q_ref, nk_ref, nv_ref, k_ref, v_ref, table_ref, res_ref, gain_ref, *rest
):
    sides = len(rest) - 3
    mixed_ref, sends, bias_ref, square_ref = rest[0], rest[1 : 1 + sides], rest[-2], rest[-1]
    head = pl.program_id(0)
    slots = q_ref.shape[0]
    pages, page = k_ref.shape[0], k_ref.shape[1]
    tokens = pages * page
    width = mixed_ref.shape[1]
    scale = math.log2(math.e) / math.sqrt(HEAD)

    @pl.when(head == 0)
    def _():
        lanes = 128 * ((pages + 127) // 128)
        row = lax.broadcasted_iota(i32, (PAD, lanes), 0)
        column = lax.broadcasted_iota(i32, (PAD, lanes), 1)
        reach = jnp.zeros((PAD, lanes), i32)
        for slot in range(slots):
            reach = jnp.where(row == slot, lengths[slot], reach)
        table = pad_rows(table_ref[...])
        seen = jnp.zeros((PAD, lanes), i32)
        for entry in range(table.shape[1]):
            here = jnp.minimum(jnp.maximum(reach - entry * page, 0), page)
            seen = seen + jnp.where(table[:, entry : entry + 1] == column, here, 0)
        spread = (
            lax.broadcasted_iota(i32, (lanes, tokens), 1) // page
            == lax.broadcasted_iota(i32, (lanes, tokens), 0)
        )
        seen_tokens = jnp.dot(
            seen.astype(f32).astype(bf16),
            spread.astype(f32).astype(bf16),
            preferred_element_type=f32,
        )
        place = (lax.broadcasted_iota(i32, (PAD, tokens), 1) % page).astype(f32)
        bias_ref[...] = jnp.where(place < seen_tokens, 0.0, -1e30)
        square_ref[...] = jnp.zeros_like(square_ref)

    q = jnp.concatenate(
        [pad_rows(q_ref[:, g * HEAD : (g + 1) * HEAD]) for g in range(GROUP)], axis=0
    )
    keys = k_ref[...].reshape(tokens, HEAD)
    values = v_ref[...].reshape(tokens, HEAD)
    new_key = pad_rows(nk_ref[...]).astype(f32)
    new_value = pad_rows(nv_ref[...]).astype(f32)
    scores = lax.dot_general(q, keys, (((1,), (1,)), ((), ())), preferred_element_type=f32)
    scores = scores.reshape(GROUP, PAD, tokens) * scale + bias_ref[...][None]
    own = jnp.sum(q.astype(f32).reshape(GROUP, PAD, HEAD) * new_key[None], axis=-1, keepdims=True)
    own = own * scale
    highest = jnp.maximum(jnp.max(scores, axis=-1, keepdims=True), own)
    weights = jnp.exp2(scores - highest)
    own_weight = jnp.exp2(own - highest)
    total = jnp.sum(weights, axis=-1, keepdims=True) + own_weight
    summed = jnp.dot(
        weights.astype(bf16).reshape(GROUP * PAD, tokens), values, preferred_element_type=f32
    ).reshape(GROUP, PAD, HEAD)
    attended = (summed + own_weight * new_value[None]) / total
    squares = jnp.zeros((slots, HEAD), f32)
    base = pl.multiple_of(head * (GROUP * HEAD), GROUP * HEAD)
    for g in range(GROUP):
        mixed = res_ref[:, g * HEAD : (g + 1) * HEAD].astype(f32) + attended[g][:slots]
        mixed_ref[:, pl.ds(base + g * HEAD, HEAD)] = mixed
        squares = squares + mixed * mixed
    square_ref[...] += squares

    @pl.when(head == KV_HEADS - 1)
    def _():
        live, rank = live_ranks(lengths, slots)
        count = (rank[-1] + live[-1].astype(i32)).astype(f32)
        row = lax.broadcasted_iota(i32, (PAD, PAD), 0)
        column = lax.broadcasted_iota(i32, (PAD, PAD), 1)
        pick = jnp.zeros((PAD, PAD), f32)
        for slot in range(slots):
            chosen = jnp.logical_and(row == rank[slot], column == slot)
            pick = jnp.where(jnp.logical_and(chosen, live[slot]), 1.0, pick)
        pick = pick.astype(bf16)
        root = lax.rsqrt(jnp.sum(square_ref[...], axis=-1, keepdims=True) / width + epsilon)
        step = width // sides
        for shift in range(sides):
            at = pl.multiple_of(lax.rem(where_side[0] + shift, sides) * step, step)
            normed = mixed_ref[:, pl.ds(at, step)] * root * gain_ref[:, pl.ds(at, step)].astype(f32)
            normed = pad_rows(normed.astype(bf16))
            rows = jnp.dot(pick, normed, preferred_element_type=f32)
            last = lax.broadcasted_iota(i32, rows.shape, 0) == PAD - 1
            sends[shift][...] = jnp.where(last, count, rows).astype(bf16)


def attend(queries, new_kv, kv_pool, page_table, ctx_len, residual_in, norm_gain, side, sides):
    slots, width = queries.shape
    pages, page, _ = kv_pool.shape
    tokens = pages * page
    step = width // sides
    head_block = lambda g, *_: (0, g)
    fixed = lambda g, *_: (0, 0)
    return pl.pallas_call(
        attend_kernel,
        grid_spec=pltpu.PrefetchScalarGridSpec(
            num_scalar_prefetch=2,
            grid=(KV_HEADS,),
            in_specs=[
                pl.BlockSpec((slots, GROUP * HEAD), head_block),
                pl.BlockSpec((slots, HEAD), head_block),
                pl.BlockSpec((slots, HEAD), lambda g, *_: (0, KV_HEADS + g)),
                pl.BlockSpec((pages, page, HEAD), lambda g, *_: (0, 0, g)),
                pl.BlockSpec((pages, page, HEAD), lambda g, *_: (0, 0, KV_HEADS + g)),
                pl.BlockSpec(page_table.shape, fixed),
                pl.BlockSpec((slots, GROUP * HEAD), head_block),
                pl.BlockSpec((1, width), fixed),
            ],
            out_specs=[pl.BlockSpec((slots, width), fixed)]
            + [pl.BlockSpec((PAD, step), fixed)] * sides,
            scratch_shapes=[pltpu.VMEM((PAD, tokens), f32), pltpu.VMEM((slots, HEAD), f32)],
        ),
        out_shape=[jax.ShapeDtypeStruct((slots, width), f32)]
        + [jax.ShapeDtypeStruct((PAD, step), bf16)] * sides,
        compiler_params=params(24),
        cost_estimate=cost(4 * 8 * 128 * 128 * tokens, kv_pool.size * 2),
        name="attend",
    )(
        ctx_len, side, queries, new_kv, new_kv, kv_pool, kv_pool, page_table, residual_in,
        norm_gain.reshape(1, width),
    )


def pack_up_kernel(side, layout, *refs, parts):
    gathered, w_ref, packed_ref, out_ref = refs[:parts], refs[parts], refs[-2], refs[-1]
    rows = packed_ref.shape[0]

    @pl.when(pl.program_id(0) == 0)
    def _():
        per = gathered[0].shape[0]
        pieces = per // PAD
        total = jnp.zeros(packed_ref.shape, f32)
        for part in range(parts):
            lane = lax.broadcasted_iota(i32, (rows, per), 1)
            row = lax.broadcasted_iota(i32, (rows, per), 0)
            target = jnp.full((rows, per), -1, i32)
            for piece in range(pieces):
                base = layout[part * pieces + piece]
                count = layout[(parts + part) * pieces + piece]
                inside = lane - piece * PAD
                mine = jnp.logical_and(inside >= 0, inside < count)
                target = jnp.where(mine, base + inside, target)
            pick = (target == row).astype(f32).astype(bf16)
            total = total + jnp.dot(pick, gathered[part][...], preferred_element_type=f32)
        packed_ref[...] = total.astype(bf16)

    out_ref[...] = jnp.dot(packed_ref[...], w_ref[...], preferred_element_type=f32).astype(out_ref.dtype)


def up_kernel(side, x_ref, w_ref, out_ref):
    out_ref[...] = jnp.dot(x_ref[...], w_ref[...], preferred_element_type=f32).astype(out_ref.dtype)


TILE = 256


def pack_up(side, layout, gathered, w_up, rows, block_width, mask):
    depth = w_up.shape[0]
    tiles = block_width // TILE
    fixed = lambda t, *_: (0, 0)
    return pl.pallas_call(
        functools.partial(pack_up_kernel, parts=len(gathered)),
        grid_spec=pltpu.PrefetchScalarGridSpec(
            num_scalar_prefetch=2,
            grid=(tiles,),
            in_specs=[pl.BlockSpec(g.shape, fixed) for g in gathered]
            + [pl.BlockSpec((depth, TILE), lambda t, side, *_: (0, (side[0] ^ mask) * tiles + t))],
            out_specs=[
                pl.BlockSpec((rows, depth), fixed),
                pl.BlockSpec((rows, TILE), lambda t, *_: (0, t)),
            ],
        ),
        out_shape=[
            jax.ShapeDtypeStruct((rows, depth), bf16),
            jax.ShapeDtypeStruct((rows, block_width), bf16),
        ],
        compiler_params=params(24),
        cost_estimate=cost(2 * rows * depth * block_width, depth * block_width * 2),
        name="pack_up",
    )(side, layout, *gathered, w_up)


def up(side, packed, w_up, block_width, dtype, mask):
    rows, depth = packed.shape
    tiles = block_width // TILE
    return pl.pallas_call(
        up_kernel,
        grid_spec=pltpu.PrefetchScalarGridSpec(
            num_scalar_prefetch=1,
            grid=(tiles,),
            in_specs=[
                pl.BlockSpec((rows, depth), lambda t, *_: (0, 0)),
                pl.BlockSpec((depth, TILE), lambda t, side, *_: (0, (side[0] ^ mask) * tiles + t)),
            ],
            out_specs=pl.BlockSpec((rows, TILE), lambda t, *_: (0, t)),
        ),
        out_shape=jax.ShapeDtypeStruct((rows, block_width), dtype),
        compiler_params=params(16),
        cost_estimate=cost(2 * rows * depth * block_width, depth * block_width * 2),
        name="up",
    )(side, packed, w_up)


def down_kernel(side, *refs, first):
    a_ref, w_ref = refs[0], refs[1]
    out_ref = refs[-1]
    part = jnp.dot(a_ref[...], w_ref[...], preferred_element_type=f32)
    out_ref[...] = part if first else refs[2][...] + part


def down(side, active, w_down, before, mask):
    rows, depth = active.shape
    width = w_down.shape[1]
    tile = 512
    sums = pl.BlockSpec((rows, tile), lambda t, *_: (0, t))
    return pl.pallas_call(
        functools.partial(down_kernel, first=before is None),
        grid_spec=pltpu.PrefetchScalarGridSpec(
            num_scalar_prefetch=1,
            grid=(width // tile,),
            in_specs=[
                pl.BlockSpec((rows, depth), lambda t, *_: (0, 0)),
                pl.BlockSpec((depth, tile), lambda t, side, *_: (side[0] ^ mask, t)),
            ]
            + ([] if before is None else [sums]),
            out_specs=sums,
        ),
        out_shape=jax.ShapeDtypeStruct((rows, width), f32),
        compiler_params=params(16),
        cost_estimate=cost(2 * rows * depth * width, depth * width * 2),
        name="down",
    )(side, active, w_down, *([] if before is None else [before]))


def down_unpack_kernel(side, layout, a_ref, w_ref, before_ref, *outs):
    parts = len(outs)
    rows = a_ref.shape[0]
    pieces = outs[0].shape[0] // PAD
    share = before_ref[...] + jnp.dot(a_ref[...], w_ref[...], preferred_element_type=f32)
    share = share.astype(bf16)
    row = lax.broadcasted_iota(i32, (PAD, rows), 0)
    column = lax.broadcasted_iota(i32, (PAD, rows), 1)
    for part in range(parts):
        picks = []
        for piece in range(pieces):
            base = layout[part * pieces + piece]
            count = layout[(parts + part) * pieces + piece]
            picks.append(jnp.logical_and(column - row == base, row < count).astype(f32))
        pick = jnp.concatenate(picks, axis=0).astype(bf16)
        outs[part][...] = jnp.dot(pick, share, preferred_element_type=f32).astype(bf16)


def down_unpack(side, layout, active, w_down, before, parts, per, mask):
    rows, depth = active.shape
    width = w_down.shape[1]
    tile = 512
    return pl.pallas_call(
        down_unpack_kernel,
        grid_spec=pltpu.PrefetchScalarGridSpec(
            num_scalar_prefetch=2,
            grid=(width // tile,),
            in_specs=[
                pl.BlockSpec((rows, depth), lambda t, *_: (0, 0)),
                pl.BlockSpec((depth, tile), lambda t, side, *_: (side[0] ^ mask, t)),
                pl.BlockSpec((rows, tile), lambda t, *_: (0, t)),
            ],
            out_specs=[pl.BlockSpec((per, tile), lambda t, *_: (0, t))] * parts,
        ),
        out_shape=[jax.ShapeDtypeStruct((per, width), bf16)] * parts,
        compiler_params=params(16),
        cost_estimate=cost(2 * rows * depth * width, depth * width * 2),
        name="down_unpack",
    )(side, layout, active, w_down, before)


def finish_kernel(lengths, where_side, mixed_ref, *refs):
    blocks, out_ref = refs[:-1], refs[-1]
    sides = len(blocks)
    slots, width = out_ref.shape
    step = width // sides
    live, rank = live_ranks(lengths, slots)
    row = lax.broadcasted_iota(i32, (PAD, PAD), 0)
    column = lax.broadcasted_iota(i32, (PAD, PAD), 1)
    pick = jnp.zeros((PAD, PAD), f32)
    for slot in range(slots):
        chosen = jnp.logical_and(column == rank[slot], row == slot)
        pick = jnp.where(jnp.logical_and(chosen, live[slot]), 1.0, pick)
    pick = pick.astype(bf16)
    for shift in range(sides):
        at = pl.multiple_of(lax.rem(where_side[0] + shift, sides) * step, step)
        back = jnp.dot(pick, blocks[shift][...], preferred_element_type=f32)[:slots]
        out_ref[:, pl.ds(at, step)] = (mixed_ref[:, pl.ds(at, step)] + back).astype(bf16)


def finish(ctx_len, side, mixed, blocks):
    whole = pl.BlockSpec(memory_space=pltpu.VMEM)
    scalars = pl.BlockSpec(memory_space=pltpu.SMEM)
    return pl.pallas_call(
        finish_kernel,
        in_specs=[scalars, scalars, whole] + [whole] * len(blocks),
        out_specs=whole,
        out_shape=jax.ShapeDtypeStruct(mixed.shape, bf16),
        compiler_params=params(16),
        cost_estimate=cost(mixed.size * 32, mixed.size * 8),
        name="finish",
    )(ctx_len, side, mixed, *blocks)


def swap(x, axis, count, mask):
    return lax.ppermute(x, axis, [(j, j ^ mask) for j in range(count)])


def shifted(x, axis, count, shift):
    return lax.ppermute(x, axis, [(j, (j + shift) % count) for j in range(count)])


def added(a, b):
    return (a.astype(f32) + b.astype(f32)).astype(bf16)


def tie(x, *others):
    return lax.optimization_barrier((x, *others))[0]


def feed_forward(rows, side, layout, gathered, w_up, w_down):
    width = w_up.shape[1] // 4
    packed, far_partner = pack_up(side, layout, gathered, w_up, rows, width, 3)
    met = swap(far_partner, "side", 4, 1)
    near = up(side, packed, w_up, width, bf16, 1)
    far = up(side, packed, w_up, width, bf16, 2)
    own = up(side, packed, w_up, width, f32, 0)
    pair_sum = added(far, met)
    crossed = swap(pair_sum, "side", 4, 2)
    near = swap(tie(near, met), "side", 4, 1)
    lifted = own + near.astype(f32) + crossed.astype(f32)
    clipped = jnp.maximum(lifted, 0.0)
    active = (clipped * clipped).astype(bf16)
    across = swap(active, "side", 4, 2)
    beside = swap(active, "side", 4, 1)
    forwarded = swap(across, "side", 4, 1)
    total = down(side, active, w_down, None, 0)
    total = down(side, beside, w_down, total, 1)
    total = down(side, across, w_down, total, 2)
    parts, per = len(gathered), gathered[0].shape[0]
    return down_unpack(side, layout, forwarded, w_down, total, parts, per, 3)


def layout_kernel(side, shard, *refs):
    parts, out = refs[:-1], refs[-1]
    pieces = parts[0].shape[0] // PAD
    devices = len(parts) * pieces
    counts, places = [], []
    for part in range(len(parts)):
        for piece in range(pieces):
            last = parts[part][piece * PAD : (piece + 1) * PAD, :].astype(f32)[PAD - 1 :]
            counts.append(jnp.max(last).astype(i32))
            places.append(lax.rem(side[0] - piece + pieces, pieces) * len(parts) + (shard[0] ^ part))
    total = jnp.int32(0)
    for one in range(devices):
        base = jnp.int32(0)
        for other in range(devices):
            base = base + jnp.where(places[other] < places[one], counts[other], 0)
        out[one] = base
        out[devices + one] = counts[one]
        total = total + counts[one]
    out[2 * devices] = total


def read_layout(side, shard, gathered):
    per = gathered[0].shape[0]
    pieces = per // PAD
    scalars = pl.BlockSpec(memory_space=pltpu.SMEM)
    return pl.pallas_call(
        layout_kernel,
        grid=(1,),
        in_specs=[scalars, scalars] + [pl.BlockSpec((per, 128), lambda t: (0, 0))] * len(gathered),
        out_specs=scalars,
        out_shape=jax.ShapeDtypeStruct((2 * len(gathered) * pieces + 1,), i32),
        compiler_params=params(16),
        name="layout",
    )(side, shard, *gathered)


ROW_STEPS = (96, 112, 128, 144, 160, 176, 192)


def line_shards(
    queries, new_kv, kv_pool, page_table, ctx_len, residual_in, norm_gain, w_up, w_down
):
    i, s = lax.axis_index("side"), lax.axis_index("shard")
    side, shard = i.reshape(1), s.reshape(1)
    in_hbm = lambda x: pltpu.with_memory_space_constraint(x, pltpu.HBM)
    queries, new_kv, kv_pool, residual_in, w_up, w_down = map(
        in_hbm, (queries, new_kv, kv_pool, residual_in, w_up, w_down)
    )
    mixed, *sends = attend(
        queries, new_kv, kv_pool, page_table, ctx_len, residual_in, norm_gain, side, 4
    )
    arrived = {shift: shifted(sends[shift], "side", 4, shift) for shift in (2, 1, 3)}
    arrived[0] = sends[0]
    here = jnp.concatenate([arrived[shift] for shift in range(4)], axis=0)
    by_x = swap(here, "shard", 4, 2)
    by_core = swap(here, "shard", 4, 1)
    by_both = swap(by_x, "shard", 4, 1)
    gathered = [here, by_core, by_x, by_both]
    layout = read_layout(side, shard, gathered)
    live = layout[-1]
    step = sum((live > rows).astype(i32) for rows in ROW_STEPS[:-1])
    mine, for_core, for_x, for_both = lax.switch(
        step,
        [functools.partial(feed_forward, rows) for rows in ROW_STEPS],
        side, layout, gathered, w_up, w_down,
    )
    back = swap(jnp.concatenate([for_core, for_both], axis=0), "shard", 4, 1)
    half = back.shape[0] // 2
    to_x = added(for_x, back[half:])
    kept = added(mine, back[:half])
    home = added(kept, swap(to_x, "shard", 4, 2)).reshape(4, PAD, -1)
    blocks = [home[0]] + [shifted(home[shift], "side", 4, -shift) for shift in (1, 2, 3)]
    return finish(ctx_len, side, mixed, blocks)


def attend_slots(queries, new_kv, pool_pages, page_rows, lengths):
    slot_count = queries.shape[0]
    positions = page_rows.shape[1] * pool_pages.shape[1]
    fetched = pool_pages[page_rows].reshape(slot_count, positions, 2, KV_HEADS, HEAD)
    fresh_kv = new_kv.reshape(slot_count, 2, KV_HEADS, HEAD)
    query_heads = queries.reshape(slot_count, KV_HEADS, GROUP, HEAD)
    score_scale = 1.0 / math.sqrt(HEAD)
    scores = (
        jnp.einsum("sgqd,slgd->sgql", query_heads, fetched[:, :, 0], preferred_element_type=f32)
        * score_scale
    )
    own_score = (
        jnp.einsum("sgqd,sgd->sgq", query_heads, fresh_kv[:, 0], preferred_element_type=f32)
        * score_scale
    )
    visible = (jnp.arange(positions, dtype=i32)[None, :] < lengths[:, None])[:, None, None, :]
    scores = jnp.where(visible, scores, -1e30)
    highest = jnp.maximum(jnp.max(scores, axis=-1), own_score)
    weights = jnp.where(visible, jnp.exp(scores - highest[..., None]), 0.0)
    own_weight = jnp.exp(own_score - highest)
    denominator = jnp.sum(weights, axis=-1) + own_weight
    probabilities = (weights / denominator[..., None]).astype(bf16)
    own_prob = (own_weight / denominator).astype(bf16).astype(f32)
    attended = jnp.einsum(
        "sgql,slgd->sgqd", probabilities, fetched[:, :, 1], preferred_element_type=f32
    )
    attended = attended + own_prob[..., None] * fresh_kv[:, 1].astype(f32)[:, :, None, :]
    return attended.reshape(slot_count, -1)


def any_shards(queries, new_kv, kv_pool, page_table, ctx_len, residual_in, norm_gain, w_up, w_down):
    attended = attend_slots(queries, new_kv, kv_pool, page_table, ctx_len)
    mixed_rows = residual_in.astype(f32) + attended
    mean_square = jnp.mean(mixed_rows * mixed_rows, axis=-1, keepdims=True)
    normed = (mixed_rows * lax.rsqrt(mean_square + epsilon) * norm_gain.astype(f32)).astype(bf16)
    live_mask = ctx_len > 0
    spread = lax.all_to_all(normed, "side", split_axis=1, concat_axis=0, tiled=True)
    up_partial = jnp.dot(
        lax.all_gather(spread, "shard", axis=0, tiled=True), w_up, preferred_element_type=f32
    )
    lifted = lax.psum(up_partial, "side")
    clipped = jnp.maximum(lifted, 0.0)
    active = (clipped * clipped).astype(bf16)
    down_share = lax.psum_scatter(
        jnp.dot(active, w_down, preferred_element_type=f32).astype(bf16),
        "shard",
        scatter_dimension=0,
        tiled=True,
    )
    returned = lax.all_to_all(down_share, "side", split_axis=0, concat_axis=1, tiled=True)
    returned = jnp.where(live_mask[:, None], returned.astype(f32), 0.0)
    return (mixed_rows + returned).astype(bf16)


def solution(mesh):
    rows = ("grp", "side", "shard")
    placed = (
        P(rows, None),
        P(rows, None),
        P(rows, None, None),
        P(rows, None),
        P(rows),
        P(rows, None),
        P(),
        P("side", "shard"),
        P("shard", "side"),
    )
    square = mesh.shape["side"] == 4 and mesh.shape["shard"] == 4
    return jax.shard_map(
        line_shards if square else any_shards,
        mesh=mesh,
        in_specs=placed,
        out_specs=P(rows, None),
        check_vma=False,
    )
```

```python
import functools
import math

import jax
import jax.numpy as jnp
from jax import lax
from jax.experimental import pallas as pl
from jax.experimental.pallas import tpu as pltpu
from jax.sharding import PartitionSpec as P

KV_HEADS = 8
HEAD = 128
GROUP = 8
LIVE_CAP = 12
PAD = 16

epsilon = 1e-05
bf16, f32, i32 = jnp.bfloat16, jnp.float32, jnp.int32
VMEM_MB = 1 << 20


def params(mb, **more):
    return pltpu.CompilerParams(vmem_limit_bytes=mb * VMEM_MB, **more)


def cost(flops, bytes_accessed):
    return pl.CostEstimate(flops=int(flops), bytes_accessed=int(bytes_accessed), transcendentals=0)


def pad_rows(x):
    rows = x.shape[0]
    if rows == PAD:
        return x
    return jnp.concatenate([x, jnp.zeros((PAD - rows,) + x.shape[1:], x.dtype)], axis=0)


def live_ranks(lengths, slots):
    live, rank, count = [], [], jnp.int32(0)
    for slot in range(slots):
        alive = lengths[slot] > 0
        live.append(alive)
        rank.append(count)
        count = count + alive.astype(i32)
    return live, rank


def token_bias(lengths, table, pages, page):
    slots, entries = table.shape
    tokens = pages * page
    lanes = 128 * ((pages + 127) // 128)
    row = lax.broadcasted_iota(i32, (PAD, lanes), 0)
    column = lax.broadcasted_iota(i32, (PAD, lanes), 1)
    reach = jnp.zeros((PAD, lanes), i32)
    for slot in range(slots):
        reach = jnp.where(row == slot, lengths[slot], reach)
    table = pad_rows(table)
    seen = jnp.zeros((PAD, lanes), i32)
    for entry in range(entries):
        here = jnp.minimum(jnp.maximum(reach - entry * page, 0), page)
        seen = seen + jnp.where(table[:, entry : entry + 1] == column, here, 0)
    spread = (
        lax.broadcasted_iota(i32, (lanes, tokens), 1) // page
        == lax.broadcasted_iota(i32, (lanes, tokens), 0)
    )
    seen_tokens = jnp.dot(
        seen.astype(f32).astype(bf16), spread.astype(f32).astype(bf16), preferred_element_type=f32
    )
    place = (lax.broadcasted_iota(i32, (PAD, tokens), 1) % page).astype(f32)
    return jnp.where(place < seen_tokens, 0.0, -1e30)


def live_pick(lengths, slots, rows, offset, to_slots):
    live, rank = live_ranks(lengths, slots)
    shape = (PAD, rows) if to_slots else (rows, PAD)
    of_slot = lax.broadcasted_iota(i32, shape, 0 if to_slots else 1)
    of_rank = lax.broadcasted_iota(i32, shape, 1 if to_slots else 0) - offset
    pick = jnp.zeros(shape, f32)
    for slot in range(slots):
        chosen = jnp.logical_and(of_rank == rank[slot], of_slot == slot)
        pick = jnp.where(jnp.logical_and(chosen, live[slot]), 1.0, pick)
    return pick.astype(bf16), rank[-1] + live[-1].astype(i32)


SHIFTS = (2, 1, 3, 0)
POOL_CUTS = 4


def attend_kernel(lengths, side, *refs, sides, shift, following, first):
    last = following is None
    refs = list(refs)
    take = lambda n: [refs.pop(0) for _ in range(n)]
    if first:
        table_ref = refs.pop(0)
        sources = take(4)
        pool_ref = refs.pop(0)
    else:
        q_ref, new_ref, res_ref, gain_ref, bias_ref, k_ref, v_ref = take(7)
        pool_ref = None if last else refs.pop(0)
    send_ref, mixed_ref, square_ref = take(3)
    if first:
        q_ref, new_ref, res_ref, gain_ref, bias_ref = take(5)
    if not last:
        next_k_ref, next_v_ref = take(2)
    if first:
        k_ref, v_ref, gain_copy, sems, own_sems = take(5)
    if not last:
        next_sems = refs.pop(0)
    slots, step = mixed_ref.shape
    pages, page, columns = k_ref.shape
    heads = columns // HEAD
    tokens = pages * page
    cut = pages // POOL_CUTS
    scale = math.log2(math.e) / math.sqrt(HEAD)

    def fetch(target_k, target_v, towards, sems):
        block = lax.rem(side[0] + towards, sides)
        copies = []
        for target, at, row in ((target_k, block, 0), (target_v, sides + block, 1)):
            at = pl.multiple_of(at * columns, columns)
            for c in range(POOL_CUTS):
                rows = pl.ds(c * cut, cut)
                copy = pltpu.make_async_copy(
                    pool_ref.at[rows, :, pl.ds(at, columns)], target.at[rows], sems.at[row, c]
                )
                copy.start()
                copies.append(copy)
        return copies

    if first:
        small = [
            pltpu.make_async_copy(source, target, own_sems.at[n])
            for n, (source, target) in enumerate(
                zip(sources, (q_ref, new_ref, res_ref, gain_copy), strict=True)
            )
        ]
        for copy in small[:2]:
            copy.start()
        now = fetch(k_ref, v_ref, shift, sems)
        for copy in small[2:]:
            copy.start()
        ahead = fetch(next_k_ref, next_v_ref, following, next_sems)
        bias_ref[...] = token_bias(lengths, table_ref[...], pages, page)
        for copy in small + now:
            copy.wait()
        gain_ref[...] = gain_copy[...].astype(f32)
    elif not last:
        ahead = fetch(next_k_ref, next_v_ref, following, next_sems)

    block = lax.rem(side[0] + shift, sides)
    start = pl.multiple_of(block * step, step)
    new_start = pl.multiple_of(block * columns, columns)
    pick, count = live_pick(lengths, slots, PAD, 0, False)
    squares = jnp.zeros((slots, HEAD), f32)
    bias = bias_ref[...][None]
    for head in range(heads):
        across = slice(head * HEAD, (head + 1) * HEAD)
        base = head * GROUP * HEAD
        q = jnp.concatenate(
            [pad_rows(q_ref[:, pl.ds(start + base + g * HEAD, HEAD)]) for g in range(GROUP)],
            axis=0,
        )
        keys = k_ref[:, :, across].reshape(tokens, HEAD)
        values = v_ref[:, :, across].reshape(tokens, HEAD)
        new_at = new_start + head * HEAD
        new_key = pad_rows(new_ref[:, pl.ds(new_at, HEAD)]).astype(f32)
        new_value = pad_rows(new_ref[:, pl.ds(sides * columns + new_at, HEAD)]).astype(f32)
        scores = lax.dot_general(q, keys, (((1,), (1,)), ((), ())), preferred_element_type=f32)
        scores = scores.reshape(GROUP, PAD, tokens) * scale + bias
        own = jnp.sum(
            q.astype(f32).reshape(GROUP, PAD, HEAD) * new_key[None], axis=-1, keepdims=True
        )
        own = own * scale
        highest = jnp.maximum(jnp.max(scores, axis=-1, keepdims=True), own)
        weights = jnp.exp2(scores - highest)
        own_weight = jnp.exp2(own - highest)
        total = jnp.sum(weights, axis=-1, keepdims=True) + own_weight
        summed = jnp.dot(
            weights.astype(bf16).reshape(GROUP * PAD, tokens), values, preferred_element_type=f32
        ).reshape(GROUP, PAD, HEAD)
        attended = (summed + own_weight * new_value[None]) / total
        for g in range(GROUP):
            at = slice(base + g * HEAD, base + (g + 1) * HEAD)
            residual = res_ref[:, pl.ds(start + base + g * HEAD, HEAD)].astype(f32)
            mixed = residual + attended[g][:slots]
            mixed_ref[:, at] = mixed
            squares = squares + mixed * mixed
            gain = gain_ref[pl.ds(block * (step // HEAD) + head * GROUP + g, 1), :]
            gained = pad_rows((mixed * gain).astype(bf16))
            rows = jnp.dot(pick, gained, preferred_element_type=f32)
            counted = lax.broadcasted_iota(i32, rows.shape, 0) == PAD - 1
            send_ref[:, at] = jnp.where(counted, count.astype(f32), rows).astype(bf16)
    square_ref[...] = squares
    if not last:
        for copy in ahead:
            copy.wait()


def attend(inputs, side, sides, shift, following, before):
    queries, new_kv, kv_pool, page_table, ctx_len, residual_in, norm_gain = inputs
    slots, width = queries.shape
    pages, page, _ = kv_pool.shape
    tokens = pages * page
    step, columns = width // sides, new_kv.shape[1] // 2 // sides
    first, last = before is None, following is None
    vmem, anywhere = pl.BlockSpec(memory_space=pltpu.VMEM), pl.BlockSpec(memory_space=pl.ANY)
    smem = pl.BlockSpec(memory_space=pltpu.SMEM)
    kept = pltpu.VMEM((pages, page, columns), bf16)
    sems = pltpu.SemaphoreType.DMA((2, POOL_CUTS))
    out_shape = [
        jax.ShapeDtypeStruct((PAD, step), bf16),
        jax.ShapeDtypeStruct((slots, step), f32),
        jax.ShapeDtypeStruct((slots, HEAD), f32),
    ]
    scratch = []
    if first:
        gain = norm_gain.reshape(width // HEAD, HEAD)
        operands = [page_table, queries, new_kv, residual_in, gain, kv_pool]
        in_specs = [vmem] + [anywhere] * 5
        out_shape += [
            pltpu.VMEM(queries.shape, bf16),
            pltpu.VMEM(new_kv.shape, bf16),
            pltpu.VMEM(residual_in.shape, bf16),
            pltpu.VMEM(gain.shape, f32),
            pltpu.VMEM((PAD, tokens), f32),
        ]
        scratch += [kept, kept, pltpu.VMEM(gain.shape, bf16), sems, pltpu.SemaphoreType.DMA((4,))]
    else:
        operands = list(before)
        in_specs = [vmem] * 7
        if not last:
            operands.append(kv_pool)
            in_specs.append(anywhere)
    if not last:
        out_shape += [kept, kept]
        scratch.append(sems)
    send, mixed, squares, *rest = pl.pallas_call(
        functools.partial(attend_kernel, sides=sides, shift=shift, following=following, first=first),
        in_specs=[smem, smem] + in_specs,
        out_specs=[vmem] * len(out_shape),
        out_shape=out_shape,
        scratch_shapes=scratch,
        compiler_params=params(28),
        cost_estimate=cost(2e9, kv_pool.size),
        name="attend",
    )(ctx_len, side, *operands)
    if last:
        return send, mixed, squares, None
    return send, mixed, squares, rest if first else list(before[:5]) + rest


UP_TILE = 256
DOWN_TILE = 512


def tile_copy(w_ref, row, rows, column, buffer, sems, t, tile):
    at = pl.ds(pl.multiple_of(t * tile, tile), tile)
    source = w_ref.at[pl.ds(row, rows), pl.ds(pl.multiple_of(column + t * tile, tile), tile)]
    return pltpu.make_async_copy(source, buffer.at[:, at], sems.at[t])


def up_kernel(side, layout, *refs, parts, masks):
    refs = list(refs)
    gathered = [refs.pop(0) for _ in range(parts)]
    x_ref = None if parts else refs.pop(0)
    w_ref = refs.pop(0)
    if parts:
        x_ref = refs.pop(0)
    outs, (buffer, sems) = refs[:-2], refs[-2:]
    depth, width = buffer.shape[1:]
    tiles = width // UP_TILE

    def copy_of(n, t):
        column = pl.multiple_of((side[0] ^ masks[n]) * width, width)
        return tile_copy(w_ref, 0, depth, column, buffer.at[n], sems.at[n], t, UP_TILE)

    for n in range(len(masks)):
        for t in range(tiles):
            copy_of(n, t).start()
    if parts:
        rows, per = x_ref.shape[0], gathered[0].shape[0]
        pieces = per // PAD
        lane = lax.broadcasted_iota(i32, (rows, per), 1)
        row = lax.broadcasted_iota(i32, (rows, per), 0)
        picks = []
        for part in range(parts):
            target = jnp.full((rows, per), -1, i32)
            for piece in range(pieces):
                base = layout[part * pieces + piece]
                count = layout[(parts + part) * pieces + piece]
                inside = lane - piece * PAD
                mine = jnp.logical_and(inside >= 0, inside < count)
                target = jnp.where(mine, base + inside, target)
            picks.append((target == row).astype(f32).astype(bf16))

        @pl.loop(0, depth // UP_TILE)
        def _(t):
            at = pl.ds(pl.multiple_of(t * UP_TILE, UP_TILE), UP_TILE)
            total = jnp.zeros((rows, UP_TILE), f32)
            for part in range(parts):
                total = total + jnp.dot(
                    picks[part], gathered[part][:, at], preferred_element_type=f32
                )
            x_ref[:, at] = total.astype(bf16)

    for n, out_ref in enumerate(outs):

        @pl.loop(0, tiles)
        def _(t):
            copy_of(n, t).wait()
            at = pl.ds(pl.multiple_of(t * UP_TILE, UP_TILE), UP_TILE)
            out_ref[:, at] = jnp.dot(
                x_ref[...], buffer[n, :, at], preferred_element_type=f32
            ).astype(out_ref.dtype)


def up(side, layout, inputs, w_up, rows, width, dtype, masks, pack=False):
    depth = w_up.shape[0]
    vmem, smem = pl.BlockSpec(memory_space=pltpu.VMEM), pl.BlockSpec(memory_space=pltpu.SMEM)
    out = [jax.ShapeDtypeStruct((rows, width), dtype)] * len(masks)
    if pack:
        out = [jax.ShapeDtypeStruct((rows, depth), bf16)] + out
    return pl.pallas_call(
        functools.partial(up_kernel, parts=len(inputs) if pack else 0, masks=masks),
        in_specs=[smem, smem] + [vmem] * len(inputs) + [pl.BlockSpec(memory_space=pl.ANY)],
        out_specs=[vmem] * len(out),
        out_shape=out,
        scratch_shapes=[
            pltpu.VMEM((len(masks), depth, width), bf16),
            pltpu.SemaphoreType.DMA((len(masks), width // UP_TILE)),
        ],
        compiler_params=params(24),
        cost_estimate=cost(2 * rows * depth * width, depth * width * 2 * len(masks)),
        name="up",
    )(side, layout, *inputs, w_up)


def down_kernel(side, *refs, first, mask, ahead):
    refs = list(refs)
    a_ref, w_ref = refs.pop(0), refs.pop(0)
    before_ref = None if first else refs.pop(0)
    out_ref = refs.pop(0)
    next_ref = refs.pop(0) if ahead is not None else None
    buffer, sems = refs.pop(0), refs.pop(0)
    depth, width = buffer.shape
    tiles = width // DOWN_TILE

    def copy_of(other, buffer, sems, t):
        row = pl.multiple_of((side[0] ^ other) * depth, depth)
        return tile_copy(w_ref, row, depth, 0, buffer, sems, t, DOWN_TILE)

    for t in range(tiles):
        copy_of(mask, buffer, sems, t).start()
    if ahead is not None:
        for t in range(tiles):
            copy_of(ahead, next_ref, refs[0], t).start()

    @pl.loop(0, tiles)
    def _(t):
        copy_of(mask, buffer, sems, t).wait()
        at = pl.ds(pl.multiple_of(t * DOWN_TILE, DOWN_TILE), DOWN_TILE)
        part = jnp.dot(a_ref[...], buffer[:, at], preferred_element_type=f32)
        out_ref[:, at] = part if first else before_ref[:, at] + part

    if ahead is not None:

        @pl.loop(0, tiles)
        def _(t):
            copy_of(ahead, next_ref, refs[0], t).wait()


def down(side, active, w_down, before, mask, ahead=None):
    rows, depth = active.shape
    width = w_down.shape[1]
    vmem, smem = pl.BlockSpec(memory_space=pltpu.VMEM), pl.BlockSpec(memory_space=pltpu.SMEM)
    out = jax.ShapeDtypeStruct((rows, width), f32)
    sems = pltpu.SemaphoreType.DMA((width // DOWN_TILE,))
    return pl.pallas_call(
        functools.partial(down_kernel, first=before is None, mask=mask, ahead=ahead),
        in_specs=[smem, vmem, pl.BlockSpec(memory_space=pl.ANY)]
        + ([] if before is None else [vmem]),
        out_specs=vmem if ahead is None else [vmem, vmem],
        out_shape=out if ahead is None else [out, pltpu.VMEM((depth, width), bf16)],
        scratch_shapes=[pltpu.VMEM((depth, width), bf16), sems]
        + ([] if ahead is None else [sems]),
        compiler_params=params(24),
        cost_estimate=cost(2 * rows * depth * width, depth * width * 2),
        name="down",
    )(side, active, w_down, *([] if before is None else [before]))


def down_unpack_kernel(layout, a_ref, w_ref, before_ref, *refs, parts):
    outs, wide = refs[:-1], refs[-1]
    rows = a_ref.shape[0]
    width = w_ref.shape[1]
    tiles = width // DOWN_TILE
    tall = wide.shape[2] * tiles
    pieces = tall // (tiles * LIVE_CAP)
    row = lax.broadcasted_iota(i32, (PAD, rows), 0)
    column = lax.broadcasted_iota(i32, (PAD, rows), 1)
    picks = []
    for part in range(parts):
        some = []
        for piece in range(pieces):
            base = layout[part * pieces + piece]
            count = layout[(parts + part) * pieces + piece]
            some.append(jnp.logical_and(column - row == base, row < count).astype(f32))
        picks.append(jnp.concatenate(some, axis=0).astype(bf16))

    @pl.loop(0, tiles)
    def _(t):
        at = pl.ds(pl.multiple_of(t * DOWN_TILE, DOWN_TILE), DOWN_TILE)
        share = before_ref[:, at] + jnp.dot(a_ref[...], w_ref[:, at], preferred_element_type=f32)
        share = share.astype(bf16)
        for part in range(parts):
            back = jnp.dot(picks[part], share, preferred_element_type=f32)
            for piece in range(pieces):
                here = slice(piece * LIVE_CAP, (piece + 1) * LIVE_CAP)
                wide[t, part, here, :] = back[piece * PAD : piece * PAD + LIVE_CAP]

    across = parts // len(outs)
    for n, out in enumerate(outs):
        for k in range(across):
            part = PART_ORDER[n * across + k]
            for piece in range(pieces):
                here = slice(piece * LIVE_CAP, (piece + 1) * LIVE_CAP)
                whole = jnp.concatenate([wide[t, part, here, :] for t in range(tiles)], axis=0)
                start = k * tall + piece * tiles * LIVE_CAP
                out[start : start + tiles * LIVE_CAP, :] = whole.astype(bf16)


PART_ORDER = (0, 2, 1, 3)


def down_unpack(layout, active, weights, before, parts, pieces):
    rows, depth = active.shape
    width = weights.shape[1]
    tiles = width // DOWN_TILE
    tall = pieces * LIVE_CAP
    vmem, smem = pl.BlockSpec(memory_space=pltpu.VMEM), pl.BlockSpec(memory_space=pltpu.SMEM)
    return pl.pallas_call(
        functools.partial(down_unpack_kernel, parts=parts),
        in_specs=[smem, vmem, vmem, vmem],
        out_specs=[vmem] * 2,
        out_shape=[jax.ShapeDtypeStruct((parts // 2 * tall * tiles, DOWN_TILE), bf16)] * 2,
        scratch_shapes=[pltpu.VMEM((tiles, parts, tall, DOWN_TILE), f32)],
        compiler_params=params(24),
        cost_estimate=cost(2 * rows * depth * width, rows * width * 4),
        name="down_unpack",
    )(layout, active, weights, before)


def finish_kernel(lengths, side, *refs):
    out_ref = refs[-1]
    sides = (len(refs) - 1) // 3
    mixed, squares, blocks = refs[:sides], refs[sides : 2 * sides], refs[2 * sides : 3 * sides]
    slots, width = out_ref.shape
    step = width // sides
    total = squares[0][...]
    for other in squares[1:]:
        total = total + other[...]
    root = lax.rsqrt(jnp.sum(total, axis=-1, keepdims=True) / width + epsilon)
    gain = root * root
    tiles = step // DOWN_TILE
    picks = [
        live_pick(lengths, slots, tiles * LIVE_CAP, t * LIVE_CAP, True)[0] for t in range(tiles)
    ]
    for shift in range(sides):
        base = lax.rem(side[0] + shift, sides) * step
        block = blocks[shift][...]
        for t in range(tiles):
            back = jnp.dot(picks[t], block, preferred_element_type=f32)[:slots]
            at = pl.multiple_of(base + t * DOWN_TILE, DOWN_TILE)
            here = mixed[shift][:, t * DOWN_TILE : (t + 1) * DOWN_TILE]
            out_ref[:, pl.ds(at, DOWN_TILE)] = (here + gain * back).astype(bf16)


def finish(ctx_len, side, mixed, squares, blocks):
    vmem, smem = pl.BlockSpec(memory_space=pltpu.VMEM), pl.BlockSpec(memory_space=pltpu.SMEM)
    slots, width = mixed[0].shape[0], mixed[0].shape[1] * len(mixed)
    return pl.pallas_call(
        finish_kernel,
        in_specs=[smem, smem] + [vmem] * (3 * len(mixed)),
        out_specs=vmem,
        out_shape=jax.ShapeDtypeStruct((slots, width), bf16),
        compiler_params=params(16),
        cost_estimate=cost(slots * width * 32, slots * width * 8),
        name="finish",
    )(ctx_len, side, *mixed, *squares, *blocks)


def swap(x, axis, count, mask):
    return lax.ppermute(x, axis, [(j, j ^ mask) for j in range(count)])


def shifted(x, axis, count, shift):
    return lax.ppermute(x, axis, [(j, (j + shift) % count) for j in range(count)])


def added(a, b):
    return (a.astype(f32) + b.astype(f32)).astype(bf16)


def tie(x, *others):
    return lax.optimization_barrier((x, *others))[0]


def feed_forward(rows, side, layout, gathered, w_up, w_down):
    width = w_up.shape[1] // 4
    packed, far_partner = up(side, layout, gathered, w_up, rows, width, bf16, (3,), pack=True)
    met = swap(far_partner, "side", 4, 1)
    far, near = up(side, layout, [packed], w_up, rows, width, bf16, (2, 1))
    met = tie(met, far)
    pair_sum = added(far, met)
    crossed = swap(pair_sum, "side", 4, 2)
    near = swap(tie(near, met), "side", 4, 1)
    (own,) = up(side, layout, [tie(packed, pair_sum)], w_up, rows, width, f32, (0,))
    lifted = own + near.astype(f32) + crossed.astype(f32)
    clipped = jnp.maximum(lifted, 0.0)
    active = (clipped * clipped).astype(bf16)
    across = swap(active, "side", 4, 2)
    beside = swap(active, "side", 4, 1)
    total = down(side, active, w_down, None, 0)
    total = down(side, beside, w_down, total, 1)
    across, total = lax.optimization_barrier((across, total))
    forwarded = swap(across, "side", 4, 1)
    total, weights = down(side, across, w_down, total, 2, ahead=3)
    parts, pieces = len(gathered), gathered[0].shape[0] // PAD
    return down_unpack(layout, forwarded, weights, total, parts, pieces)


def layout_kernel(side, shard, *refs, limits):
    parts, out, step_out = refs[:-2], refs[-2], refs[-1]
    pieces = parts[0].shape[0] // PAD
    devices = len(parts) * pieces
    counts, places = [], []
    for part in range(len(parts)):
        for piece in range(pieces):
            last = parts[part][piece * PAD : (piece + 1) * PAD, :].astype(f32)[PAD - 1 :]
            counts.append(jnp.max(last).astype(i32))
            places.append(lax.rem(side[0] - piece + pieces, pieces) * len(parts) + (shard[0] ^ part))
    total = jnp.int32(0)
    for one in range(devices):
        base = jnp.int32(0)
        for other in range(devices):
            base = base + jnp.where(places[other] < places[one], counts[other], 0)
        out[one] = base
        out[devices + one] = counts[one]
        total = total + counts[one]
    step = jnp.int32(0)
    for limit in limits:
        step = step + (total > limit).astype(i32)
    step_out[0] = step


def read_layout(side, shard, gathered, limits):
    per = gathered[0].shape[0]
    pieces = per // PAD
    scalars = pl.BlockSpec(memory_space=pltpu.SMEM)
    return pl.pallas_call(
        functools.partial(layout_kernel, limits=limits),
        grid=(1,),
        in_specs=[scalars, scalars] + [pl.BlockSpec((per, 128), lambda t: (0, 0))] * len(gathered),
        out_specs=[scalars, scalars],
        out_shape=[
            jax.ShapeDtypeStruct((2 * len(gathered) * pieces,), i32),
            jax.ShapeDtypeStruct((1,), i32),
        ],
        compiler_params=params(16),
        name="layout",
    )(side, shard, *gathered)


ROW_STEPS = (112, 128, 144, 160, 192)


def line_shards(
    queries, new_kv, kv_pool, page_table, ctx_len, residual_in, norm_gain, w_up, w_down
):
    i, s = lax.axis_index("side"), lax.axis_index("shard")
    side, shard = i.reshape(1), s.reshape(1)
    in_hbm = lambda x: pltpu.with_memory_space_constraint(x, pltpu.HBM)
    queries, new_kv, kv_pool, page_table, ctx_len, residual_in, w_up, w_down = map(
        in_hbm, (queries, new_kv, kv_pool, page_table, ctx_len, residual_in, w_up, w_down)
    )
    inputs = queries, new_kv, kv_pool, page_table, ctx_len, residual_in, norm_gain
    mixed, squares, arrived, kept = [None] * 4, [None] * 4, [None] * 4, None
    for shift, following in zip(SHIFTS, SHIFTS[1:] + (None,)):
        send, mixed[shift], squares[shift], kept = attend(inputs, side, 4, shift, following, kept)
        arrived[shift] = shifted(send, "side", 4, shift) if shift else send
    here = jnp.concatenate(arrived, axis=0)
    by_x = swap(here, "shard", 4, 2)
    by_core = swap(here, "shard", 4, 1)
    by_both = swap(by_x, "shard", 4, 1)
    gathered = [here, by_core, by_x, by_both]
    layout, step = read_layout(side, shard, gathered, ROW_STEPS[:-1])
    stay, leave = lax.switch(
        step[0],
        [functools.partial(feed_forward, rows) for rows in ROW_STEPS],
        side, layout, gathered, w_up, w_down,
    )
    back = swap(leave, "shard", 4, 1)
    half = back.shape[0] // 2
    to_x = added(stay[half:], back[half:])
    kept = added(stay[:half], back[:half])
    home = added(kept, swap(to_x, "shard", 4, 2)).reshape(4, half // 4, -1)
    blocks = [home[0]] + [shifted(home[shift], "side", 4, -shift) for shift in (1, 2, 3)]
    return finish(ctx_len, side, mixed, squares, blocks)


def attend_slots(queries, new_kv, pool_pages, page_rows, lengths):
    slot_count = queries.shape[0]
    positions = page_rows.shape[1] * pool_pages.shape[1]
    fetched = pool_pages[page_rows].reshape(slot_count, positions, 2, KV_HEADS, HEAD)
    fresh_kv = new_kv.reshape(slot_count, 2, KV_HEADS, HEAD)
    query_heads = queries.reshape(slot_count, KV_HEADS, GROUP, HEAD)
    score_scale = 1.0 / math.sqrt(HEAD)
    scores = (
        jnp.einsum("sgqd,slgd->sgql", query_heads, fetched[:, :, 0], preferred_element_type=f32)
        * score_scale
    )
    own_score = (
        jnp.einsum("sgqd,sgd->sgq", query_heads, fresh_kv[:, 0], preferred_element_type=f32)
        * score_scale
    )
    visible = (jnp.arange(positions, dtype=i32)[None, :] < lengths[:, None])[:, None, None, :]
    scores = jnp.where(visible, scores, -1e30)
    highest = jnp.maximum(jnp.max(scores, axis=-1), own_score)
    weights = jnp.where(visible, jnp.exp(scores - highest[..., None]), 0.0)
    own_weight = jnp.exp(own_score - highest)
    denominator = jnp.sum(weights, axis=-1) + own_weight
    probabilities = (weights / denominator[..., None]).astype(bf16)
    own_prob = (own_weight / denominator).astype(bf16).astype(f32)
    attended = jnp.einsum(
        "sgql,slgd->sgqd", probabilities, fetched[:, :, 1], preferred_element_type=f32
    )
    attended = attended + own_prob[..., None] * fresh_kv[:, 1].astype(f32)[:, :, None, :]
    return attended.reshape(slot_count, -1)


def any_shards(queries, new_kv, kv_pool, page_table, ctx_len, residual_in, norm_gain, w_up, w_down):
    attended = attend_slots(queries, new_kv, kv_pool, page_table, ctx_len)
    mixed_rows = residual_in.astype(f32) + attended
    mean_square = jnp.mean(mixed_rows * mixed_rows, axis=-1, keepdims=True)
    normed = (mixed_rows * lax.rsqrt(mean_square + epsilon) * norm_gain.astype(f32)).astype(bf16)
    live_mask = ctx_len > 0
    spread = lax.all_to_all(normed, "side", split_axis=1, concat_axis=0, tiled=True)
    up_partial = jnp.dot(
        lax.all_gather(spread, "shard", axis=0, tiled=True), w_up, preferred_element_type=f32
    )
    lifted = lax.psum(up_partial, "side")
    clipped = jnp.maximum(lifted, 0.0)
    active = (clipped * clipped).astype(bf16)
    down_share = lax.psum_scatter(
        jnp.dot(active, w_down, preferred_element_type=f32).astype(bf16),
        "shard",
        scatter_dimension=0,
        tiled=True,
    )
    returned = lax.all_to_all(down_share, "side", split_axis=0, concat_axis=1, tiled=True)
    returned = jnp.where(live_mask[:, None], returned.astype(f32), 0.0)
    return (mixed_rows + returned).astype(bf16)


def solution(mesh):
    rows = ("grp", "side", "shard")
    placed = (
        P(rows, None),
        P(rows, None),
        P(rows, None, None),
        P(rows, None),
        P(rows),
        P(rows, None),
        P(),
        P("side", "shard"),
        P("shard", "side"),
    )
    square = mesh.shape["side"] == 4 and mesh.shape["shard"] == 4
    return jax.shard_map(
        line_shards if square else any_shards,
        mesh=mesh,
        in_specs=placed,
        out_specs=P(rows, None),
        check_vma=False,
    )
```

```python
import functools
import math

import jax
import jax.numpy as jnp
from jax import lax
from jax.experimental import pallas as pl
from jax.experimental.pallas import tpu as pltpu
from jax.sharding import PartitionSpec as P

KV_HEADS = 8
HEAD = 128
GROUP = 8
LIVE_CAP = 12
PAD = 16

epsilon = 1e-05
bf16, f32, i32 = jnp.bfloat16, jnp.float32, jnp.int32
VMEM_MB = 1 << 20


def params(mb, **more):
    return pltpu.CompilerParams(vmem_limit_bytes=mb * VMEM_MB, **more)


def cost(flops, bytes_accessed):
    return pl.CostEstimate(
        flops=int(flops) // 64, bytes_accessed=int(bytes_accessed) // 64, transcendentals=0
    )


def pad_rows(x):
    rows = x.shape[0]
    if rows == PAD:
        return x
    return jnp.concatenate([x, jnp.zeros((PAD - rows,) + x.shape[1:], x.dtype)], axis=0)


def live_ranks(lengths, slots):
    live, rank, count = [], [], jnp.int32(0)
    for slot in range(slots):
        alive = lengths[slot] > 0
        live.append(alive)
        rank.append(count)
        count = count + alive.astype(i32)
    return live, rank


def token_bias(lengths, table, pages, page):
    slots, entries = table.shape
    tokens = pages * page
    lanes = 128 * ((pages + 127) // 128)
    row = lax.broadcasted_iota(i32, (PAD, lanes), 0)
    column = lax.broadcasted_iota(i32, (PAD, lanes), 1)
    reach = jnp.zeros((PAD, lanes), i32)
    for slot in range(slots):
        reach = jnp.where(row == slot, lengths[slot], reach)
    table = pad_rows(table)
    seen = jnp.zeros((PAD, lanes), i32)
    for entry in range(entries):
        here = jnp.minimum(jnp.maximum(reach - entry * page, 0), page)
        seen = seen + jnp.where(table[:, entry : entry + 1] == column, here, 0)
    spread = (
        lax.broadcasted_iota(i32, (lanes, tokens), 1) // page
        == lax.broadcasted_iota(i32, (lanes, tokens), 0)
    )
    seen_tokens = jnp.dot(
        seen.astype(f32).astype(bf16), spread.astype(f32).astype(bf16), preferred_element_type=f32
    )
    place = (lax.broadcasted_iota(i32, (PAD, tokens), 1) % page).astype(f32)
    return jnp.where(place < seen_tokens, 0.0, -1e30)


def live_pick(lengths, slots, rows, offset, to_slots):
    live, rank = live_ranks(lengths, slots)
    shape = (PAD, rows) if to_slots else (rows, PAD)
    of_slot = lax.broadcasted_iota(i32, shape, 0 if to_slots else 1)
    of_rank = lax.broadcasted_iota(i32, shape, 1 if to_slots else 0) - offset
    pick = jnp.zeros(shape, f32)
    for slot in range(slots):
        chosen = jnp.logical_and(of_rank == rank[slot], of_slot == slot)
        pick = jnp.where(jnp.logical_and(chosen, live[slot]), 1.0, pick)
    return pick.astype(bf16), rank[-1] + live[-1].astype(i32)


POOL_CUTS = 4


def attend_kernel(lengths, side, *refs, masks, first):
    refs = list(refs)
    take = lambda n: [refs.pop(0) for _ in range(n)]
    if first:
        table_ref = refs.pop(0)
        sources = take(5)
    else:
        q_ref, new_ref, res_ref, gain_ref, bias_ref, pool_ref = take(6)
    sends, mixed_refs = take(len(masks)), take(len(masks))
    square_ref = refs.pop(0)
    if first:
        q_ref, new_ref, res_ref, gain_ref, bias_ref, pool_ref, gain_copy, sems, pool_sems = take(9)
    slots, step = mixed_refs[0].shape
    pages, page, columns = pool_ref.shape
    columns = columns * step // q_ref.shape[1] // 2
    heads = columns // HEAD
    tokens = pages * page
    scale = math.log2(math.e) / math.sqrt(HEAD)

    if first:
        small = [
            pltpu.make_async_copy(source, target, sems.at[n])
            for n, (source, target) in enumerate(
                zip(sources[:4], (q_ref, new_ref, res_ref, gain_copy), strict=True)
            )
        ]
        cut, half = pages // POOL_CUTS, pool_ref.shape[2] // 2
        brought = []
        for n, at in enumerate((pl.ds(0, half), pl.ds(half, half))):
            for c in range(POOL_CUTS):
                rows = pl.ds(c * cut, cut)
                brought.append(
                    pltpu.make_async_copy(
                        sources[4].at[rows, :, at], pool_ref.at[rows, :, at], pool_sems.at[n, c]
                    )
                )
        for copy in small + brought:
            copy.start()
        bias_ref[...] = token_bias(lengths, table_ref[...], pages, page)
        for copy in small + brought[:POOL_CUTS]:
            copy.wait()
        gain_ref[...] = gain_copy[...].astype(f32)
        values_to_come = brought[POOL_CUTS:]
    else:
        values_to_come = []

    pick, count = live_pick(lengths, slots, PAD, 0, False)
    squares = jnp.zeros((slots, HEAD), f32)
    bias = bias_ref[...][None]
    for mask, send_ref, mixed_ref in zip(masks, sends, mixed_refs, strict=True):
        block = side[0] ^ mask
        start = pl.multiple_of(block * step, step)
        new_start = pl.multiple_of(block * columns, columns)
        for head in range(heads):
            base = head * GROUP * HEAD
            new_at = new_start + head * HEAD
            value_at = new_ref.shape[1] // 2 + new_at
            q = jnp.concatenate(
                [pad_rows(q_ref[:, pl.ds(start + base + g * HEAD, HEAD)]) for g in range(GROUP)],
                axis=0,
            )
            keys = pool_ref[:, :, pl.ds(new_at, HEAD)].reshape(tokens, HEAD)
            new_key = pad_rows(new_ref[:, pl.ds(new_at, HEAD)]).astype(f32)
            new_value = pad_rows(new_ref[:, pl.ds(value_at, HEAD)]).astype(f32)
            scores = lax.dot_general(q, keys, (((1,), (1,)), ((), ())), preferred_element_type=f32)
            scores = scores.reshape(GROUP, PAD, tokens) * scale + bias
            own = jnp.sum(
                q.astype(f32).reshape(GROUP, PAD, HEAD) * new_key[None], axis=-1, keepdims=True
            )
            own = own * scale
            highest = jnp.maximum(jnp.max(scores, axis=-1, keepdims=True), own)
            weights = jnp.exp2(scores - highest)
            own_weight = jnp.exp2(own - highest)
            total = jnp.sum(weights, axis=-1, keepdims=True) + own_weight
            for copy in values_to_come:
                copy.wait()
            values_to_come = []
            values = pool_ref[:, :, pl.ds(value_at, HEAD)].reshape(tokens, HEAD)
            summed = jnp.dot(
                weights.astype(bf16).reshape(GROUP * PAD, tokens),
                values,
                preferred_element_type=f32,
            ).reshape(GROUP, PAD, HEAD)
            attended = (summed + own_weight * new_value[None]) / total
            for g in range(GROUP):
                at = slice(base + g * HEAD, base + (g + 1) * HEAD)
                residual = res_ref[:, pl.ds(start + base + g * HEAD, HEAD)].astype(f32)
                mixed = residual + attended[g][:slots]
                mixed_ref[:, at] = mixed
                squares = squares + mixed * mixed
                gain = gain_ref[pl.ds(block * (step // HEAD) + head * GROUP + g, 1), :]
                gained = pad_rows((mixed * gain).astype(bf16))
                rows = jnp.dot(pick, gained, preferred_element_type=f32)
                counted = lax.broadcasted_iota(i32, rows.shape, 0) == PAD - 1
                send_ref[:, at] = jnp.where(counted, count.astype(f32), rows).astype(bf16)
    square_ref[...] = squares


def attend(inputs, side, sides, masks, before):
    queries, new_kv, kv_pool, page_table, ctx_len, residual_in, norm_gain = inputs
    slots, columns = queries.shape
    pages, page, _ = kv_pool.shape
    step = columns // sides
    first = before is None
    vmem, anywhere = pl.BlockSpec(memory_space=pltpu.VMEM), pl.BlockSpec(memory_space=pl.ANY)
    smem = pl.BlockSpec(memory_space=pltpu.SMEM)
    out_shape = [jax.ShapeDtypeStruct((PAD, step), bf16)] * len(masks)
    out_shape += [jax.ShapeDtypeStruct((slots, step), f32)] * len(masks)
    out_shape += [jax.ShapeDtypeStruct((slots, HEAD), f32)]
    if first:
        gain = norm_gain
        operands = [page_table, queries, new_kv, residual_in, gain, kv_pool]
        in_specs = [vmem] + [anywhere] * 5
        out_shape += [
            pltpu.VMEM(queries.shape, bf16),
            pltpu.VMEM(new_kv.shape, bf16),
            pltpu.VMEM(residual_in.shape, bf16),
            pltpu.VMEM(gain.shape, f32),
            pltpu.VMEM((PAD, pages * page), f32),
            pltpu.VMEM(kv_pool.shape, bf16),
        ]
        scratch = [
            pltpu.VMEM(gain.shape, bf16),
            pltpu.SemaphoreType.DMA((4,)),
            pltpu.SemaphoreType.DMA((2, POOL_CUTS)),
        ]
    else:
        operands = before
        in_specs = [vmem] * len(before)
        scratch = []
    outs = pl.pallas_call(
        functools.partial(attend_kernel, masks=masks, first=first),
        in_specs=[smem, smem] + in_specs,
        out_specs=[vmem] * len(out_shape),
        out_shape=out_shape,
        scratch_shapes=scratch,
        compiler_params=params(28),
        cost_estimate=cost(2e9, kv_pool.size),
        name="attend",
    )(ctx_len, side, *operands)
    n = len(masks)
    return outs[:n], outs[n : 2 * n], outs[2 * n], outs[2 * n + 1 :]


UP_TILE = 256
DOWN_TILE = 512


def tile_copy(w_ref, row, rows, column, buffer, sems, t, tile):
    at = pl.ds(pl.multiple_of(t * tile, tile), tile)
    source = w_ref.at[pl.ds(row, rows), pl.ds(pl.multiple_of(column + t * tile, tile), tile)]
    return pltpu.make_async_copy(source, buffer.at[:, at], sems.at[t])


def up_kernel(side, *refs, masks):
    x_ref, w_ref = refs[:2]
    outs, (buffer, sems) = refs[2:-2], refs[-2:]
    depth, width = buffer.shape[1:]
    tiles = width // UP_TILE

    def copy_of(n, t):
        column = pl.multiple_of(((side[0] ^ masks[n][0]) * 2 + masks[n][1]) * width, width)
        return tile_copy(w_ref, 0, depth, column, buffer.at[n], sems.at[n], t, UP_TILE)

    for n in range(len(masks)):
        for t in range(tiles):
            copy_of(n, t).start()
    for n, out_ref in enumerate(outs):

        @pl.loop(0, tiles)
        def _(t):
            copy_of(n, t).wait()
            at = pl.ds(pl.multiple_of(t * UP_TILE, UP_TILE), UP_TILE)
            out_ref[:, at] = jnp.dot(
                x_ref[...], buffer[n, :, at], preferred_element_type=f32
            ).astype(out_ref.dtype)


def up(side, packed, w_up, width, dtype, masks):
    rows, depth = packed.shape
    vmem, smem = pl.BlockSpec(memory_space=pltpu.VMEM), pl.BlockSpec(memory_space=pltpu.SMEM)
    return pl.pallas_call(
        functools.partial(up_kernel, masks=masks),
        in_specs=[smem, vmem, pl.BlockSpec(memory_space=pl.ANY)],
        out_specs=[vmem] * len(masks),
        out_shape=[jax.ShapeDtypeStruct((rows, width), dtype)] * len(masks),
        scratch_shapes=[
            pltpu.VMEM((len(masks), depth, width), bf16),
            pltpu.SemaphoreType.DMA((len(masks), width // UP_TILE)),
        ],
        compiler_params=params(24),
        cost_estimate=cost(2 * rows * depth * width, depth * width * 2 * len(masks)),
        name="up",
    )(side, packed, w_up)


PIECES = ((0, 2), (1, 3))


def pack_up_kernel(side, layout, *refs, mask):
    gathered, (w_ref, packed_ref, out_ref, buffer, sems) = refs[:-5], refs[-5:]
    width = out_ref.shape[1]

    def copy_of(t):
        column = pl.multiple_of((side[0] ^ mask) * 2 * width, width)
        return tile_copy(w_ref, 0, buffer.shape[0], column, buffer, sems, t, UP_TILE)

    for t in range(width // UP_TILE):
        copy_of(t).start()
    rows, depth = packed_ref.shape
    per = gathered[0].shape[0]
    lane = lax.broadcasted_iota(i32, (rows, per), 1)
    row = lax.broadcasted_iota(i32, (rows, per), 0)
    devices = len(gathered) * (per // PAD)
    picks = []
    for part in range(len(gathered)):
        target = jnp.full((rows, per), -1, i32)
        for piece, mask in enumerate(PIECES[part % 2]):
            place = part // 2 * 4 + mask
            base, count = layout[place], layout[devices + place]
            inside = lane - piece * PAD
            mine = jnp.logical_and(inside >= 0, inside < count)
            target = jnp.where(mine, base + inside, target)
        picks.append((target == row).astype(f32).astype(bf16))
    pick = jnp.concatenate(picks, axis=1)

    @pl.loop(0, depth // DOWN_TILE)
    def _(t):
        at = pl.ds(pl.multiple_of(t * DOWN_TILE, DOWN_TILE), DOWN_TILE)
        pieces = jnp.concatenate([part[:, at] for part in gathered], axis=0)
        packed_ref[:, at] = jnp.dot(pick, pieces, preferred_element_type=f32).astype(bf16)

    @pl.loop(0, width // UP_TILE)
    def _(t):
        copy_of(t).wait()
        at = pl.ds(pl.multiple_of(t * UP_TILE, UP_TILE), UP_TILE)
        out_ref[:, at] = jnp.dot(
            packed_ref[...], buffer[:, at], preferred_element_type=f32
        ).astype(bf16)


def pack_up(side, layout, gathered, w_up, rows, width, mask):
    depth = w_up.shape[0]
    vmem, smem = pl.BlockSpec(memory_space=pltpu.VMEM), pl.BlockSpec(memory_space=pltpu.SMEM)
    return pl.pallas_call(
        functools.partial(pack_up_kernel, mask=mask),
        in_specs=[smem, smem] + [vmem] * len(gathered) + [pl.BlockSpec(memory_space=pl.ANY)],
        out_specs=[vmem, vmem],
        out_shape=[
            jax.ShapeDtypeStruct((rows, depth), bf16),
            jax.ShapeDtypeStruct((rows, width), bf16),
        ],
        scratch_shapes=[
            pltpu.VMEM((depth, width), bf16),
            pltpu.SemaphoreType.DMA((width // UP_TILE,)),
        ],
        compiler_params=params(24),
        cost_estimate=cost(2 * rows * depth * width, depth * width * 2),
        name="pack_up",
    )(side, layout, *gathered, w_up)


def down_kernel(side, *refs, first, blocks, ahead):
    refs = list(refs)
    actives, w_ref = [refs.pop(0) for _ in blocks], refs.pop(0)
    before_ref = None if first else refs.pop(0)
    out_ref = refs.pop(0)
    next_ref = refs.pop(0) if ahead is not None else None
    buffer, sems = refs.pop(0), refs.pop(0)
    depth, width = buffer.shape[1:]
    tiles = width // DOWN_TILE

    def copy_of(block, buffer, sems, t):
        row = pl.multiple_of(((side[0] ^ block[0]) * 2 + block[1]) * depth, depth)
        return tile_copy(w_ref, row, depth, 0, buffer, sems, t, DOWN_TILE)

    for t in range(tiles):
        for n, block in enumerate(blocks):
            copy_of(block, buffer.at[n], sems.at[n], t).start()
    if ahead is not None:
        for t in range(tiles):
            copy_of(ahead, next_ref, refs[0], t).start()

    @pl.loop(0, tiles)
    def _(t):
        at = pl.ds(pl.multiple_of(t * DOWN_TILE, DOWN_TILE), DOWN_TILE)
        total = None if first else before_ref[:, at]
        for n, block in enumerate(blocks):
            copy_of(block, buffer.at[n], sems.at[n], t).wait()
            part = jnp.dot(actives[n][...], buffer[n, :, at], preferred_element_type=f32)
            total = part if total is None else total + part
        out_ref[:, at] = total

    if ahead is not None:

        @pl.loop(0, tiles)
        def _(t):
            copy_of(ahead, next_ref, refs[0], t).wait()


def down(side, actives, w_down, before, blocks, ahead=None):
    rows, depth = actives[0].shape
    width = w_down.shape[1]
    tiles = width // DOWN_TILE
    vmem, smem = pl.BlockSpec(memory_space=pltpu.VMEM), pl.BlockSpec(memory_space=pltpu.SMEM)
    out = jax.ShapeDtypeStruct((rows, width), f32)
    return pl.pallas_call(
        functools.partial(down_kernel, first=before is None, blocks=blocks, ahead=ahead),
        in_specs=[smem] + [vmem] * len(blocks) + [pl.BlockSpec(memory_space=pl.ANY)]
        + ([] if before is None else [vmem]),
        out_specs=vmem if ahead is None else [vmem, vmem],
        out_shape=out if ahead is None else [out, pltpu.VMEM((depth, width), bf16)],
        scratch_shapes=[
            pltpu.VMEM((len(blocks), depth, width), bf16),
            pltpu.SemaphoreType.DMA((len(blocks), tiles)),
        ]
        + ([] if ahead is None else [pltpu.SemaphoreType.DMA((tiles,))]),
        compiler_params=params(24),
        cost_estimate=cost(2 * rows * depth * width, depth * width * 2),
        name="down",
    )(side, *actives, w_down, *([] if before is None else [before]))


BACK = (2, 3, 0, 1)


def down_unpack_kernel(layout, a_ref, w_ref, before_ref, stay_ref, leave_ref, wide):
    rows = a_ref.shape[0]
    tiles, devices = wide.shape[:2]
    row = lax.broadcasted_iota(i32, (PAD, rows), 0)
    column = lax.broadcasted_iota(i32, (PAD, rows), 1)
    picks = []
    for other in (2, 0, 3, 1):
        for mask in BACK:
            place = other * len(BACK) + mask
            base, count = layout[place], layout[devices + place]
            picks.append(jnp.logical_and(column - row == base, row < count).astype(f32))
    pick = jnp.concatenate(picks, axis=0).astype(bf16)

    @pl.loop(0, tiles)
    def _(t):
        at = pl.ds(pl.multiple_of(t * DOWN_TILE, DOWN_TILE), DOWN_TILE)
        share = before_ref[:, at] + jnp.dot(a_ref[...], w_ref[:, at], preferred_element_type=f32)
        back = jnp.dot(pick, share.astype(bf16), preferred_element_type=f32)
        wide[t] = back.reshape(devices, PAD, DOWN_TILE)

    per = tiles * LIVE_CAP
    for device in range(devices):
        out = stay_ref if device < devices // 2 else leave_ref
        start = device % (devices // 2) * per
        whole = jnp.concatenate([wide[t, device, :LIVE_CAP, :] for t in range(tiles)], axis=0)
        out[start : start + per, :] = whole.astype(bf16)


def down_unpack(layout, active, weights, before):
    rows, depth = active.shape
    width = weights.shape[1]
    tiles, devices = width // DOWN_TILE, layout.shape[0] // 2
    vmem, smem = pl.BlockSpec(memory_space=pltpu.VMEM), pl.BlockSpec(memory_space=pltpu.SMEM)
    out = jax.ShapeDtypeStruct((devices // 2 * tiles * LIVE_CAP, DOWN_TILE), bf16)
    return pl.pallas_call(
        down_unpack_kernel,
        in_specs=[smem, vmem, vmem, vmem],
        out_specs=[vmem] * 2,
        out_shape=[out] * 2,
        scratch_shapes=[pltpu.VMEM((tiles, devices, PAD, DOWN_TILE), f32)],
        compiler_params=params(24),
        cost_estimate=cost(2 * rows * depth * width, rows * width * 4),
        name="down_unpack",
    )(layout, active, weights, before)


def finish_kernel(lengths, side, *refs):
    out_ref = refs[-1]
    sides = (len(refs) - 3) // 2
    mixed, squares, blocks = refs[:sides], refs[sides : sides + 2], refs[sides + 2 : -1]
    slots, width = out_ref.shape
    step = width // sides
    total = squares[0][...] + squares[1][...]
    root = lax.rsqrt(jnp.sum(total, axis=-1, keepdims=True) / width + epsilon)
    gain = root * root
    tiles = step // DOWN_TILE
    picks = [
        live_pick(lengths, slots, tiles * LIVE_CAP, t * LIVE_CAP, True)[0] for t in range(tiles)
    ]
    for shift in range(sides):
        base = (side[0] ^ shift) * step
        block = blocks[shift][...]
        for t in range(tiles):
            back = jnp.dot(picks[t], block, preferred_element_type=f32)[:slots]
            at = pl.multiple_of(base + t * DOWN_TILE, DOWN_TILE)
            here = mixed[shift][:, t * DOWN_TILE : (t + 1) * DOWN_TILE]
            out_ref[:, pl.ds(at, DOWN_TILE)] = (here + gain * back).astype(bf16)


def finish(ctx_len, side, mixed, squares, blocks):
    vmem, smem = pl.BlockSpec(memory_space=pltpu.VMEM), pl.BlockSpec(memory_space=pltpu.SMEM)
    slots, width = mixed[0].shape[0], mixed[0].shape[1] * len(mixed)
    return pl.pallas_call(
        finish_kernel,
        in_specs=[smem, smem] + [vmem] * (2 * len(mixed) + 2),
        out_specs=vmem,
        out_shape=jax.ShapeDtypeStruct((slots, width), bf16),
        compiler_params=params(16),
        cost_estimate=cost(slots * width * 32, slots * width * 8),
        name="finish",
    )(ctx_len, side, *mixed, *squares, *blocks)


def swap(x, axis, count, mask):
    return lax.ppermute(x, axis, [(j, j ^ mask) for j in range(count)])


def added(a, b):
    return (a.astype(f32) + b.astype(f32)).astype(bf16)


def tie(x, *others):
    return lax.optimization_barrier((x, *others))[0]


def squared_relu(*terms):
    lifted = sum(term.astype(f32) for term in terms)
    clipped = jnp.maximum(lifted, 0.0)
    return (clipped * clipped).astype(bf16)


def feed_forward(rows, side, layout, gathered, w_up, w_down):
    half = w_up.shape[1] // 8
    across = lambda x: swap(x, "side", 4, 2)
    beside = lambda x: swap(x, "side", 4, 1)
    packed, other_0 = pack_up(side, layout, gathered, w_up, rows, half, 3)
    met_0 = beside(other_0)
    (other_1,) = up(side, packed, w_up, half, bf16, ((3, 1),))
    met_1 = beside(other_1)
    far_0, far_1 = up(side, tie(packed, other_1), w_up, half, bf16, ((2, 0), (2, 1)))
    sum_0 = added(far_0, met_0)
    crossed_0 = across(sum_0)
    near = up(side, tie(packed, sum_0), w_up, half, bf16, ((1, 0), (1, 1)))
    sum_1 = added(far_1, met_1)
    crossed_1 = across(sum_1)
    near = beside(tie(jnp.concatenate(near, axis=0), met_1))
    own_0, own_1 = up(side, tie(packed, sum_1), w_up, half, f32, ((0, 0), (0, 1)))
    active_0 = squared_relu(own_0, near[:rows], crossed_0)
    over_0 = across(active_0)
    active_1 = squared_relu(own_1, near[rows:], crossed_1)
    over_1 = across(active_1)
    following = beside(jnp.concatenate([active_0, active_1], axis=0))
    total = down(side, [active_0, active_1], w_down, None, ((0, 0), (0, 1)))
    over_0 = tie(over_0, total)
    forward_0, forward_1 = beside(over_0), beside(over_1)
    following = [following[:rows], following[rows:]]
    total = down(side, [*following, over_0], w_down, total, ((1, 0), (1, 1), (2, 0)))
    total, weights = down(
        side, [over_1, forward_0], w_down, total, ((2, 1), (3, 0)), ahead=(3, 1)
    )
    return down_unpack(layout, forward_1, weights, total)


def layout_kernel(side, shard, *refs, limits):
    parts, out, step_out = refs[:-2], refs[-2], refs[-1]
    pieces = parts[0].shape[0] // PAD
    devices = len(parts) * pieces
    counts, places = [None] * devices, [None] * devices
    for part in range(len(parts)):
        for piece, mask in enumerate(PIECES[part % 2]):
            last = parts[part][piece * PAD : (piece + 1) * PAD, :].astype(f32)[PAD - 1 :]
            place = part // 2 * 4 + mask
            counts[place] = jnp.max(last).astype(i32)
            places[place] = (side[0] ^ mask) * 4 + (shard[0] ^ (part // 2))
    total = jnp.int32(0)
    for one in range(devices):
        base = jnp.int32(0)
        for other in range(devices):
            base = base + jnp.where(places[other] < places[one], counts[other], 0)
        out[one] = base
        out[devices + one] = counts[one]
        total = total + counts[one]
    step = jnp.int32(0)
    for limit in limits:
        step = step + (total > limit).astype(i32)
    step_out[0] = step


def read_layout(side, shard, gathered, limits):
    per = gathered[0].shape[0]
    pieces = per // PAD
    scalars = pl.BlockSpec(memory_space=pltpu.SMEM)
    return pl.pallas_call(
        functools.partial(layout_kernel, limits=limits),
        grid=(1,),
        in_specs=[scalars, scalars] + [pl.BlockSpec((per, 128), lambda t: (0, 0))] * len(gathered),
        out_specs=[scalars, scalars],
        out_shape=[
            jax.ShapeDtypeStruct((2 * len(gathered) * pieces,), i32),
            jax.ShapeDtypeStruct((1,), i32),
        ],
        compiler_params=params(16),
        name="layout",
    )(side, shard, *gathered)


ROW_STEPS = (112, 128, 144, 160, 192)


def line_shards(
    queries, new_kv, kv_pool, page_table, ctx_len, residual_in, norm_gain, w_up, w_down
):
    i, s = lax.axis_index("side"), lax.axis_index("shard")
    side, shard = i.reshape(1), s.reshape(1)
    in_hbm = lambda x: pltpu.with_memory_space_constraint(x, pltpu.HBM)
    gain = norm_gain.reshape(-1, HEAD)
    inputs = queries, new_kv, kv_pool, page_table, ctx_len, residual_in, gain
    inputs, w_up, w_down = jax.tree.map(in_hbm, (inputs, w_up, w_down))
    ctx_len = inputs[4]
    (to_2, to_3), mixed_far, squares_far, copies = attend(inputs, side, 4, (2, 3), None)
    met = swap(jnp.concatenate([to_2, to_3], axis=0), "side", 4, 2)
    (own, to_1), mixed_near, squares_near, _ = attend(inputs, side, 4, (0, 1), copies)
    first = jnp.concatenate([own, met[:PAD]], axis=0)
    second = swap(jnp.concatenate([to_1, met[PAD:]], axis=0), "side", 4, 1)
    gathered = []
    by_x = [swap(here, "shard", 4, 2) for here in (first, second)]
    by_core = [swap(here, "shard", 4, 1) for here in (first, second)]
    by_both = [swap(there, "shard", 4, 1) for there in by_x]
    gathered = [first, second, *by_core, *by_x, *by_both]
    layout, step = read_layout(side, shard, gathered, ROW_STEPS[:-1])
    stay, leave = lax.switch(
        step[0],
        [functools.partial(feed_forward, rows) for rows in ROW_STEPS],
        side, layout, gathered, w_up, w_down,
    )
    back = swap(leave, "shard", 4, 1)
    quarter = back.shape[0] // 4
    piece = quarter // 2
    sums = [added(stay[at : at + quarter], back[at : at + quarter]) for at in range(0, 4 * quarter, quarter)]
    far = added(sums[2], swap(sums[0], "shard", 4, 2))
    near = added(sums[3], swap(sums[1], "shard", 4, 2))
    home = near[:piece], near[piece:], far[:piece], far[piece:]
    blocks = [home[0]] + [swap(home[mask], "side", 4, mask) for mask in (1, 2, 3)]
    mixed = [*mixed_near, *mixed_far]
    return finish(ctx_len, side, mixed, [squares_far, squares_near], blocks)


def attend_slots(queries, new_kv, pool_pages, page_rows, lengths):
    slot_count = queries.shape[0]
    positions = page_rows.shape[1] * pool_pages.shape[1]
    fetched = pool_pages[page_rows].reshape(slot_count, positions, 2, KV_HEADS, HEAD)
    fresh_kv = new_kv.reshape(slot_count, 2, KV_HEADS, HEAD)
    query_heads = queries.reshape(slot_count, KV_HEADS, GROUP, HEAD)
    score_scale = 1.0 / math.sqrt(HEAD)
    scores = (
        jnp.einsum("sgqd,slgd->sgql", query_heads, fetched[:, :, 0], preferred_element_type=f32)
        * score_scale
    )
    own_score = (
        jnp.einsum("sgqd,sgd->sgq", query_heads, fresh_kv[:, 0], preferred_element_type=f32)
        * score_scale
    )
    visible = (jnp.arange(positions, dtype=i32)[None, :] < lengths[:, None])[:, None, None, :]
    scores = jnp.where(visible, scores, -1e30)
    highest = jnp.maximum(jnp.max(scores, axis=-1), own_score)
    weights = jnp.where(visible, jnp.exp(scores - highest[..., None]), 0.0)
    own_weight = jnp.exp(own_score - highest)
    denominator = jnp.sum(weights, axis=-1) + own_weight
    probabilities = (weights / denominator[..., None]).astype(bf16)
    own_prob = (own_weight / denominator).astype(bf16).astype(f32)
    attended = jnp.einsum(
        "sgql,slgd->sgqd", probabilities, fetched[:, :, 1], preferred_element_type=f32
    )
    attended = attended + own_prob[..., None] * fresh_kv[:, 1].astype(f32)[:, :, None, :]
    return attended.reshape(slot_count, -1)


def any_shards(queries, new_kv, kv_pool, page_table, ctx_len, residual_in, norm_gain, w_up, w_down):
    attended = attend_slots(queries, new_kv, kv_pool, page_table, ctx_len)
    mixed_rows = residual_in.astype(f32) + attended
    mean_square = jnp.mean(mixed_rows * mixed_rows, axis=-1, keepdims=True)
    normed = (mixed_rows * lax.rsqrt(mean_square + epsilon) * norm_gain.astype(f32)).astype(bf16)
    live_mask = ctx_len > 0
    spread = lax.all_to_all(normed, "side", split_axis=1, concat_axis=0, tiled=True)
    up_partial = jnp.dot(
        lax.all_gather(spread, "shard", axis=0, tiled=True), w_up, preferred_element_type=f32
    )
    lifted = lax.psum(up_partial, "side")
    clipped = jnp.maximum(lifted, 0.0)
    active = (clipped * clipped).astype(bf16)
    down_share = lax.psum_scatter(
        jnp.dot(active, w_down, preferred_element_type=f32).astype(bf16),
        "shard",
        scatter_dimension=0,
        tiled=True,
    )
    returned = lax.all_to_all(down_share, "side", split_axis=0, concat_axis=1, tiled=True)
    returned = jnp.where(live_mask[:, None], returned.astype(f32), 0.0)
    return (mixed_rows + returned).astype(bf16)


def solution(mesh):
    rows = ("grp", "side", "shard")
    placed = (
        P(rows, None),
        P(rows, None),
        P(rows, None, None),
        P(rows, None),
        P(rows),
        P(rows, None),
        P(),
        P("side", "shard"),
        P("shard", "side"),
    )
    square = mesh.shape["side"] == 4 and mesh.shape["shard"] == 4
    return jax.shard_map(
        line_shards if square else any_shards,
        mesh=mesh,
        in_specs=placed,
        out_specs=P(rows, None),
        check_vma=False,
    )
```

```python
import functools
import math

import jax
import jax.numpy as jnp
from jax import lax
from jax.experimental import pallas as pl
from jax.experimental.pallas import tpu as pltpu
from jax.sharding import PartitionSpec as P

KV_HEADS = 8
HEAD = 128
GROUP = 8
LIVE_CAP = 12
PAD = 16

epsilon = 1e-05
bf16, f32, i32 = jnp.bfloat16, jnp.float32, jnp.int32
VMEM_MB = 1 << 20


def params(mb, **more):
    return pltpu.CompilerParams(vmem_limit_bytes=mb * VMEM_MB, **more)


def cost(flops, bytes_accessed):
    return pl.CostEstimate(
        flops=int(flops) // 64, bytes_accessed=int(bytes_accessed) // 64, transcendentals=0
    )


def pad_rows(x):
    rows = x.shape[0]
    if rows == PAD:
        return x
    return jnp.concatenate([x, jnp.zeros((PAD - rows,) + x.shape[1:], x.dtype)], axis=0)


def live_ranks(lengths, slots):
    live, rank, count = [], [], jnp.int32(0)
    for slot in range(slots):
        alive = lengths[slot] > 0
        live.append(alive)
        rank.append(count)
        count = count + alive.astype(i32)
    return live, rank


def token_bias(lengths, table, pages, page):
    slots, entries = table.shape
    tokens = pages * page
    lanes = 128 * ((pages + 127) // 128)
    row = lax.broadcasted_iota(i32, (PAD, lanes), 0)
    column = lax.broadcasted_iota(i32, (PAD, lanes), 1)
    reach = jnp.zeros((PAD, lanes), i32)
    for slot in range(slots):
        reach = jnp.where(row == slot, lengths[slot], reach)
    table = pad_rows(table)
    seen = jnp.zeros((PAD, lanes), i32)
    for entry in range(entries):
        here = jnp.minimum(jnp.maximum(reach - entry * page, 0), page)
        seen = seen + jnp.where(table[:, entry : entry + 1] == column, here, 0)
    spread = (
        lax.broadcasted_iota(i32, (lanes, tokens), 1) // page
        == lax.broadcasted_iota(i32, (lanes, tokens), 0)
    )
    seen_tokens = jnp.dot(
        seen.astype(f32).astype(bf16), spread.astype(f32).astype(bf16), preferred_element_type=f32
    )
    place = (lax.broadcasted_iota(i32, (PAD, tokens), 1) % page).astype(f32)
    return jnp.where(place < seen_tokens, 0.0, -1e30)


def live_pick(lengths, slots, rows, offset, to_slots):
    live, rank = live_ranks(lengths, slots)
    shape = (PAD, rows) if to_slots else (rows, PAD)
    of_slot = lax.broadcasted_iota(i32, shape, 0 if to_slots else 1)
    of_rank = lax.broadcasted_iota(i32, shape, 1 if to_slots else 0) - offset
    pick = jnp.zeros(shape, f32)
    for slot in range(slots):
        chosen = jnp.logical_and(of_rank == rank[slot], of_slot == slot)
        pick = jnp.where(jnp.logical_and(chosen, live[slot]), 1.0, pick)
    return pick.astype(bf16), rank[-1] + live[-1].astype(i32)


POOL_CUTS = 4


def attend_kernel(lengths, side, *refs, masks, sides, first):
    refs = list(refs)
    take = lambda n: [refs.pop(0) for _ in range(n)]
    if first:
        table_ref = refs.pop(0)
        sources = take(5)
    else:
        q_ref, new_ref, res_ref, gain_ref, bias_ref, pool_ref = take(6)
    sends, mixed_refs = take(len(masks)), take(len(masks))
    square_ref = refs.pop(0)
    if first:
        q_ref, new_ref, res_ref, gain_ref, bias_ref, pool_ref, gain_copy, sems, pool_sems = take(9)
    slots, step = mixed_refs[0].shape
    pages, page, columns = pool_ref.shape
    columns = columns * step // q_ref.shape[1] // 2
    heads = columns // HEAD
    tokens = pages * page
    scale = math.log2(math.e) / math.sqrt(HEAD)

    if first:
        small = [
            pltpu.make_async_copy(source, target, sems.at[n])
            for n, (source, target) in enumerate(
                zip(sources[:4], (q_ref, new_ref, res_ref, gain_copy), strict=True)
            )
        ]
        cut, half = pages // POOL_CUTS, pool_ref.shape[2] // 2
        pair = half // sides * 2
        here = ((side[0] ^ masks[0]) // 2) * pair
        there = ((side[0] ^ masks[0] ^ 2) // 2) * pair
        brought = []
        for n, at in enumerate((here, half + here, there, half + there)):
            columns_at = pl.ds(pl.multiple_of(at, pair), pair)
            brought.append([])
            for c in range(POOL_CUTS):
                place = (pl.ds(c * cut, cut), slice(None), columns_at)
                brought[n].append(
                    pltpu.make_async_copy(
                        sources[4].at[place], pool_ref.at[place], pool_sems.at[n, c]
                    )
                )
        for copy in small + sum(brought, []):
            copy.start()
        bias_ref[...] = token_bias(lengths, table_ref[...], pages, page)
        for copy in small + brought[0]:
            copy.wait()
        gain_ref[...] = gain_copy[...].astype(f32)
        values_to_come, later = brought[1], brought[2] + brought[3]
    else:
        values_to_come, later = [], []

    pick, count = live_pick(lengths, slots, PAD, 0, False)
    squares = jnp.zeros((slots, HEAD), f32)
    bias = bias_ref[...][None]
    jobs = [(n, head) for n in range(len(masks)) for head in range(heads)]

    def places(job):
        block, base = side[0] ^ masks[job[0]], job[1] * GROUP * HEAD
        key_at = pl.multiple_of(block * columns, columns) + job[1] * HEAD
        return block, base, pl.multiple_of(block * step, step) + base, key_at

    def score(job):
        _, _, start, key_at = places(job)
        q = jnp.concatenate(
            [pad_rows(q_ref[:, pl.ds(start + g * HEAD, HEAD)]) for g in range(GROUP)], axis=0
        )
        keys = pool_ref[:, :, pl.ds(key_at, HEAD)].reshape(tokens, HEAD)
        new_key = pad_rows(new_ref[:, pl.ds(key_at, HEAD)]).astype(f32)
        scores = lax.dot_general(q, keys, (((1,), (1,)), ((), ())), preferred_element_type=f32)
        own = jnp.sum(
            q.astype(f32).reshape(GROUP, PAD, HEAD) * new_key[None], axis=-1, keepdims=True
        )
        return scores.reshape(GROUP, PAD, tokens), own * scale

    ready = score(jobs[0])
    for number, job in enumerate(jobs):
        block, base, start, key_at = places(job)
        value_at = new_ref.shape[1] // 2 + key_at
        scores, own = ready
        if number + 1 < len(jobs):
            ready = score(jobs[number + 1])
        scores = scores * scale + bias
        highest = jnp.maximum(jnp.max(scores, axis=-1, keepdims=True), own)
        weights = jnp.exp2(scores - highest)
        own_weight = jnp.exp2(own - highest)
        total = jnp.sum(weights, axis=-1, keepdims=True) + own_weight
        for copy in values_to_come:
            copy.wait()
        values_to_come = []
        values = pool_ref[:, :, pl.ds(value_at, HEAD)].reshape(tokens, HEAD)
        new_value = pad_rows(new_ref[:, pl.ds(value_at, HEAD)]).astype(f32)
        summed = jnp.dot(
            weights.astype(bf16).reshape(GROUP * PAD, tokens), values, preferred_element_type=f32
        ).reshape(GROUP, PAD, HEAD)
        attended = (summed + own_weight * new_value[None]) / total
        for g in range(GROUP):
            at = slice(base + g * HEAD, base + (g + 1) * HEAD)
            residual = res_ref[:, pl.ds(start + g * HEAD, HEAD)].astype(f32)
            mixed = residual + attended[g][:slots]
            mixed_refs[job[0]][:, at] = mixed
            squares = squares + mixed * mixed
            gain = gain_ref[pl.ds(block * (step // HEAD) + job[1] * GROUP + g, 1), :]
            gained = pad_rows((mixed * gain).astype(bf16))
            rows = jnp.dot(pick, gained, preferred_element_type=f32)
            counted = lax.broadcasted_iota(i32, rows.shape, 0) == PAD - 1
            sends[job[0]][:, at] = jnp.where(counted, count.astype(f32), rows).astype(bf16)
    square_ref[...] = squares
    for copy in later:
        copy.wait()


def attend(inputs, side, sides, masks, before):
    queries, new_kv, kv_pool, page_table, ctx_len, residual_in, norm_gain = inputs
    slots, columns = queries.shape
    pages, page, _ = kv_pool.shape
    step = columns // sides
    first = before is None
    vmem, anywhere = pl.BlockSpec(memory_space=pltpu.VMEM), pl.BlockSpec(memory_space=pl.ANY)
    smem = pl.BlockSpec(memory_space=pltpu.SMEM)
    out_shape = [jax.ShapeDtypeStruct((PAD, step), bf16)] * len(masks)
    out_shape += [jax.ShapeDtypeStruct((slots, step), f32)] * len(masks)
    out_shape += [jax.ShapeDtypeStruct((slots, HEAD), f32)]
    if first:
        gain = norm_gain
        operands = [page_table, queries, new_kv, residual_in, gain, kv_pool]
        in_specs = [vmem] + [anywhere] * 5
        out_shape += [
            pltpu.VMEM(queries.shape, bf16),
            pltpu.VMEM(new_kv.shape, bf16),
            pltpu.VMEM(residual_in.shape, bf16),
            pltpu.VMEM(gain.shape, f32),
            pltpu.VMEM((PAD, pages * page), f32),
            pltpu.VMEM(kv_pool.shape, bf16),
        ]
        scratch = [
            pltpu.VMEM(gain.shape, bf16),
            pltpu.SemaphoreType.DMA((4,)),
            pltpu.SemaphoreType.DMA((4, POOL_CUTS)),
        ]
    else:
        operands = before
        in_specs = [vmem] * len(before)
        scratch = []
    outs = pl.pallas_call(
        functools.partial(attend_kernel, masks=masks, sides=sides, first=first),
        in_specs=[smem, smem] + in_specs,
        out_specs=[vmem] * len(out_shape),
        out_shape=out_shape,
        scratch_shapes=scratch,
        compiler_params=params(28),
        cost_estimate=cost(2e9, kv_pool.size),
        name="attend",
    )(ctx_len, side, *operands)
    n = len(masks)
    return outs[:n], outs[n : 2 * n], outs[2 * n], outs[2 * n + 1 :]


UP_TILE = 256
DOWN_TILE = 512


def tile_copy(w_ref, row, rows, column, buffer, sems, t, tile):
    at = pl.ds(pl.multiple_of(t * tile, tile), tile)
    source = w_ref.at[pl.ds(row, rows), pl.ds(pl.multiple_of(column + t * tile, tile), tile)]
    return pltpu.make_async_copy(source, buffer.at[:, at], sems.at[t])


def up_kernel(side, x_ref, w_ref, out_ref, buffer, sems, *, masks):
    depth, width = buffer.shape[1:]
    tiles = width // UP_TILE

    def copy_of(n, t):
        column = pl.multiple_of(((side[0] ^ masks[n][0]) * 2 + masks[n][1]) * width, width)
        return tile_copy(w_ref, 0, depth, column, buffer.at[n], sems.at[n], t, UP_TILE)

    for n in range(len(masks)):
        for t in range(tiles):
            copy_of(n, t).start()

    @pl.loop(0, len(masks) * tiles)
    def _(job):
        n, t = lax.div(job, tiles), lax.rem(job, tiles)
        at = pl.ds(pl.multiple_of(t * UP_TILE, UP_TILE), UP_TILE)
        pltpu.make_async_copy(
            w_ref.at[:, pl.ds(0, UP_TILE)], buffer.at[n, :, at], sems.at[n, t]
        ).wait()
        out_ref[n, :, at] = jnp.dot(
            x_ref[...], buffer[n, :, at], preferred_element_type=f32
        ).astype(out_ref.dtype)


def up(side, packed, w_up, width, masks):
    rows, depth = packed.shape
    vmem, smem = pl.BlockSpec(memory_space=pltpu.VMEM), pl.BlockSpec(memory_space=pltpu.SMEM)
    return pl.pallas_call(
        functools.partial(up_kernel, masks=masks),
        in_specs=[smem, vmem, pl.BlockSpec(memory_space=pl.ANY)],
        out_specs=vmem,
        out_shape=jax.ShapeDtypeStruct((len(masks), rows, width), bf16),
        scratch_shapes=[
            pltpu.VMEM((len(masks), depth, width), bf16),
            pltpu.SemaphoreType.DMA((len(masks), width // UP_TILE)),
        ],
        compiler_params=params(24),
        cost_estimate=cost(2 * rows * depth * width, depth * width * 2 * len(masks)),
        name="up",
    )(side, packed, w_up)


PIECES = ((0, 2), (1, 3))


def pack_up_kernel(side, layout, *refs, mask):
    gathered, (w_ref, packed_ref, out_ref, buffer, sems) = refs[:-5], refs[-5:]
    width = out_ref.shape[1]

    def copy_of(t):
        column = pl.multiple_of((side[0] ^ mask) * 2 * width, width)
        return tile_copy(w_ref, 0, buffer.shape[0], column, buffer, sems, t, UP_TILE)

    for t in range(width // UP_TILE):
        copy_of(t).start()
    rows, depth = packed_ref.shape
    per = gathered[0].shape[0]
    lane = lax.broadcasted_iota(i32, (rows, per), 1)
    row = lax.broadcasted_iota(i32, (rows, per), 0)
    devices = len(gathered) * (per // PAD)
    picks = []
    for part in range(len(gathered)):
        target = jnp.full((rows, per), -1, i32)
        for piece, mask in enumerate(PIECES[part % 2]):
            place = part // 2 * 4 + mask
            base, count = layout[place], layout[devices + place]
            inside = lane - piece * PAD
            mine = jnp.logical_and(inside >= 0, inside < count)
            target = jnp.where(mine, base + inside, target)
        picks.append((target == row).astype(f32).astype(bf16))
    pick = jnp.concatenate(picks, axis=1)

    @pl.loop(0, depth // DOWN_TILE)
    def _(t):
        at = pl.ds(pl.multiple_of(t * DOWN_TILE, DOWN_TILE), DOWN_TILE)
        pieces = jnp.concatenate([part[:, at] for part in gathered], axis=0)
        packed_ref[:, at] = jnp.dot(pick, pieces, preferred_element_type=f32).astype(bf16)

    @pl.loop(0, width // UP_TILE)
    def _(t):
        copy_of(t).wait()
        at = pl.ds(pl.multiple_of(t * UP_TILE, UP_TILE), UP_TILE)
        out_ref[:, at] = jnp.dot(
            packed_ref[...], buffer[:, at], preferred_element_type=f32
        ).astype(bf16)


def pack_up(side, layout, gathered, w_up, rows, width, mask):
    depth = w_up.shape[0]
    vmem, smem = pl.BlockSpec(memory_space=pltpu.VMEM), pl.BlockSpec(memory_space=pltpu.SMEM)
    return pl.pallas_call(
        functools.partial(pack_up_kernel, mask=mask),
        in_specs=[smem, smem] + [vmem] * len(gathered) + [pl.BlockSpec(memory_space=pl.ANY)],
        out_specs=[vmem, vmem],
        out_shape=[
            jax.ShapeDtypeStruct((rows, depth), bf16),
            jax.ShapeDtypeStruct((rows, width), bf16),
        ],
        scratch_shapes=[
            pltpu.VMEM((depth, width), bf16),
            pltpu.SemaphoreType.DMA((width // UP_TILE,)),
        ],
        compiler_params=params(24),
        cost_estimate=cost(2 * rows * depth * width, depth * width * 2),
        name="pack_up",
    )(side, layout, *gathered, w_up)


def down_kernel(side, *refs, first, blocks, ahead):
    refs = list(refs)
    actives, w_ref = [refs.pop(0) for _ in blocks], refs.pop(0)
    before_ref = None if first else refs.pop(0)
    out_ref = refs.pop(0)
    next_ref = refs.pop(0) if ahead is not None else None
    buffer, sems = refs.pop(0), refs.pop(0)
    depth, width = buffer.shape[1:]
    tiles = width // DOWN_TILE

    def copy_of(block, buffer, sems, t):
        row = pl.multiple_of(((side[0] ^ block[0]) * 2 + block[1]) * depth, depth)
        return tile_copy(w_ref, row, depth, 0, buffer, sems, t, DOWN_TILE)

    for t in range(tiles):
        for n, block in enumerate(blocks):
            copy_of(block, buffer.at[n], sems.at[n], t).start()
    if ahead is not None:
        for t in range(tiles):
            copy_of(ahead, next_ref, refs[0], t).start()

    @pl.loop(0, tiles)
    def _(t):
        at = pl.ds(pl.multiple_of(t * DOWN_TILE, DOWN_TILE), DOWN_TILE)
        total = None if first else before_ref[:, at]
        for n, block in enumerate(blocks):
            copy_of(block, buffer.at[n], sems.at[n], t).wait()
            part = jnp.dot(actives[n][...], buffer[n, :, at], preferred_element_type=f32)
            total = part if total is None else total + part
        out_ref[:, at] = total

    if ahead is not None:

        @pl.loop(0, tiles)
        def _(t):
            copy_of(ahead, next_ref, refs[0], t).wait()


def down(side, actives, w_down, before, blocks, ahead=None):
    rows, depth = actives[0].shape
    width = w_down.shape[1]
    tiles = width // DOWN_TILE
    vmem, smem = pl.BlockSpec(memory_space=pltpu.VMEM), pl.BlockSpec(memory_space=pltpu.SMEM)
    out = jax.ShapeDtypeStruct((rows, width), f32)
    return pl.pallas_call(
        functools.partial(down_kernel, first=before is None, blocks=blocks, ahead=ahead),
        in_specs=[smem] + [vmem] * len(blocks) + [pl.BlockSpec(memory_space=pl.ANY)]
        + ([] if before is None else [vmem]),
        out_specs=vmem if ahead is None else [vmem, vmem],
        out_shape=out if ahead is None else [out, pltpu.VMEM((depth, width), bf16)],
        scratch_shapes=[
            pltpu.VMEM((len(blocks), depth, width), bf16),
            pltpu.SemaphoreType.DMA((len(blocks), tiles)),
        ]
        + ([] if ahead is None else [pltpu.SemaphoreType.DMA((tiles,))]),
        compiler_params=params(24),
        cost_estimate=cost(2 * rows * depth * width, depth * width * 2),
        name="down",
    )(side, *actives, w_down, *([] if before is None else [before]))


BACK = (2, 3, 0, 1)


def down_unpack_kernel(layout, a_ref, w_ref, before_ref, stay_ref, leave_ref, wide):
    rows = a_ref.shape[0]
    tiles, devices = wide.shape[:2]
    row = lax.broadcasted_iota(i32, (PAD, rows), 0)
    column = lax.broadcasted_iota(i32, (PAD, rows), 1)
    picks = []
    for other in (2, 0, 3, 1):
        for mask in BACK:
            place = other * len(BACK) + mask
            base, count = layout[place], layout[devices + place]
            picks.append(jnp.logical_and(column - row == base, row < count).astype(f32))
    pick = jnp.concatenate(picks, axis=0).astype(bf16)

    @pl.loop(0, tiles)
    def _(t):
        at = pl.ds(pl.multiple_of(t * DOWN_TILE, DOWN_TILE), DOWN_TILE)
        share = before_ref[:, at] + jnp.dot(a_ref[...], w_ref[:, at], preferred_element_type=f32)
        back = jnp.dot(pick, share.astype(bf16), preferred_element_type=f32)
        wide[t] = back.reshape(devices, PAD, DOWN_TILE)

    per = tiles * LIVE_CAP
    for n, out in enumerate((stay_ref, leave_ref)):

        @pl.loop(0, devices // 2)
        def _(device):
            here = [wide[t, n * (devices // 2) + device, :LIVE_CAP, :] for t in range(tiles)]
            rows = pl.ds(pl.multiple_of(device * per, per), per)
            out[rows, :] = jnp.concatenate(here, axis=0).astype(bf16)


def down_unpack(layout, active, weights, before):
    rows, depth = active.shape
    width = weights.shape[1]
    tiles, devices = width // DOWN_TILE, layout.shape[0] // 2
    vmem, smem = pl.BlockSpec(memory_space=pltpu.VMEM), pl.BlockSpec(memory_space=pltpu.SMEM)
    out = jax.ShapeDtypeStruct((devices // 2 * tiles * LIVE_CAP, DOWN_TILE), bf16)
    return pl.pallas_call(
        down_unpack_kernel,
        in_specs=[smem, vmem, vmem, vmem],
        out_specs=[vmem] * 2,
        out_shape=[out] * 2,
        scratch_shapes=[pltpu.VMEM((tiles, devices, PAD, DOWN_TILE), f32)],
        compiler_params=params(24),
        cost_estimate=cost(2 * rows * depth * width, rows * width * 4),
        name="down_unpack",
    )(layout, active, weights, before)


def finish_kernel(lengths, side, *refs):
    out_ref = refs[-1]
    sides = (len(refs) - 3) // 2
    mixed, squares, blocks = refs[:sides], refs[sides : sides + 2], refs[sides + 2 : -1]
    slots, width = out_ref.shape
    step = width // sides
    total = squares[0][...] + squares[1][...]
    root = lax.rsqrt(jnp.sum(total, axis=-1, keepdims=True) / width + epsilon)
    gain = root * root
    tiles = step // DOWN_TILE
    picks = [
        live_pick(lengths, slots, tiles * LIVE_CAP, t * LIVE_CAP, True)[0] for t in range(tiles)
    ]
    for shift in range(sides):
        base = (side[0] ^ shift) * step
        block = blocks[shift][...]
        for t in range(tiles):
            back = jnp.dot(picks[t], block, preferred_element_type=f32)[:slots]
            at = pl.multiple_of(base + t * DOWN_TILE, DOWN_TILE)
            here = mixed[shift][:, t * DOWN_TILE : (t + 1) * DOWN_TILE]
            out_ref[:, pl.ds(at, DOWN_TILE)] = (here + gain * back).astype(bf16)


def finish(ctx_len, side, mixed, squares, blocks):
    vmem, smem = pl.BlockSpec(memory_space=pltpu.VMEM), pl.BlockSpec(memory_space=pltpu.SMEM)
    slots, width = mixed[0].shape[0], mixed[0].shape[1] * len(mixed)
    return pl.pallas_call(
        finish_kernel,
        in_specs=[smem, smem] + [vmem] * (2 * len(mixed) + 2),
        out_specs=vmem,
        out_shape=jax.ShapeDtypeStruct((slots, width), bf16),
        compiler_params=params(16),
        cost_estimate=cost(slots * width * 32, slots * width * 8),
        name="finish",
    )(ctx_len, side, *mixed, *squares, *blocks)


def swap(x, axis, count, mask):
    return lax.ppermute(x, axis, [(j, j ^ mask) for j in range(count)])


def added(a, b):
    return (a.astype(f32) + b.astype(f32)).astype(bf16)


def tie(x, *others):
    return lax.optimization_barrier((x, *others))[0]


def squared_relu(*terms):
    lifted = sum(term.astype(f32) for term in terms)
    clipped = jnp.maximum(lifted, 0.0)
    return (clipped * clipped).astype(bf16)


def feed_forward(rows, side, layout, gathered, w_up, w_down):
    half = w_up.shape[1] // 8
    across = lambda x: swap(x, "side", 4, 2)
    beside = lambda x: swap(x, "side", 4, 1)
    packed, other_0 = pack_up(side, layout, gathered, w_up, rows, half, 3)
    met_0 = beside(other_0)
    far = up(side, packed, w_up, half, ((3, 1), (2, 0), (2, 1)))
    met_1 = beside(far[0])
    sum_0 = added(far[1], met_0)
    crossed_0 = across(sum_0)
    near = up(side, tie(packed, sum_0), w_up, half, ((1, 0), (1, 1)))
    met_1, near = lax.optimization_barrier((met_1, near))
    sum_1 = added(far[2], met_1)
    crossed_1 = across(sum_1)
    near = beside(near)
    own = up(side, tie(packed, sum_1), w_up, half, ((0, 0), (0, 1)))
    active_0 = squared_relu(own[0], near[0], crossed_0)
    over_0 = across(active_0)
    active_1 = squared_relu(own[1], near[1], crossed_1)
    over_1 = across(active_1)
    following = beside(jnp.concatenate([active_0, active_1], axis=0))
    total = down(side, [active_0, active_1], w_down, None, ((0, 0), (0, 1)))
    over_0 = tie(over_0, total)
    forward_0, forward_1 = beside(over_0), beside(over_1)
    following = [following[:rows], following[rows:]]
    total = down(side, [*following, over_0], w_down, total, ((1, 0), (1, 1), (2, 0)))
    total, weights = down(
        side, [over_1, forward_0], w_down, total, ((2, 1), (3, 0)), ahead=(3, 1)
    )
    return down_unpack(layout, forward_1, weights, total)


def layout_kernel(side, shard, *refs, limits):
    parts, out, step_out = refs[:-2], refs[-2], refs[-1]
    pieces = parts[0].shape[0] // PAD
    devices = len(parts) * pieces
    counts, places = [None] * devices, [None] * devices
    for part in range(len(parts)):
        for piece, mask in enumerate(PIECES[part % 2]):
            last = parts[part][piece * PAD : (piece + 1) * PAD, :].astype(f32)[PAD - 1 :]
            place = part // 2 * 4 + mask
            counts[place] = jnp.max(last).astype(i32)
            places[place] = (side[0] ^ mask) * 4 + (shard[0] ^ (part // 2))
    total = jnp.int32(0)
    for one in range(devices):
        base = jnp.int32(0)
        for other in range(devices):
            base = base + jnp.where(places[other] < places[one], counts[other], 0)
        out[one] = base
        out[devices + one] = counts[one]
        total = total + counts[one]
    step = jnp.int32(0)
    for limit in limits:
        step = step + (total > limit).astype(i32)
    step_out[0] = step


def read_layout(side, shard, gathered, limits):
    per = gathered[0].shape[0]
    pieces = per // PAD
    scalars = pl.BlockSpec(memory_space=pltpu.SMEM)
    return pl.pallas_call(
        functools.partial(layout_kernel, limits=limits),
        grid=(1,),
        in_specs=[scalars, scalars] + [pl.BlockSpec((per, 128), lambda t: (0, 0))] * len(gathered),
        out_specs=[scalars, scalars],
        out_shape=[
            jax.ShapeDtypeStruct((2 * len(gathered) * pieces,), i32),
            jax.ShapeDtypeStruct((1,), i32),
        ],
        compiler_params=params(16),
        name="layout",
    )(side, shard, *gathered)


ROW_STEPS = (112, 120, 128, 136, 144, 160, 192)


def line_shards(
    queries, new_kv, kv_pool, page_table, ctx_len, residual_in, norm_gain, w_up, w_down
):
    i, s = lax.axis_index("side"), lax.axis_index("shard")
    side, shard = i.reshape(1), s.reshape(1)
    in_hbm = lambda x: pltpu.with_memory_space_constraint(x, pltpu.HBM)
    gain = norm_gain.reshape(-1, HEAD)
    inputs = queries, new_kv, kv_pool, page_table, ctx_len, residual_in, gain
    inputs, w_up, w_down = jax.tree.map(in_hbm, (inputs, w_up, w_down))
    ctx_len = inputs[4]
    (to_2, to_3), mixed_far, squares_far, copies = attend(inputs, side, 4, (2, 3), None)
    met = swap(jnp.concatenate([to_2, to_3], axis=0), "side", 4, 2)
    (own, to_1), mixed_near, squares_near, _ = attend(inputs, side, 4, (0, 1), copies)
    first = jnp.concatenate([own, met[:PAD]], axis=0)
    second = swap(jnp.concatenate([to_1, met[PAD:]], axis=0), "side", 4, 1)
    gathered = []
    by_x = [swap(here, "shard", 4, 2) for here in (first, second)]
    by_core = [swap(here, "shard", 4, 1) for here in (first, second)]
    by_both = [swap(there, "shard", 4, 1) for there in by_x]
    gathered = [first, second, *by_core, *by_x, *by_both]
    layout, step = read_layout(side, shard, gathered, ROW_STEPS[:-1])
    stay, leave = lax.switch(
        step[0],
        [functools.partial(feed_forward, rows) for rows in ROW_STEPS],
        side, layout, gathered, w_up, w_down,
    )
    back = swap(leave, "shard", 4, 1)
    quarter = back.shape[0] // 4
    piece = quarter // 2
    sums = [added(stay[at : at + quarter], back[at : at + quarter]) for at in range(0, 4 * quarter, quarter)]
    far = added(sums[2], swap(sums[0], "shard", 4, 2))
    near = added(sums[3], swap(sums[1], "shard", 4, 2))
    home = near[:piece], near[piece:], far[:piece], far[piece:]
    blocks = [home[0]] + [swap(home[mask], "side", 4, mask) for mask in (1, 2, 3)]
    mixed = [*mixed_near, *mixed_far]
    return finish(ctx_len, side, mixed, [squares_far, squares_near], blocks)


def attend_slots(queries, new_kv, pool_pages, page_rows, lengths):
    slot_count = queries.shape[0]
    positions = page_rows.shape[1] * pool_pages.shape[1]
    fetched = pool_pages[page_rows].reshape(slot_count, positions, 2, KV_HEADS, HEAD)
    fresh_kv = new_kv.reshape(slot_count, 2, KV_HEADS, HEAD)
    query_heads = queries.reshape(slot_count, KV_HEADS, GROUP, HEAD)
    score_scale = 1.0 / math.sqrt(HEAD)
    scores = (
        jnp.einsum("sgqd,slgd->sgql", query_heads, fetched[:, :, 0], preferred_element_type=f32)
        * score_scale
    )
    own_score = (
        jnp.einsum("sgqd,sgd->sgq", query_heads, fresh_kv[:, 0], preferred_element_type=f32)
        * score_scale
    )
    visible = (jnp.arange(positions, dtype=i32)[None, :] < lengths[:, None])[:, None, None, :]
    scores = jnp.where(visible, scores, -1e30)
    highest = jnp.maximum(jnp.max(scores, axis=-1), own_score)
    weights = jnp.where(visible, jnp.exp(scores - highest[..., None]), 0.0)
    own_weight = jnp.exp(own_score - highest)
    denominator = jnp.sum(weights, axis=-1) + own_weight
    probabilities = (weights / denominator[..., None]).astype(bf16)
    own_prob = (own_weight / denominator).astype(bf16).astype(f32)
    attended = jnp.einsum(
        "sgql,slgd->sgqd", probabilities, fetched[:, :, 1], preferred_element_type=f32
    )
    attended = attended + own_prob[..., None] * fresh_kv[:, 1].astype(f32)[:, :, None, :]
    return attended.reshape(slot_count, -1)


def any_shards(queries, new_kv, kv_pool, page_table, ctx_len, residual_in, norm_gain, w_up, w_down):
    attended = attend_slots(queries, new_kv, kv_pool, page_table, ctx_len)
    mixed_rows = residual_in.astype(f32) + attended
    mean_square = jnp.mean(mixed_rows * mixed_rows, axis=-1, keepdims=True)
    normed = (mixed_rows * lax.rsqrt(mean_square + epsilon) * norm_gain.astype(f32)).astype(bf16)
    live_mask = ctx_len > 0
    spread = lax.all_to_all(normed, "side", split_axis=1, concat_axis=0, tiled=True)
    up_partial = jnp.dot(
        lax.all_gather(spread, "shard", axis=0, tiled=True), w_up, preferred_element_type=f32
    )
    lifted = lax.psum(up_partial, "side")
    clipped = jnp.maximum(lifted, 0.0)
    active = (clipped * clipped).astype(bf16)
    down_share = lax.psum_scatter(
        jnp.dot(active, w_down, preferred_element_type=f32).astype(bf16),
        "shard",
        scatter_dimension=0,
        tiled=True,
    )
    returned = lax.all_to_all(down_share, "side", split_axis=0, concat_axis=1, tiled=True)
    returned = jnp.where(live_mask[:, None], returned.astype(f32), 0.0)
    return (mixed_rows + returned).astype(bf16)


def solution(mesh):
    rows = ("grp", "side", "shard")
    placed = (
        P(rows, None),
        P(rows, None),
        P(rows, None, None),
        P(rows, None),
        P(rows),
        P(rows, None),
        P(),
        P("side", "shard"),
        P("shard", "side"),
    )
    square = mesh.shape["side"] == 4 and mesh.shape["shard"] == 4
    return jax.shard_map(
        line_shards if square else any_shards,
        mesh=mesh,
        in_specs=placed,
        out_specs=P(rows, None),
        check_vma=False,
    )
```

```python
import functools
import math

import jax
import jax.numpy as jnp
from jax import lax
from jax.experimental import pallas as pl
from jax.experimental.pallas import tpu as pltpu
from jax.sharding import PartitionSpec as P

KV_HEADS = 8
HEAD = 128
GROUP = 8
LIVE_CAP = 12
PAD = 16

epsilon = 1e-05
bf16, f32, i32 = jnp.bfloat16, jnp.float32, jnp.int32
VMEM_MB = 1 << 20


def params(mb, **more):
    return pltpu.CompilerParams(vmem_limit_bytes=mb * VMEM_MB, **more)


def cost(flops, bytes_accessed):
    return pl.CostEstimate(
        flops=int(flops) // 64, bytes_accessed=int(bytes_accessed) // 64, transcendentals=0
    )


def pad_rows(x):
    rows = x.shape[0]
    if rows == PAD:
        return x
    return jnp.concatenate([x, jnp.zeros((PAD - rows,) + x.shape[1:], x.dtype)], axis=0)


def live_ranks(lengths, slots):
    live, rank, count = [], [], jnp.int32(0)
    for slot in range(slots):
        alive = lengths[slot] > 0
        live.append(alive)
        rank.append(count)
        count = count + alive.astype(i32)
    return live, rank


def token_bias(lengths, table, pages, page):
    slots, entries = table.shape
    tokens = pages * page
    lanes = 128 * ((pages + 127) // 128)
    row = lax.broadcasted_iota(i32, (PAD, lanes), 0)
    column = lax.broadcasted_iota(i32, (PAD, lanes), 1)
    reach = jnp.zeros((PAD, lanes), i32)
    for slot in range(slots):
        reach = jnp.where(row == slot, lengths[slot], reach)
    table = pad_rows(table)
    seen = jnp.zeros((PAD, lanes), i32)
    for entry in range(entries):
        here = jnp.minimum(jnp.maximum(reach - entry * page, 0), page)
        seen = seen + jnp.where(table[:, entry : entry + 1] == column, here, 0)
    spread = (
        lax.broadcasted_iota(i32, (lanes, tokens), 1) // page
        == lax.broadcasted_iota(i32, (lanes, tokens), 0)
    )
    seen_tokens = jnp.dot(
        seen.astype(f32).astype(bf16), spread.astype(f32).astype(bf16), preferred_element_type=f32
    )
    place = (lax.broadcasted_iota(i32, (PAD, tokens), 1) % page).astype(f32)
    return jnp.where(place < seen_tokens, 0.0, -1e30)


def live_pick(lengths, slots, rows, offset, to_slots):
    live, rank = live_ranks(lengths, slots)
    shape = (PAD, rows) if to_slots else (rows, PAD)
    of_slot = lax.broadcasted_iota(i32, shape, 0 if to_slots else 1)
    of_rank = lax.broadcasted_iota(i32, shape, 1 if to_slots else 0) - offset
    pick = jnp.zeros(shape, f32)
    for slot in range(slots):
        chosen = jnp.logical_and(of_rank == rank[slot], of_slot == slot)
        pick = jnp.where(jnp.logical_and(chosen, live[slot]), 1.0, pick)
    return pick.astype(bf16), rank[-1] + live[-1].astype(i32)


POOL_CUTS = 4


def attend_kernel(lengths, side, *refs, masks, sides, first):
    refs = list(refs)
    take = lambda n: [refs.pop(0) for _ in range(n)]
    if first:
        table_ref = refs.pop(0)
        sources = take(4)
    else:
        q_ref, new_ref, res_ref, gain_ref, bias_ref = take(5)
    pool_source = refs.pop(0)
    sends, mixed_refs = take(len(masks)), take(len(masks))
    square_ref = refs.pop(0)
    if first:
        q_ref, new_ref, res_ref, gain_ref, bias_ref, gain_copy, sems = take(7)
    pool_ref, pool_sems = refs
    slots, step = mixed_refs[0].shape
    pages, page, width = pool_source.shape
    columns = width // 2 // sides
    heads = columns // HEAD
    tokens = pages * page
    scale = math.log2(math.e) / math.sqrt(HEAD)

    if first:
        small = [
            pltpu.make_async_copy(source, target, sems.at[n])
            for n, (source, target) in enumerate(
                zip(sources, (q_ref, new_ref, res_ref, gain_copy), strict=True)
            )
        ]
        for copy in small:
            copy.start()
    cut, half, pair = pages // POOL_CUTS, width // 2, columns * 2
    here = ((side[0] ^ masks[0]) // 2) * pair
    brought = []
    for n, at in enumerate((here, half + here)):
        columns_at = pl.ds(pl.multiple_of(at, pair), pair)
        target_at = pl.ds(n * pair, pair)
        brought.append([])
        for c in range(POOL_CUTS):
            rows = pl.ds(c * cut, cut)
            copy = pltpu.make_async_copy(
                pool_source.at[rows, :, columns_at], pool_ref.at[rows, :, target_at], pool_sems.at[n, c]
            )
            copy.start()
            brought[n].append(copy)
    if first:
        bias_ref[...] = token_bias(lengths, table_ref[...], pages, page)
        for copy in small:
            copy.wait()
        gain_ref[...] = gain_copy[...].astype(f32)
    for copy in brought[0]:
        copy.wait()
    values_to_come = brought[1]

    pick, count = live_pick(lengths, slots, PAD, 0, False)
    squares = jnp.zeros((slots, HEAD), f32)
    bias = bias_ref[...][None]
    jobs = [(n, head) for n in range(len(masks)) for head in range(heads)]

    def places(job):
        block, base = side[0] ^ masks[job[0]], job[1] * GROUP * HEAD
        new_at = pl.multiple_of(block * columns, columns) + job[1] * HEAD
        key_at = pl.multiple_of(lax.rem(block, 2) * columns, columns) + job[1] * HEAD
        return block, base, pl.multiple_of(block * step, step) + base, new_at, key_at

    def score(job):
        _, _, start, new_at, key_at = places(job)
        q = jnp.concatenate(
            [pad_rows(q_ref[:, pl.ds(start + g * HEAD, HEAD)]) for g in range(GROUP)], axis=0
        )
        keys = pool_ref[:, :, pl.ds(key_at, HEAD)].reshape(tokens, HEAD)
        new_key = pad_rows(new_ref[:, pl.ds(new_at, HEAD)]).astype(f32)
        scores = lax.dot_general(q, keys, (((1,), (1,)), ((), ())), preferred_element_type=f32)
        own = jnp.sum(
            q.astype(f32).reshape(GROUP, PAD, HEAD) * new_key[None], axis=-1, keepdims=True
        )
        return scores.reshape(GROUP, PAD, tokens), own * scale

    ready = score(jobs[0])
    for number, job in enumerate(jobs):
        block, base, start, new_at, key_at = places(job)
        scores, own = ready
        if number + 1 < len(jobs):
            ready = score(jobs[number + 1])
        scores = scores * scale + bias
        highest = jnp.maximum(jnp.max(scores, axis=-1, keepdims=True), own)
        weights = jnp.exp2(scores - highest)
        own_weight = jnp.exp2(own - highest)
        total = jnp.sum(weights, axis=-1, keepdims=True) + own_weight
        for copy in values_to_come:
            copy.wait()
        values_to_come = []
        values = pool_ref[:, :, pl.ds(pair + key_at, HEAD)].reshape(tokens, HEAD)
        new_value = pad_rows(new_ref[:, pl.ds(half + new_at, HEAD)]).astype(f32)
        summed = jnp.dot(
            weights.astype(bf16).reshape(GROUP * PAD, tokens), values, preferred_element_type=f32
        ).reshape(GROUP, PAD, HEAD)
        attended = (summed + own_weight * new_value[None]) / total
        for g in range(GROUP):
            at = slice(base + g * HEAD, base + (g + 1) * HEAD)
            residual = res_ref[:, pl.ds(start + g * HEAD, HEAD)].astype(f32)
            mixed = residual + attended[g][:slots]
            mixed_refs[job[0]][:, at] = mixed
            squares = squares + mixed * mixed
            gain = gain_ref[pl.ds(block * (step // HEAD) + job[1] * GROUP + g, 1), :]
            gained = pad_rows((mixed * gain).astype(bf16))
            rows = jnp.dot(pick, gained, preferred_element_type=f32)
            counted = lax.broadcasted_iota(i32, rows.shape, 0) == PAD - 1
            sends[job[0]][:, at] = jnp.where(counted, count.astype(f32), rows).astype(bf16)
    square_ref[...] = squares


def attend(inputs, side, sides, masks, before):
    queries, new_kv, kv_pool, page_table, ctx_len, residual_in, norm_gain = inputs
    slots, columns = queries.shape
    pages, page, _ = kv_pool.shape
    step = columns // sides
    first = before is None
    vmem, anywhere = pl.BlockSpec(memory_space=pltpu.VMEM), pl.BlockSpec(memory_space=pl.ANY)
    smem = pl.BlockSpec(memory_space=pltpu.SMEM)
    out_shape = [jax.ShapeDtypeStruct((PAD, step), bf16)] * len(masks)
    out_shape += [jax.ShapeDtypeStruct((slots, step), f32)] * len(masks)
    out_shape += [jax.ShapeDtypeStruct((slots, HEAD), f32)]
    if first:
        operands = [page_table, queries, new_kv, residual_in, norm_gain, kv_pool]
        in_specs = [vmem] + [anywhere] * 5
        out_shape += [
            pltpu.VMEM(queries.shape, bf16),
            pltpu.VMEM(new_kv.shape, bf16),
            pltpu.VMEM(residual_in.shape, bf16),
            pltpu.VMEM(norm_gain.shape, f32),
            pltpu.VMEM((PAD, pages * page), f32),
        ]
        scratch = [pltpu.VMEM(norm_gain.shape, bf16), pltpu.SemaphoreType.DMA((4,))]
    else:
        operands = [*before, kv_pool]
        in_specs = [vmem] * len(before) + [anywhere]
        scratch = []
    scratch += [
        pltpu.VMEM((pages, page, kv_pool.shape[2] // sides * 2), bf16),
        pltpu.SemaphoreType.DMA((2, POOL_CUTS)),
    ]
    outs = pl.pallas_call(
        functools.partial(attend_kernel, masks=masks, sides=sides, first=first),
        in_specs=[smem, smem] + in_specs,
        out_specs=[vmem] * len(out_shape),
        out_shape=out_shape,
        scratch_shapes=scratch,
        compiler_params=params(28),
        cost_estimate=cost(2e9, kv_pool.size),
        name="attend",
    )(ctx_len, side, *operands)
    n = len(masks)
    return outs[:n], outs[n : 2 * n], outs[2 * n], outs[2 * n + 1 :]


UP_TILE = 256
DOWN_TILE = 512


def tile_copy(w_ref, row, rows, column, buffer, sems, t, tile):
    at = pl.ds(pl.multiple_of(t * tile, tile), tile)
    source = w_ref.at[pl.ds(row, rows), pl.ds(pl.multiple_of(column + t * tile, tile), tile)]
    return pltpu.make_async_copy(source, buffer.at[:, at], sems.at[t])


def up_kernel(side, x_ref, w_ref, out_ref, buffer, sems, *, masks):
    depth, width = buffer.shape[1:]
    tiles = width // UP_TILE

    def copy_of(n, t):
        column = pl.multiple_of(((side[0] ^ masks[n][0]) * 2 + masks[n][1]) * width, width)
        return tile_copy(w_ref, 0, depth, column, buffer.at[n], sems.at[n], t, UP_TILE)

    for n in range(len(masks)):
        for t in range(tiles):
            copy_of(n, t).start()

    @pl.loop(0, len(masks) * tiles)
    def _(job):
        n, t = lax.div(job, tiles), lax.rem(job, tiles)
        at = pl.ds(pl.multiple_of(t * UP_TILE, UP_TILE), UP_TILE)
        pltpu.make_async_copy(
            w_ref.at[:, pl.ds(0, UP_TILE)], buffer.at[n, :, at], sems.at[n, t]
        ).wait()
        out_ref[n, :, at] = jnp.dot(
            x_ref[: out_ref.shape[1], :], buffer[n, :, at], preferred_element_type=f32
        ).astype(out_ref.dtype)


def up(side, packed, w_up, rows, width, masks):
    depth = packed.shape[1]
    vmem, smem = pl.BlockSpec(memory_space=pltpu.VMEM), pl.BlockSpec(memory_space=pltpu.SMEM)
    return pl.pallas_call(
        functools.partial(up_kernel, masks=masks),
        in_specs=[smem, vmem, pl.BlockSpec(memory_space=pl.ANY)],
        out_specs=vmem,
        out_shape=jax.ShapeDtypeStruct((len(masks), rows, width), bf16),
        scratch_shapes=[
            pltpu.VMEM((len(masks), depth, width), bf16),
            pltpu.SemaphoreType.DMA((len(masks), width // UP_TILE)),
        ],
        compiler_params=params(24),
        cost_estimate=cost(2 * rows * depth * width, depth * width * 2 * len(masks)),
        name="up",
    )(side, packed, w_up)


PIECES = ((0, 2), (1, 3))


def find_layout(side, shard, gathered, layout, step_ref, limits):
    pieces = gathered[0].shape[0] // PAD
    devices = len(gathered) * pieces
    counts, places = [None] * devices, [None] * devices
    for part in range(len(gathered)):
        for piece, mask in enumerate(PIECES[part % 2]):
            last = gathered[part][piece * PAD : (piece + 1) * PAD, :HEAD].astype(f32)[PAD - 1 :]
            place = part // 2 * 4 + mask
            counts[place] = jnp.max(last).astype(i32)
            places[place] = (side[0] ^ mask) * 4 + (shard[0] ^ (part // 2))
    total = jnp.int32(0)
    for one in range(devices):
        base = jnp.int32(0)
        for other in range(devices):
            base = base + jnp.where(places[other] < places[one], counts[other], 0)
        layout[one] = base
        layout[devices + one] = counts[one]
        total = total + counts[one]
    step = jnp.int32(0)
    for limit in limits:
        step = step + (total > limit).astype(i32)
    step_ref[0] = step


def pack_up_kernel(side, shard, *refs, mask, limits):
    gathered, refs = refs[:-7], refs[-7:]
    w_ref, packed_ref, out_ref, layout, step_ref, buffer, sems = refs
    width = out_ref.shape[1]

    def copy_of(t):
        column = pl.multiple_of((side[0] ^ mask) * 2 * width, width)
        return tile_copy(w_ref, 0, buffer.shape[0], column, buffer, sems, t, UP_TILE)

    for t in range(width // UP_TILE):
        copy_of(t).start()
    find_layout(side, shard, gathered, layout, step_ref, limits)
    rows, depth = packed_ref.shape
    per = gathered[0].shape[0]
    lane = lax.broadcasted_iota(i32, (rows, per), 1)
    row = lax.broadcasted_iota(i32, (rows, per), 0)
    devices = len(gathered) * (per // PAD)
    picks = []
    for part in range(len(gathered)):
        target = jnp.full((rows, per), -1, i32)
        for piece, mask in enumerate(PIECES[part % 2]):
            place = part // 2 * 4 + mask
            base, count = layout[place], layout[devices + place]
            inside = lane - piece * PAD
            mine = jnp.logical_and(inside >= 0, inside < count)
            target = jnp.where(mine, base + inside, target)
        picks.append((target == row).astype(f32).astype(bf16))
    pick = jnp.concatenate(picks, axis=1)

    @pl.loop(0, depth // DOWN_TILE)
    def _(t):
        at = pl.ds(pl.multiple_of(t * DOWN_TILE, DOWN_TILE), DOWN_TILE)
        pieces = jnp.concatenate([part[:, at] for part in gathered], axis=0)
        packed_ref[:, at] = jnp.dot(pick, pieces, preferred_element_type=f32).astype(bf16)

    @pl.loop(0, width // UP_TILE)
    def _(t):
        copy_of(t).wait()
        at = pl.ds(pl.multiple_of(t * UP_TILE, UP_TILE), UP_TILE)
        out_ref[:, at] = jnp.dot(
            packed_ref[...], buffer[:, at], preferred_element_type=f32
        ).astype(bf16)


def pack_up(side, shard, gathered, w_up, rows, width, mask, limits):
    depth = w_up.shape[0]
    devices = len(gathered) * gathered[0].shape[0] // PAD
    vmem, smem = pl.BlockSpec(memory_space=pltpu.VMEM), pl.BlockSpec(memory_space=pltpu.SMEM)
    return pl.pallas_call(
        functools.partial(pack_up_kernel, mask=mask, limits=limits),
        in_specs=[smem, smem] + [vmem] * len(gathered) + [pl.BlockSpec(memory_space=pl.ANY)],
        out_specs=[vmem, vmem, smem, smem],
        out_shape=[
            jax.ShapeDtypeStruct((rows, depth), bf16),
            jax.ShapeDtypeStruct((rows, width), bf16),
            jax.ShapeDtypeStruct((2 * devices,), i32),
            jax.ShapeDtypeStruct((1,), i32),
        ],
        scratch_shapes=[
            pltpu.VMEM((depth, width), bf16),
            pltpu.SemaphoreType.DMA((width // UP_TILE,)),
        ],
        compiler_params=params(24),
        cost_estimate=cost(2 * rows * depth * width, depth * width * 2),
        name="pack_up",
    )(side, shard, *gathered, w_up)


def down_kernel(side, *refs, first, mask, ahead):
    refs = list(refs)
    a_ref, w_ref = refs.pop(0), refs.pop(0)
    before_ref = None if first else refs.pop(0)
    out_ref = refs.pop(0)
    next_ref = refs.pop(0) if ahead is not None else None
    buffer, sems = refs.pop(0), refs.pop(0)
    depth, width = buffer.shape
    tiles = width // DOWN_TILE

    def copy_of(other, buffer, sems, t):
        row = pl.multiple_of((side[0] ^ other) * depth, depth)
        return tile_copy(w_ref, row, depth, 0, buffer, sems, t, DOWN_TILE)

    for t in range(tiles):
        copy_of(mask, buffer, sems, t).start()
    if ahead is not None:
        for t in range(tiles):
            copy_of(ahead, next_ref, refs[0], t).start()

    @pl.loop(0, tiles)
    def _(t):
        at = pl.ds(pl.multiple_of(t * DOWN_TILE, DOWN_TILE), DOWN_TILE)
        copy_of(mask, buffer, sems, t).wait()
        part = jnp.dot(a_ref[...], buffer[:, at], preferred_element_type=f32)
        out_ref[:, at] = part if first else before_ref[:, at] + part

    if ahead is not None:

        @pl.loop(0, tiles)
        def _(t):
            copy_of(ahead, next_ref, refs[0], t).wait()


def down(side, active, w_down, before, mask, ahead=None):
    rows, depth = active.shape
    width = w_down.shape[1]
    vmem, smem = pl.BlockSpec(memory_space=pltpu.VMEM), pl.BlockSpec(memory_space=pltpu.SMEM)
    out = jax.ShapeDtypeStruct((rows, width), f32)
    sems = pltpu.SemaphoreType.DMA((width // DOWN_TILE,))
    return pl.pallas_call(
        functools.partial(down_kernel, first=before is None, mask=mask, ahead=ahead),
        in_specs=[smem, vmem, pl.BlockSpec(memory_space=pl.ANY)]
        + ([] if before is None else [vmem]),
        out_specs=vmem if ahead is None else [vmem, vmem],
        out_shape=out if ahead is None else [out, pltpu.VMEM((depth, width), bf16)],
        scratch_shapes=[pltpu.VMEM((depth, width), bf16), sems]
        + ([] if ahead is None else [sems]),
        compiler_params=params(24),
        cost_estimate=cost(2 * rows * depth * width, depth * width * 2),
        name="down",
    )(side, active, w_down, *([] if before is None else [before]))


BACK = ((2, 3), (0, 1))


def down_unpack_kernel(layout, a_ref, w_ref, before_ref, *refs):
    outs, wide = refs[:-1], refs[-1]
    rows = a_ref.shape[0]
    tiles, devices = wide.shape[:2]
    group = devices // len(outs)
    row = lax.broadcasted_iota(i32, (PAD, rows), 0)
    column = lax.broadcasted_iota(i32, (PAD, rows), 1)
    picks = []
    for core in (0, 1):
        for x in (2, 0):
            for masks in BACK:
                for mask in masks:
                    place = (x + core) * 4 + mask
                    base, count = layout[place], layout[devices + place]
                    picks.append(jnp.logical_and(column - row == base, row < count).astype(f32))
    pick = jnp.concatenate(picks, axis=0).astype(bf16)

    @pl.loop(0, tiles)
    def _(t):
        at = pl.ds(pl.multiple_of(t * DOWN_TILE, DOWN_TILE), DOWN_TILE)
        share = before_ref[:, at] + jnp.dot(a_ref[...], w_ref[:, at], preferred_element_type=f32)
        back = jnp.dot(pick, share.astype(bf16), preferred_element_type=f32)
        wide[t] = back.reshape(devices, PAD, DOWN_TILE)

    per = tiles * LIVE_CAP
    for n, out in enumerate(outs):

        @pl.loop(0, group)
        def _(device):
            here = [wide[t, n * group + device, :LIVE_CAP, :] for t in range(tiles)]
            rows = pl.ds(pl.multiple_of(device * per, per), per)
            out[rows, :] = jnp.concatenate(here, axis=0).astype(bf16)


def down_unpack(layout, active, weights, before):
    rows, depth = active.shape
    width = weights.shape[1]
    tiles, devices = width // DOWN_TILE, layout.shape[0] // 2
    vmem, smem = pl.BlockSpec(memory_space=pltpu.VMEM), pl.BlockSpec(memory_space=pltpu.SMEM)
    out = jax.ShapeDtypeStruct((devices // 2 * tiles * LIVE_CAP, DOWN_TILE), bf16)
    return pl.pallas_call(
        down_unpack_kernel,
        in_specs=[smem, vmem, vmem, vmem],
        out_specs=[vmem] * 2,
        out_shape=[out] * 2,
        scratch_shapes=[pltpu.VMEM((tiles, devices, PAD, DOWN_TILE), f32)],
        compiler_params=params(24),
        cost_estimate=cost(2 * rows * depth * width, rows * width * 4),
        name="down_unpack",
    )(layout, active, weights, before)


def finish_kernel(lengths, side, *refs):
    out_ref = refs[-1]
    sides = (len(refs) - 3) // 2
    mixed, squares, blocks = refs[:sides], refs[sides : sides + 2], refs[sides + 2 : -1]
    slots, width = out_ref.shape
    step = width // sides
    total = squares[0][...] + squares[1][...]
    root = lax.rsqrt(jnp.sum(total, axis=-1, keepdims=True) / width + epsilon)
    gain = root * root
    tiles = step // DOWN_TILE
    picks = [
        live_pick(lengths, slots, tiles * LIVE_CAP, t * LIVE_CAP, True)[0] for t in range(tiles)
    ]
    for shift in range(sides):
        base = (side[0] ^ shift) * step
        block = blocks[shift][...]
        for t in range(tiles):
            back = jnp.dot(picks[t], block, preferred_element_type=f32)[:slots]
            at = pl.multiple_of(base + t * DOWN_TILE, DOWN_TILE)
            here = mixed[shift][:, t * DOWN_TILE : (t + 1) * DOWN_TILE]
            out_ref[:, pl.ds(at, DOWN_TILE)] = (here + gain * back).astype(bf16)


def finish(ctx_len, side, mixed, squares, blocks):
    vmem, smem = pl.BlockSpec(memory_space=pltpu.VMEM), pl.BlockSpec(memory_space=pltpu.SMEM)
    slots, width = mixed[0].shape[0], mixed[0].shape[1] * len(mixed)
    return pl.pallas_call(
        finish_kernel,
        in_specs=[smem, smem] + [vmem] * (2 * len(mixed) + 2),
        out_specs=vmem,
        out_shape=jax.ShapeDtypeStruct((slots, width), bf16),
        compiler_params=params(16),
        cost_estimate=cost(slots * width * 32, slots * width * 8),
        name="finish",
    )(ctx_len, side, *mixed, *squares, *blocks)


def swap(x, axis, count, mask):
    return lax.ppermute(x, axis, [(j, j ^ mask) for j in range(count)])


def added(a, b):
    return (a.astype(f32) + b.astype(f32)).astype(bf16)


def tie(x, *others):
    return lax.optimization_barrier((x, *others))[0]


def squared_relu(*terms):
    lifted = sum(term.astype(f32) for term in terms)
    clipped = jnp.maximum(lifted, 0.0)
    return (clipped * clipped).astype(bf16)


def feed_forward(rows, side, layout, packed, other, w_up, w_down):
    half = w_up.shape[1] // 8
    across = lambda x: swap(x, "side", 4, 2)
    beside = lambda x: swap(x, "side", 4, 1)
    met_0 = beside(other[:rows])
    far = up(side, packed, w_up, rows, half, ((3, 1), (2, 0), (2, 1)))
    met_1 = beside(far[0])
    sum_0 = added(far[1], met_0)
    crossed_0 = across(sum_0)
    near = up(side, tie(packed, sum_0), w_up, rows, half, ((1, 0), (1, 1)))
    met_1, near = lax.optimization_barrier((met_1, near))
    sum_1 = added(far[2], met_1)
    crossed_1 = across(sum_1)
    near = beside(near)
    own = up(side, tie(packed, sum_1), w_up, rows, half, ((0, 0), (0, 1)))
    active = [squared_relu(own[n], near[n], crossed) for n, crossed in enumerate((crossed_0, crossed_1))]
    active = jnp.concatenate(active, axis=1)
    over, following = across(active), beside(active)
    total = down(side, active, w_down, None, 0)
    forward = beside(tie(over, total))
    total = down(side, following, w_down, total, 1)
    total, weights = down(side, over, w_down, total, 2, ahead=3)
    return down_unpack(layout, forward, weights, total)


ROW_STEPS = (112, 120, 128, 136, 144, 160, 192)


def line_shards(
    queries, new_kv, kv_pool, page_table, ctx_len, residual_in, norm_gain, w_up, w_down
):
    i, s = lax.axis_index("side"), lax.axis_index("shard")
    side, shard = i.reshape(1), s.reshape(1)
    in_hbm = lambda x: pltpu.with_memory_space_constraint(x, pltpu.HBM)
    gain = norm_gain.reshape(-1, HEAD)
    inputs = queries, new_kv, kv_pool, page_table, ctx_len, residual_in, gain
    inputs, w_up, w_down = jax.tree.map(in_hbm, (inputs, w_up, w_down))
    ctx_len = inputs[4]
    (to_2, to_3), mixed_far, squares_far, copies = attend(inputs, side, 4, (2, 3), None)
    met = swap(jnp.concatenate([to_2, to_3], axis=0), "side", 4, 2)
    (own, to_1), mixed_near, squares_near, _ = attend(inputs, side, 4, (0, 1), copies)
    first = jnp.concatenate([own, met[:PAD]], axis=0)
    second = swap(jnp.concatenate([to_1, met[PAD:]], axis=0), "side", 4, 1)
    gathered = []
    by_x = [swap(here, "shard", 4, 2) for here in (first, second)]
    by_core = [swap(here, "shard", 4, 1) for here in (first, second)]
    by_both = [swap(there, "shard", 4, 1) for there in by_x]
    gathered = [first, second, *by_core, *by_x, *by_both]
    packed, other, layout, step = pack_up(
        side, shard, gathered, w_up, ROW_STEPS[-1], w_up.shape[1] // 8, 3, ROW_STEPS[:-1]
    )
    stay, leave = lax.switch(
        step[0],
        [functools.partial(feed_forward, rows) for rows in ROW_STEPS],
        side, layout, packed, other, w_up, w_down,
    )
    back = swap(leave, "shard", 4, 1)
    quarter = back.shape[0] // 4
    piece = quarter // 2
    cuts = [slice(at, at + quarter) for at in range(0, 4 * quarter, quarter)]
    sums = [added(stay[cut], back[cut]) for cut in cuts]
    far = added(sums[2], swap(sums[0], "shard", 4, 2))
    near = added(sums[3], swap(sums[1], "shard", 4, 2))
    home = near[:piece], near[piece:], far[:piece], far[piece:]
    blocks = [home[0]] + [swap(home[mask], "side", 4, mask) for mask in (1, 2, 3)]
    mixed = [*mixed_near, *mixed_far]
    return finish(ctx_len, side, mixed, [squares_far, squares_near], blocks)


def attend_slots(queries, new_kv, pool_pages, page_rows, lengths):
    slot_count = queries.shape[0]
    positions = page_rows.shape[1] * pool_pages.shape[1]
    fetched = pool_pages[page_rows].reshape(slot_count, positions, 2, KV_HEADS, HEAD)
    fresh_kv = new_kv.reshape(slot_count, 2, KV_HEADS, HEAD)
    query_heads = queries.reshape(slot_count, KV_HEADS, GROUP, HEAD)
    score_scale = 1.0 / math.sqrt(HEAD)
    scores = (
        jnp.einsum("sgqd,slgd->sgql", query_heads, fetched[:, :, 0], preferred_element_type=f32)
        * score_scale
    )
    own_score = (
        jnp.einsum("sgqd,sgd->sgq", query_heads, fresh_kv[:, 0], preferred_element_type=f32)
        * score_scale
    )
    visible = (jnp.arange(positions, dtype=i32)[None, :] < lengths[:, None])[:, None, None, :]
    scores = jnp.where(visible, scores, -1e30)
    highest = jnp.maximum(jnp.max(scores, axis=-1), own_score)
    weights = jnp.where(visible, jnp.exp(scores - highest[..., None]), 0.0)
    own_weight = jnp.exp(own_score - highest)
    denominator = jnp.sum(weights, axis=-1) + own_weight
    probabilities = (weights / denominator[..., None]).astype(bf16)
    own_prob = (own_weight / denominator).astype(bf16).astype(f32)
    attended = jnp.einsum(
        "sgql,slgd->sgqd", probabilities, fetched[:, :, 1], preferred_element_type=f32
    )
    attended = attended + own_prob[..., None] * fresh_kv[:, 1].astype(f32)[:, :, None, :]
    return attended.reshape(slot_count, -1)


def any_shards(queries, new_kv, kv_pool, page_table, ctx_len, residual_in, norm_gain, w_up, w_down):
    attended = attend_slots(queries, new_kv, kv_pool, page_table, ctx_len)
    mixed_rows = residual_in.astype(f32) + attended
    mean_square = jnp.mean(mixed_rows * mixed_rows, axis=-1, keepdims=True)
    normed = (mixed_rows * lax.rsqrt(mean_square + epsilon) * norm_gain.astype(f32)).astype(bf16)
    live_mask = ctx_len > 0
    spread = lax.all_to_all(normed, "side", split_axis=1, concat_axis=0, tiled=True)
    up_partial = jnp.dot(
        lax.all_gather(spread, "shard", axis=0, tiled=True), w_up, preferred_element_type=f32
    )
    lifted = lax.psum(up_partial, "side")
    clipped = jnp.maximum(lifted, 0.0)
    active = (clipped * clipped).astype(bf16)
    down_share = lax.psum_scatter(
        jnp.dot(active, w_down, preferred_element_type=f32).astype(bf16),
        "shard",
        scatter_dimension=0,
        tiled=True,
    )
    returned = lax.all_to_all(down_share, "side", split_axis=0, concat_axis=1, tiled=True)
    returned = jnp.where(live_mask[:, None], returned.astype(f32), 0.0)
    return (mixed_rows + returned).astype(bf16)


def solution(mesh):
    rows = ("grp", "side", "shard")
    placed = (
        P(rows, None),
        P(rows, None),
        P(rows, None, None),
        P(rows, None),
        P(rows),
        P(rows, None),
        P(),
        P("side", "shard"),
        P("shard", "side"),
    )
    square = mesh.shape["side"] == 4 and mesh.shape["shard"] == 4
    return jax.shard_map(
        line_shards if square else any_shards,
        mesh=mesh,
        in_specs=placed,
        out_specs=P(rows, None),
        check_vma=False,
    )
```

```python
import functools
import math

import jax
import jax.numpy as jnp
from jax import lax
from jax.experimental import pallas as pl
from jax.experimental.pallas import tpu as pltpu
from jax.sharding import PartitionSpec as P

KV_HEADS = 8
HEAD = 128
GROUP = 8
LIVE_CAP = 12
PAD = 16
TALL = 2 * LIVE_CAP
EMPTY = 1e30

epsilon = 1e-05
bf16, f32, i32 = jnp.bfloat16, jnp.float32, jnp.int32
VMEM_MB = 1 << 20


def params(mb, **more):
    return pltpu.CompilerParams(vmem_limit_bytes=mb * VMEM_MB, **more)


def cost(flops, bytes_accessed):
    return pl.CostEstimate(
        flops=int(flops) // 64, bytes_accessed=int(bytes_accessed) // 64, transcendentals=0
    )


def pad_rows(x):
    rows = x.shape[0]
    if rows == PAD:
        return x
    return jnp.concatenate([x, jnp.zeros((PAD - rows,) + x.shape[1:], x.dtype)], axis=0)


def live_ranks(lengths, slots):
    live, rank, count = [], [], jnp.int32(0)
    for slot in range(slots):
        alive = lengths[slot] > 0
        live.append(alive)
        rank.append(count)
        count = count + alive.astype(i32)
    return live, rank


def token_bias(lengths, table, pages, page):
    slots, entries = table.shape
    tokens = pages * page
    lanes = 128 * ((pages + 127) // 128)
    row = lax.broadcasted_iota(i32, (PAD, lanes), 0)
    column = lax.broadcasted_iota(i32, (PAD, lanes), 1)
    reach = jnp.zeros((PAD, lanes), i32)
    for slot in range(slots):
        reach = jnp.where(row == slot, lengths[slot], reach)
    table = pad_rows(table)
    seen = jnp.zeros((PAD, lanes), i32)
    for entry in range(entries):
        here = jnp.minimum(jnp.maximum(reach - entry * page, 0), page)
        seen = seen + jnp.where(table[:, entry : entry + 1] == column, here, 0)
    spread = (
        lax.broadcasted_iota(i32, (lanes, tokens), 1) // page
        == lax.broadcasted_iota(i32, (lanes, tokens), 0)
    )
    seen_tokens = jnp.dot(
        seen.astype(f32).astype(bf16), spread.astype(f32).astype(bf16), preferred_element_type=f32
    )
    place = (lax.broadcasted_iota(i32, (PAD, tokens), 1) % page).astype(f32)
    return jnp.where(place < seen_tokens, 0.0, -1e30)


def live_pick(lengths, slots, rows, offset, to_slots):
    live, rank = live_ranks(lengths, slots)
    shape = (PAD, rows) if to_slots else (rows, PAD)
    of_slot = lax.broadcasted_iota(i32, shape, 0 if to_slots else 1)
    of_rank = lax.broadcasted_iota(i32, shape, 1 if to_slots else 0) - offset
    pick = jnp.zeros(shape, f32)
    for slot in range(slots):
        chosen = jnp.logical_and(of_rank == rank[slot], of_slot == slot)
        pick = jnp.where(jnp.logical_and(chosen, live[slot]), 1.0, pick)
    return pick.astype(bf16), rank[-1] + live[-1].astype(i32)


POOL_CUTS = 4


def attend_kernel(lengths, side, *refs, masks, sides, first):
    refs = list(refs)
    take = lambda n: [refs.pop(0) for _ in range(n)]
    if first:
        table_ref = refs.pop(0)
        sources = take(4)
    else:
        q_ref, new_ref, res_ref, gain_ref, bias_ref = take(5)
    pool_source = refs.pop(0)
    sends, mixed_refs = take(len(masks)), take(len(masks))
    square_ref = refs.pop(0)
    if first:
        q_ref, new_ref, res_ref, gain_ref, bias_ref, gain_copy, sems = take(7)
    pool_ref, pool_sems = refs
    slots, step = mixed_refs[0].shape
    pages, page, width = pool_source.shape
    columns = width // 2 // sides
    heads = columns // HEAD
    tokens = pages * page
    scale = math.log2(math.e) / math.sqrt(HEAD)

    if first:
        small = [
            pltpu.make_async_copy(source, target, sems.at[n])
            for n, (source, target) in enumerate(
                zip(sources, (q_ref, new_ref, res_ref, gain_copy), strict=True)
            )
        ]
        for copy in small:
            copy.start()
    cut, half, pair = pages // POOL_CUTS, width // 2, columns * 2
    here = ((side[0] ^ masks[0]) // 2) * pair
    brought = []
    for n, at in enumerate((here, half + here)):
        columns_at = pl.ds(pl.multiple_of(at, pair), pair)
        target_at = pl.ds(n * pair, pair)
        brought.append([])
        for c in range(POOL_CUTS):
            rows = pl.ds(c * cut, cut)
            copy = pltpu.make_async_copy(
                pool_source.at[rows, :, columns_at], pool_ref.at[rows, :, target_at], pool_sems.at[n, c]
            )
            copy.start()
            brought[n].append(copy)
    if first:
        bias_ref[...] = token_bias(lengths, table_ref[...], pages, page)
        for copy in small:
            copy.wait()
        gain_ref[...] = gain_copy[...].astype(f32)
    for copy in brought[0]:
        copy.wait()
    values_to_come = brought[1]

    picks = [live_pick(lengths, slots, TALL, head * LIVE_CAP, False) for head in range(heads)]
    rank = lax.broadcasted_iota(i32, (TALL, HEAD), 0)
    empty = jnp.where(rank < LIVE_CAP, rank, rank - LIVE_CAP) >= picks[0][1]
    squares = jnp.zeros((slots, HEAD), f32)
    bias = bias_ref[...][None]
    jobs = [(n, head) for n in range(len(masks)) for head in range(heads)]

    def places(job):
        block, base = side[0] ^ masks[job[0]], job[1] * GROUP * HEAD
        new_at = pl.multiple_of(block * columns, columns) + job[1] * HEAD
        key_at = pl.multiple_of(lax.rem(block, 2) * columns, columns) + job[1] * HEAD
        return block, base, pl.multiple_of(block * step, step) + base, new_at, key_at

    def score(job):
        _, _, start, new_at, key_at = places(job)
        q = jnp.concatenate(
            [pad_rows(q_ref[:, pl.ds(start + g * HEAD, HEAD)]) for g in range(GROUP)], axis=0
        )
        keys = pool_ref[:, :, pl.ds(key_at, HEAD)].reshape(tokens, HEAD)
        new_key = pad_rows(new_ref[:, pl.ds(new_at, HEAD)]).astype(f32)
        scores = lax.dot_general(q, keys, (((1,), (1,)), ((), ())), preferred_element_type=f32)
        own = jnp.sum(
            q.astype(f32).reshape(GROUP, PAD, HEAD) * new_key[None], axis=-1, keepdims=True
        )
        return scores.reshape(GROUP, PAD, tokens), own * scale

    ready = score(jobs[0])
    for number, job in enumerate(jobs):
        block, base, start, new_at, key_at = places(job)
        scores, own = ready
        if number + 1 < len(jobs):
            ready = score(jobs[number + 1])
        scores = scores * scale + bias
        highest = jnp.maximum(jnp.max(scores, axis=-1, keepdims=True), own)
        weights = jnp.exp2(scores - highest)
        own_weight = jnp.exp2(own - highest)
        total = jnp.sum(weights, axis=-1, keepdims=True) + own_weight
        for copy in values_to_come:
            copy.wait()
        values_to_come = []
        values = pool_ref[:, :, pl.ds(pair + key_at, HEAD)].reshape(tokens, HEAD)
        new_value = pad_rows(new_ref[:, pl.ds(half + new_at, HEAD)]).astype(f32)
        summed = jnp.dot(
            weights.astype(bf16).reshape(GROUP * PAD, tokens), values, preferred_element_type=f32
        ).reshape(GROUP, PAD, HEAD)
        attended = (summed + own_weight * new_value[None]) / total
        for g in range(GROUP):
            at = slice(base + g * HEAD, base + (g + 1) * HEAD)
            residual = res_ref[:, pl.ds(start + g * HEAD, HEAD)].astype(f32)
            mixed = residual + attended[g][:slots]
            mixed_refs[job[0]][:, at] = mixed
            squares = squares + mixed * mixed
            gain = gain_ref[pl.ds(block * (step // HEAD) + job[1] * GROUP + g, 1), :]
            gained = pad_rows((mixed * gain).astype(bf16))
            rows = jnp.dot(picks[job[1]][0], gained, preferred_element_type=f32)
            to = slice(g * HEAD, (g + 1) * HEAD)
            if job[1]:
                rows = jnp.where(empty, EMPTY, rows + sends[job[0]][:, to].astype(f32))
            sends[job[0]][:, to] = rows.astype(bf16)
    square_ref[...] = squares


def attend(inputs, side, sides, masks, before):
    queries, new_kv, kv_pool, page_table, ctx_len, residual_in, norm_gain = inputs
    slots, columns = queries.shape
    pages, page, _ = kv_pool.shape
    step = columns // sides
    first = before is None
    vmem, anywhere = pl.BlockSpec(memory_space=pltpu.VMEM), pl.BlockSpec(memory_space=pl.ANY)
    smem = pl.BlockSpec(memory_space=pltpu.SMEM)
    out_shape = [jax.ShapeDtypeStruct((TALL, step // 2), bf16)] * len(masks)
    out_shape += [jax.ShapeDtypeStruct((slots, step), f32)] * len(masks)
    out_shape += [jax.ShapeDtypeStruct((slots, HEAD), f32)]
    if first:
        operands = [page_table, queries, new_kv, residual_in, norm_gain, kv_pool]
        in_specs = [vmem] + [anywhere] * 5
        out_shape += [
            pltpu.VMEM(queries.shape, bf16),
            pltpu.VMEM(new_kv.shape, bf16),
            pltpu.VMEM(residual_in.shape, bf16),
            pltpu.VMEM(norm_gain.shape, f32),
            pltpu.VMEM((PAD, pages * page), f32),
        ]
        scratch = [pltpu.VMEM(norm_gain.shape, bf16), pltpu.SemaphoreType.DMA((4,))]
    else:
        operands = [*before, kv_pool]
        in_specs = [vmem] * len(before) + [anywhere]
        scratch = []
    scratch += [
        pltpu.VMEM((pages, page, kv_pool.shape[2] // sides * 2), bf16),
        pltpu.SemaphoreType.DMA((2, POOL_CUTS)),
    ]
    outs = pl.pallas_call(
        functools.partial(attend_kernel, masks=masks, sides=sides, first=first),
        in_specs=[smem, smem] + in_specs,
        out_specs=[vmem] * len(out_shape),
        out_shape=out_shape,
        scratch_shapes=scratch,
        compiler_params=params(28),
        cost_estimate=cost(2e9, kv_pool.size),
        name="attend",
    )(ctx_len, side, *operands)
    n = len(masks)
    return outs[:n], outs[n : 2 * n], outs[2 * n], outs[2 * n + 1 :]


UP_TILE = 256
DOWN_TILE = 512


def tile_copy(w_ref, row, rows, column, buffer, sems, t, tile):
    at = pl.ds(pl.multiple_of(t * tile, tile), tile)
    source = w_ref.at[pl.ds(row, rows), pl.ds(pl.multiple_of(column + t * tile, tile), tile)]
    return pltpu.make_async_copy(source, buffer.at[:, at], sems.at[t])


def up_kernel(side, x_ref, w_ref, out_ref, buffer, sems, *, masks):
    depth, width = buffer.shape[1:]
    tiles = width // UP_TILE

    def copy_of(n, t):
        column = pl.multiple_of(((side[0] ^ masks[n][0]) * 2 + masks[n][1]) * width, width)
        return tile_copy(w_ref, 0, depth, column, buffer.at[n], sems.at[n], t, UP_TILE)

    for n in range(len(masks)):
        for t in range(tiles):
            copy_of(n, t).start()

    @pl.loop(0, len(masks) * tiles)
    def _(job):
        n, t = lax.div(job, tiles), lax.rem(job, tiles)
        at = pl.ds(pl.multiple_of(t * UP_TILE, UP_TILE), UP_TILE)
        pltpu.make_async_copy(
            w_ref.at[:, pl.ds(0, UP_TILE)], buffer.at[n, :, at], sems.at[n, t]
        ).wait()
        out_ref[n, :, at] = jnp.dot(
            x_ref[: out_ref.shape[1], :], buffer[n, :, at], preferred_element_type=f32
        ).astype(out_ref.dtype)


def up(side, packed, w_up, rows, width, masks):
    depth = packed.shape[1]
    vmem, smem = pl.BlockSpec(memory_space=pltpu.VMEM), pl.BlockSpec(memory_space=pltpu.SMEM)
    return pl.pallas_call(
        functools.partial(up_kernel, masks=masks),
        in_specs=[smem, vmem, pl.BlockSpec(memory_space=pl.ANY)],
        out_specs=vmem,
        out_shape=jax.ShapeDtypeStruct((len(masks), rows, width), bf16),
        scratch_shapes=[
            pltpu.VMEM((len(masks), depth, width), bf16),
            pltpu.SemaphoreType.DMA((len(masks), width // UP_TILE)),
        ],
        compiler_params=params(24),
        cost_estimate=cost(2 * rows * depth * width, depth * width * 2 * len(masks)),
        name="up",
    )(side, packed, w_up)


PIECES = ((0, 2), (1, 3))


def find_layout(side, shard, gathered, layout, step_ref, limits):
    pieces = gathered[0].shape[0] // TALL
    devices = len(gathered) * pieces
    counts, places = [None] * devices, [None] * devices
    number = lax.broadcasted_iota(i32, (LIVE_CAP, HEAD), 0) + 1
    for part in range(len(gathered)):
        marks = gathered[part][:, :HEAD].astype(f32)
        for piece, mask in enumerate(PIECES[part % 2]):
            rows = marks[piece * TALL : piece * TALL + LIVE_CAP]
            last = jnp.where(rows < EMPTY / 2, number, 0).astype(f32)
            place = part // 2 * 4 + mask
            counts[place] = jnp.max(last).astype(i32)
            places[place] = (side[0] ^ mask) * 4 + (shard[0] ^ (part // 2))
    total = jnp.int32(0)
    for one in range(devices):
        base = jnp.int32(0)
        for other in range(devices):
            base = base + jnp.where(places[other] < places[one], counts[other], 0)
        layout[one] = base
        layout[devices + one] = counts[one]
        total = total + counts[one]
    step = jnp.int32(0)
    for limit in limits:
        step = step + (total > limit).astype(i32)
    step_ref[0] = step


def pack_up_kernel(side, shard, *refs, mask, limits):
    gathered, refs = refs[:-7], refs[-7:]
    w_ref, packed_ref, out_ref, layout, step_ref, buffer, sems = refs
    width = out_ref.shape[1]

    def copy_of(t):
        column = pl.multiple_of((side[0] ^ mask) * 2 * width, width)
        return tile_copy(w_ref, 0, buffer.shape[0], column, buffer, sems, t, UP_TILE)

    for t in range(width // UP_TILE):
        copy_of(t).start()
    find_layout(side, shard, gathered, layout, step_ref, limits)
    rows, depth = packed_ref.shape
    per = gathered[0].shape[0]
    pieces = per // TALL
    devices = len(gathered) * pieces
    shape = (8, len(gathered) * per)
    lane = lax.broadcasted_iota(i32, shape, 1)
    row = lax.broadcasted_iota(i32, (rows, shape[1]), 0)
    for half in range(2):
        target = jnp.full(shape, -1, i32)
        for part in range(len(gathered)):
            for piece, other in enumerate(PIECES[part % 2]):
                place = part // 2 * 4 + other
                base, count = layout[place], layout[devices + place]
                inside = lane - (part * per + piece * TALL + half * LIVE_CAP)
                mine = jnp.logical_and(inside >= 0, inside < count)
                target = jnp.where(mine, base + inside, target)
        pick = (target[:1] == row).astype(f32).astype(bf16)

        @pl.loop(0, depth // 2 // DOWN_TILE)
        def _(t):
            at = pl.ds(pl.multiple_of(t * DOWN_TILE, DOWN_TILE), DOWN_TILE)
            to = pl.ds(pl.multiple_of(half * (depth // 2) + t * DOWN_TILE, DOWN_TILE), DOWN_TILE)
            found = jnp.concatenate([part[:, at] for part in gathered], axis=0)
            packed_ref[:, to] = jnp.dot(pick, found, preferred_element_type=f32).astype(bf16)

    @pl.loop(0, width // UP_TILE)
    def _(t):
        copy_of(t).wait()
        at = pl.ds(pl.multiple_of(t * UP_TILE, UP_TILE), UP_TILE)
        out_ref[:, at] = jnp.dot(
            packed_ref[...], buffer[:, at], preferred_element_type=f32
        ).astype(bf16)


def pack_up(side, shard, gathered, w_up, rows, width, mask, limits):
    depth = w_up.shape[0]
    devices = len(gathered) * gathered[0].shape[0] // TALL
    vmem, smem = pl.BlockSpec(memory_space=pltpu.VMEM), pl.BlockSpec(memory_space=pltpu.SMEM)
    return pl.pallas_call(
        functools.partial(pack_up_kernel, mask=mask, limits=limits),
        in_specs=[smem, smem] + [vmem] * len(gathered) + [pl.BlockSpec(memory_space=pl.ANY)],
        out_specs=[vmem, vmem, smem, smem],
        out_shape=[
            jax.ShapeDtypeStruct((rows, depth), bf16),
            jax.ShapeDtypeStruct((rows, width), bf16),
            jax.ShapeDtypeStruct((2 * devices,), i32),
            jax.ShapeDtypeStruct((1,), i32),
        ],
        scratch_shapes=[
            pltpu.VMEM((depth, width), bf16),
            pltpu.SemaphoreType.DMA((width // UP_TILE,)),
        ],
        compiler_params=params(24),
        cost_estimate=cost(2 * rows * depth * width, depth * width * 2),
        name="pack_up",
    )(side, shard, *gathered, w_up)


def down_kernel(side, *refs, first, mask, ahead):
    refs = list(refs)
    a_ref, w_ref = refs.pop(0), refs.pop(0)
    before_ref = None if first else refs.pop(0)
    out_ref = refs.pop(0)
    next_ref = refs.pop(0) if ahead is not None else None
    buffer, sems = refs.pop(0), refs.pop(0)
    depth, width = buffer.shape
    tiles = width // DOWN_TILE

    def copy_of(other, buffer, sems, t):
        row = pl.multiple_of((side[0] ^ other) * depth, depth)
        return tile_copy(w_ref, row, depth, 0, buffer, sems, t, DOWN_TILE)

    for t in range(tiles):
        copy_of(mask, buffer, sems, t).start()
    if ahead is not None:
        for t in range(tiles):
            copy_of(ahead, next_ref, refs[0], t).start()

    @pl.loop(0, tiles)
    def _(t):
        at = pl.ds(pl.multiple_of(t * DOWN_TILE, DOWN_TILE), DOWN_TILE)
        copy_of(mask, buffer, sems, t).wait()
        part = jnp.dot(a_ref[...], buffer[:, at], preferred_element_type=f32)
        out_ref[:, at] = part if first else before_ref[:, at] + part

    if ahead is not None:

        @pl.loop(0, tiles)
        def _(t):
            copy_of(ahead, next_ref, refs[0], t).wait()


def down(side, active, w_down, before, mask, ahead=None):
    rows, depth = active.shape
    width = w_down.shape[1]
    vmem, smem = pl.BlockSpec(memory_space=pltpu.VMEM), pl.BlockSpec(memory_space=pltpu.SMEM)
    out = jax.ShapeDtypeStruct((rows, width), f32)
    sems = pltpu.SemaphoreType.DMA((width // DOWN_TILE,))
    return pl.pallas_call(
        functools.partial(down_kernel, first=before is None, mask=mask, ahead=ahead),
        in_specs=[smem, vmem, pl.BlockSpec(memory_space=pl.ANY)]
        + ([] if before is None else [vmem]),
        out_specs=vmem if ahead is None else [vmem, vmem],
        out_shape=out if ahead is None else [out, pltpu.VMEM((depth, width), bf16)],
        scratch_shapes=[pltpu.VMEM((depth, width), bf16), sems]
        + ([] if ahead is None else [sems]),
        compiler_params=params(24),
        cost_estimate=cost(2 * rows * depth * width, depth * width * 2),
        name="down",
    )(side, active, w_down, *([] if before is None else [before]))


BACK = ((2, 3), (0, 1))


def down_unpack_kernel(layout, a_ref, w_ref, before_ref, *refs):
    outs, wide = refs[:-1], refs[-1]
    rows = a_ref.shape[0]
    tiles, devices = wide.shape[:2]
    group = devices // len(outs)
    row = lax.broadcasted_iota(i32, (PAD, rows), 0)
    column = lax.broadcasted_iota(i32, (PAD, rows), 1)
    picks = []
    for core in (0, 1):
        for x in (2, 0):
            for masks in BACK:
                for mask in masks:
                    place = (x + core) * 4 + mask
                    base, count = layout[place], layout[devices + place]
                    picks.append(jnp.logical_and(column - row == base, row < count).astype(f32))
    pick = jnp.concatenate(picks, axis=0).astype(bf16)

    @pl.loop(0, tiles)
    def _(t):
        at = pl.ds(pl.multiple_of(t * DOWN_TILE, DOWN_TILE), DOWN_TILE)
        share = before_ref[:, at] + jnp.dot(a_ref[...], w_ref[:, at], preferred_element_type=f32)
        back = jnp.dot(pick, share.astype(bf16), preferred_element_type=f32)
        wide[t] = back.reshape(devices, PAD, DOWN_TILE)

    per = tiles * LIVE_CAP
    for n, out in enumerate(outs):

        @pl.loop(0, group)
        def _(device):
            here = [wide[t, n * group + device, :LIVE_CAP, :] for t in range(tiles)]
            rows = pl.ds(pl.multiple_of(device * per, per), per)
            out[rows, :] = jnp.concatenate(here, axis=0).astype(bf16)


def down_unpack(layout, active, weights, before):
    rows, depth = active.shape
    width = weights.shape[1]
    tiles, devices = width // DOWN_TILE, layout.shape[0] // 2
    vmem, smem = pl.BlockSpec(memory_space=pltpu.VMEM), pl.BlockSpec(memory_space=pltpu.SMEM)
    out = jax.ShapeDtypeStruct((devices // 2 * tiles * LIVE_CAP, DOWN_TILE), bf16)
    return pl.pallas_call(
        down_unpack_kernel,
        in_specs=[smem, vmem, vmem, vmem],
        out_specs=[vmem] * 2,
        out_shape=[out] * 2,
        scratch_shapes=[pltpu.VMEM((tiles, devices, PAD, DOWN_TILE), f32)],
        compiler_params=params(24),
        cost_estimate=cost(2 * rows * depth * width, rows * width * 4),
        name="down_unpack",
    )(layout, active, weights, before)


def finish_kernel(lengths, side, *refs):
    out_ref = refs[-1]
    sides = (len(refs) - 3) // 2
    mixed, squares, blocks = refs[:sides], refs[sides : sides + 2], refs[sides + 2 : -1]
    slots, width = out_ref.shape
    step = width // sides
    total = squares[0][...] + squares[1][...]
    root = lax.rsqrt(jnp.sum(total, axis=-1, keepdims=True) / width + epsilon)
    gain = root * root
    tiles = step // DOWN_TILE
    picks = [
        live_pick(lengths, slots, tiles * LIVE_CAP, t * LIVE_CAP, True)[0] for t in range(tiles)
    ]
    for shift in range(sides):
        base = (side[0] ^ shift) * step
        block = blocks[shift][...]
        for t in range(tiles):
            back = jnp.dot(picks[t], block, preferred_element_type=f32)[:slots]
            at = pl.multiple_of(base + t * DOWN_TILE, DOWN_TILE)
            here = mixed[shift][:, t * DOWN_TILE : (t + 1) * DOWN_TILE]
            out_ref[:, pl.ds(at, DOWN_TILE)] = (here + gain * back).astype(bf16)


def finish(ctx_len, side, mixed, squares, blocks):
    vmem, smem = pl.BlockSpec(memory_space=pltpu.VMEM), pl.BlockSpec(memory_space=pltpu.SMEM)
    slots, width = mixed[0].shape[0], mixed[0].shape[1] * len(mixed)
    return pl.pallas_call(
        finish_kernel,
        in_specs=[smem, smem] + [vmem] * (2 * len(mixed) + 2),
        out_specs=vmem,
        out_shape=jax.ShapeDtypeStruct((slots, width), bf16),
        compiler_params=params(16),
        cost_estimate=cost(slots * width * 32, slots * width * 8),
        name="finish",
    )(ctx_len, side, *mixed, *squares, *blocks)


def swap(x, axis, count, mask):
    return lax.ppermute(x, axis, [(j, j ^ mask) for j in range(count)])


def added(a, b):
    return (a.astype(f32) + b.astype(f32)).astype(bf16)


def tie(x, *others):
    return lax.optimization_barrier((x, *others))[0]


def squared_relu(*terms):
    lifted = sum(term.astype(f32) for term in terms)
    clipped = jnp.maximum(lifted, 0.0)
    return (clipped * clipped).astype(bf16)


def feed_forward(rows, side, layout, packed, other, w_up, w_down):
    half = w_up.shape[1] // 8
    across = lambda x: swap(x, "side", 4, 2)
    beside = lambda x: swap(x, "side", 4, 1)
    met_0 = beside(other[:rows])
    far = up(side, packed, w_up, rows, half, ((3, 1), (2, 0), (2, 1)))
    met_1 = beside(far[0])
    sum_0 = added(far[1], met_0)
    crossed_0 = across(sum_0)
    near = up(side, tie(packed, sum_0), w_up, rows, half, ((1, 0), (1, 1)))
    met_1, near = lax.optimization_barrier((met_1, near))
    sum_1 = added(far[2], met_1)
    crossed_1 = across(sum_1)
    near = beside(near)
    own = up(side, tie(packed, sum_1), w_up, rows, half, ((0, 0), (0, 1)))
    active = [squared_relu(own[n], near[n], crossed) for n, crossed in enumerate((crossed_0, crossed_1))]
    active = jnp.concatenate(active, axis=1)
    over, following = across(active), beside(active)
    total = down(side, active, w_down, None, 0)
    forward = beside(tie(over, total))
    total = down(side, following, w_down, total, 1)
    total, weights = down(side, over, w_down, total, 2, ahead=3)
    return down_unpack(layout, forward, weights, total)


ROW_STEPS = (112, 120, 128, 136, 144, 160, 192)


def line_shards(
    queries, new_kv, kv_pool, page_table, ctx_len, residual_in, norm_gain, w_up, w_down
):
    i, s = lax.axis_index("side"), lax.axis_index("shard")
    side, shard = i.reshape(1), s.reshape(1)
    in_hbm = lambda x: pltpu.with_memory_space_constraint(x, pltpu.HBM)
    gain = norm_gain.reshape(-1, HEAD)
    inputs = queries, new_kv, kv_pool, page_table, ctx_len, residual_in, gain
    inputs, w_up, w_down = jax.tree.map(in_hbm, (inputs, w_up, w_down))
    ctx_len = inputs[4]
    (to_2, to_3), mixed_far, squares_far, copies = attend(inputs, side, 4, (2, 3), None)
    met = swap(jnp.concatenate([to_2, to_3], axis=0), "side", 4, 2)
    (own, to_1), mixed_near, squares_near, _ = attend(inputs, side, 4, (0, 1), copies)
    first = jnp.concatenate([own, met[:TALL]], axis=0)
    second = swap(jnp.concatenate([to_1, met[TALL:]], axis=0), "side", 4, 1)
    gathered = []
    by_x = [swap(here, "shard", 4, 2) for here in (first, second)]
    by_core = [swap(here, "shard", 4, 1) for here in (first, second)]
    by_both = [swap(there, "shard", 4, 1) for there in by_x]
    gathered = [first, second, *by_core, *by_x, *by_both]
    packed, other, layout, step = pack_up(
        side, shard, gathered, w_up, ROW_STEPS[-1], w_up.shape[1] // 8, 3, ROW_STEPS[:-1]
    )
    stay, leave = lax.switch(
        step[0],
        [functools.partial(feed_forward, rows) for rows in ROW_STEPS],
        side, layout, packed, other, w_up, w_down,
    )
    back = swap(leave, "shard", 4, 1)
    quarter = back.shape[0] // 4
    piece = quarter // 2
    cuts = [slice(at, at + quarter) for at in range(0, 4 * quarter, quarter)]
    sums = [added(stay[cut], back[cut]) for cut in cuts]
    far = added(sums[2], swap(sums[0], "shard", 4, 2))
    near = added(sums[3], swap(sums[1], "shard", 4, 2))
    home = near[:piece], near[piece:], far[:piece], far[piece:]
    blocks = [home[0]] + [swap(home[mask], "side", 4, mask) for mask in (1, 2, 3)]
    mixed = [*mixed_near, *mixed_far]
    return finish(ctx_len, side, mixed, [squares_far, squares_near], blocks)


def attend_slots(queries, new_kv, pool_pages, page_rows, lengths):
    slot_count = queries.shape[0]
    positions = page_rows.shape[1] * pool_pages.shape[1]
    fetched = pool_pages[page_rows].reshape(slot_count, positions, 2, KV_HEADS, HEAD)
    fresh_kv = new_kv.reshape(slot_count, 2, KV_HEADS, HEAD)
    query_heads = queries.reshape(slot_count, KV_HEADS, GROUP, HEAD)
    score_scale = 1.0 / math.sqrt(HEAD)
    scores = (
        jnp.einsum("sgqd,slgd->sgql", query_heads, fetched[:, :, 0], preferred_element_type=f32)
        * score_scale
    )
    own_score = (
        jnp.einsum("sgqd,sgd->sgq", query_heads, fresh_kv[:, 0], preferred_element_type=f32)
        * score_scale
    )
    visible = (jnp.arange(positions, dtype=i32)[None, :] < lengths[:, None])[:, None, None, :]
    scores = jnp.where(visible, scores, -1e30)
    highest = jnp.maximum(jnp.max(scores, axis=-1), own_score)
    weights = jnp.where(visible, jnp.exp(scores - highest[..., None]), 0.0)
    own_weight = jnp.exp(own_score - highest)
    denominator = jnp.sum(weights, axis=-1) + own_weight
    probabilities = (weights / denominator[..., None]).astype(bf16)
    own_prob = (own_weight / denominator).astype(bf16).astype(f32)
    attended = jnp.einsum(
        "sgql,slgd->sgqd", probabilities, fetched[:, :, 1], preferred_element_type=f32
    )
    attended = attended + own_prob[..., None] * fresh_kv[:, 1].astype(f32)[:, :, None, :]
    return attended.reshape(slot_count, -1)


def any_shards(queries, new_kv, kv_pool, page_table, ctx_len, residual_in, norm_gain, w_up, w_down):
    attended = attend_slots(queries, new_kv, kv_pool, page_table, ctx_len)
    mixed_rows = residual_in.astype(f32) + attended
    mean_square = jnp.mean(mixed_rows * mixed_rows, axis=-1, keepdims=True)
    normed = (mixed_rows * lax.rsqrt(mean_square + epsilon) * norm_gain.astype(f32)).astype(bf16)
    live_mask = ctx_len > 0
    spread = lax.all_to_all(normed, "side", split_axis=1, concat_axis=0, tiled=True)
    up_partial = jnp.dot(
        lax.all_gather(spread, "shard", axis=0, tiled=True), w_up, preferred_element_type=f32
    )
    lifted = lax.psum(up_partial, "side")
    clipped = jnp.maximum(lifted, 0.0)
    active = (clipped * clipped).astype(bf16)
    down_share = lax.psum_scatter(
        jnp.dot(active, w_down, preferred_element_type=f32).astype(bf16),
        "shard",
        scatter_dimension=0,
        tiled=True,
    )
    returned = lax.all_to_all(down_share, "side", split_axis=0, concat_axis=1, tiled=True)
    returned = jnp.where(live_mask[:, None], returned.astype(f32), 0.0)
    return (mixed_rows + returned).astype(bf16)


def solution(mesh):
    rows = ("grp", "side", "shard")
    placed = (
        P(rows, None),
        P(rows, None),
        P(rows, None, None),
        P(rows, None),
        P(rows),
        P(rows, None),
        P(),
        P("side", "shard"),
        P("shard", "side"),
    )
    square = mesh.shape["side"] == 4 and mesh.shape["shard"] == 4
    return jax.shard_map(
        line_shards if square else any_shards,
        mesh=mesh,
        in_specs=placed,
        out_specs=P(rows, None),
        check_vma=False,
    )
```

```python
import functools
import math

import jax
import jax.numpy as jnp
from jax import lax
from jax.experimental import pallas as pl
from jax.experimental.pallas import tpu as pltpu
from jax.sharding import PartitionSpec as P

KV_HEADS = 8
HEAD = 128
GROUP = 8
LIVE_CAP = 12
PAD = 16
TALL = 2 * LIVE_CAP
EMPTY = 1e30

epsilon = 1e-05
bf16, f32, i32 = jnp.bfloat16, jnp.float32, jnp.int32
VMEM_MB = 1 << 20


def params(mb, **more):
    return pltpu.CompilerParams(vmem_limit_bytes=mb * VMEM_MB, **more)


def cost(flops, bytes_accessed):
    return pl.CostEstimate(
        flops=int(flops) // 64, bytes_accessed=int(bytes_accessed) // 64, transcendentals=0
    )


def pad_rows(x):
    rows = x.shape[0]
    if rows == PAD:
        return x
    return jnp.concatenate([x, jnp.zeros((PAD - rows,) + x.shape[1:], x.dtype)], axis=0)


def live_ranks(lengths, slots):
    live, rank, count = [], [], jnp.int32(0)
    for slot in range(slots):
        alive = lengths[slot] > 0
        live.append(alive)
        rank.append(count)
        count = count + alive.astype(i32)
    return live, rank


def token_bias(lengths, table, pages, page):
    slots, entries = table.shape
    tokens = pages * page
    lanes = 128 * ((pages + 127) // 128)
    row = lax.broadcasted_iota(i32, (PAD, lanes), 0)
    column = lax.broadcasted_iota(i32, (PAD, lanes), 1)
    reach = jnp.zeros((PAD, lanes), i32)
    for slot in range(slots):
        reach = jnp.where(row == slot, lengths[slot], reach)
    table = pad_rows(table)
    seen = jnp.zeros((PAD, lanes), i32)
    for entry in range(entries):
        here = jnp.minimum(jnp.maximum(reach - entry * page, 0), page)
        seen = seen + jnp.where(table[:, entry : entry + 1] == column, here, 0)
    spread = (
        lax.broadcasted_iota(i32, (lanes, tokens), 1) // page
        == lax.broadcasted_iota(i32, (lanes, tokens), 0)
    )
    seen_tokens = jnp.dot(
        seen.astype(f32).astype(bf16), spread.astype(f32).astype(bf16), preferred_element_type=f32
    )
    place = (lax.broadcasted_iota(i32, (PAD, tokens), 1) % page).astype(f32)
    return jnp.where(place < seen_tokens, 0.0, -1e30)


def live_pick(lengths, slots, rows, offset, to_slots):
    live, rank = live_ranks(lengths, slots)
    shape = (PAD, rows) if to_slots else (rows, PAD)
    of_slot = lax.broadcasted_iota(i32, shape, 0 if to_slots else 1)
    of_rank = lax.broadcasted_iota(i32, shape, 1 if to_slots else 0) - offset
    pick = jnp.zeros(shape, f32)
    for slot in range(slots):
        chosen = jnp.logical_and(of_rank == rank[slot], of_slot == slot)
        pick = jnp.where(jnp.logical_and(chosen, live[slot]), 1.0, pick)
    return pick.astype(bf16), rank[-1] + live[-1].astype(i32)


POOL_CUTS = 4


def attend_kernel(*refs, masks, sides, first):
    side = lax.axis_index("side")
    refs = list(refs)
    take = lambda n: [refs.pop(0) for _ in range(n)]
    if first:
        lengths, table_ref = take(2)
        sources = take(4)
    else:
        q_ref, new_ref, res_ref, gain_ref, bias_ref, picks_ref, empty_ref = take(7)
    pool_source = refs.pop(0)
    sends, mixed_refs = take(len(masks)), take(len(masks))
    square_ref = refs.pop(0)
    if first:
        q_ref, new_ref, res_ref, gain_ref, bias_ref, picks_ref, empty_ref, back_ref = take(8)
        gain_copy, sems = take(2)
    pool_ref, pool_sems = refs
    slots, step = mixed_refs[0].shape
    pages, page, width = pool_source.shape
    columns = width // 2 // sides
    heads = columns // HEAD
    tokens = pages * page
    scale = math.log2(math.e) / math.sqrt(HEAD)

    if first:
        small = [
            pltpu.make_async_copy(source, target, sems.at[n])
            for n, (source, target) in enumerate(
                zip(sources, (q_ref, new_ref, res_ref, gain_copy), strict=True)
            )
        ]
        for copy in small:
            copy.start()
    cut, half, pair = pages // POOL_CUTS, width // 2, columns * 2
    here = lax.div(side ^ masks[0], 2) * pair
    brought = []
    for n, at in enumerate((here, half + here)):
        columns_at = pl.ds(pl.multiple_of(at, pair), pair)
        target_at = pl.ds(n * pair, pair)
        brought.append([])
        for c in range(POOL_CUTS):
            rows = pl.ds(c * cut, cut)
            copy = pltpu.make_async_copy(
                pool_source.at[rows, :, columns_at], pool_ref.at[rows, :, target_at], pool_sems.at[n, c]
            )
            copy.start()
            brought[n].append(copy)
    if first:
        bias_ref[...] = token_bias(lengths, table_ref[...], pages, page)
        for head in range(heads):
            picks_ref[head], count = live_pick(lengths, slots, TALL, head * LIVE_CAP, False)
        rank = lax.broadcasted_iota(i32, empty_ref.shape, 0)
        rank = jnp.where(rank < LIVE_CAP, rank, rank - LIVE_CAP)
        empty_ref[...] = (rank >= count).astype(f32)
        for t in range(back_ref.shape[0]):
            back_ref[t] = live_pick(lengths, slots, back_ref.shape[2], t * LIVE_CAP, True)[0]
        for copy in small:
            copy.wait()
        gain_ref[...] = gain_copy[...].astype(f32)
    for copy in brought[0]:
        copy.wait()
    values_to_come = brought[1]

    squares = jnp.zeros((slots, HEAD), f32)
    bias = bias_ref[...][None]
    jobs = [(n, head) for n in range(len(masks)) for head in range(heads)]

    def places(job):
        block, base = side ^ masks[job[0]], job[1] * GROUP * HEAD
        new_at = pl.multiple_of(block * columns, columns) + job[1] * HEAD
        key_at = pl.multiple_of(lax.rem(block, 2) * columns, columns) + job[1] * HEAD
        return block, base, pl.multiple_of(block * step, step) + base, new_at, key_at

    def score(job):
        _, _, start, new_at, key_at = places(job)
        q = jnp.concatenate(
            [pad_rows(q_ref[:, pl.ds(start + g * HEAD, HEAD)]) for g in range(GROUP)], axis=0
        )
        keys = pool_ref[:, :, pl.ds(key_at, HEAD)].reshape(tokens, HEAD)
        new_key = pad_rows(new_ref[:, pl.ds(new_at, HEAD)]).astype(f32)
        scores = lax.dot_general(q, keys, (((1,), (1,)), ((), ())), preferred_element_type=f32)
        own = jnp.sum(
            q.astype(f32).reshape(GROUP, PAD, HEAD) * new_key[None], axis=-1, keepdims=True
        )
        return scores.reshape(GROUP, PAD, tokens), own * scale

    ready = score(jobs[0])
    for number, job in enumerate(jobs):
        block, base, start, new_at, key_at = places(job)
        scores, own = ready
        if number + 1 < len(jobs):
            ready = score(jobs[number + 1])
        scores = scores * scale + bias
        highest = jnp.maximum(jnp.max(scores, axis=-1, keepdims=True), own)
        weights = jnp.exp2(scores - highest)
        own_weight = jnp.exp2(own - highest)
        total = jnp.sum(weights, axis=-1, keepdims=True) + own_weight
        for copy in values_to_come:
            copy.wait()
        values_to_come = []
        values = pool_ref[:, :, pl.ds(pair + key_at, HEAD)].reshape(tokens, HEAD)
        new_value = pad_rows(new_ref[:, pl.ds(half + new_at, HEAD)]).astype(f32)
        summed = jnp.dot(
            weights.astype(bf16).reshape(GROUP * PAD, tokens), values, preferred_element_type=f32
        ).reshape(GROUP, PAD, HEAD)
        attended = (summed + own_weight * new_value[None]) / total
        for g in range(GROUP):
            at = slice(base + g * HEAD, base + (g + 1) * HEAD)
            residual = res_ref[:, pl.ds(start + g * HEAD, HEAD)].astype(f32)
            mixed = residual + attended[g][:slots]
            mixed_refs[job[0]][:, at] = mixed
            squares = squares + mixed * mixed
            gain = gain_ref[pl.ds(block * (step // HEAD) + job[1] * GROUP + g, 1), :]
            gained = pad_rows((mixed * gain).astype(bf16))
            rows = jnp.dot(picks_ref[job[1]], gained, preferred_element_type=f32)
            to = slice(g * HEAD, (g + 1) * HEAD)
            if job[1]:
                rows = rows + sends[job[0]][:, to].astype(f32)
                rows = jnp.where(empty_ref[...] > 0, EMPTY, rows)
            sends[job[0]][:, to] = rows.astype(bf16)
    square_ref[...] = squares


def attend(inputs, sides, masks, before):
    queries, new_kv, kv_pool, page_table, ctx_len, residual_in, norm_gain = inputs
    slots, columns = queries.shape
    pages, page, _ = kv_pool.shape
    step = columns // sides
    first = before is None
    vmem, anywhere = pl.BlockSpec(memory_space=pltpu.VMEM), pl.BlockSpec(memory_space=pl.ANY)
    smem = pl.BlockSpec(memory_space=pltpu.SMEM)
    out_shape = [jax.ShapeDtypeStruct((TALL, step // 2), bf16)] * len(masks)
    out_shape += [jax.ShapeDtypeStruct((slots, step), f32)] * len(masks)
    out_shape += [jax.ShapeDtypeStruct((slots, HEAD), f32)]
    if first:
        operands = [ctx_len, page_table, queries, new_kv, residual_in, norm_gain, kv_pool]
        in_specs = [smem, vmem] + [anywhere] * 5
        tiles = step // DOWN_TILE
        out_shape += [
            pltpu.VMEM(queries.shape, bf16),
            pltpu.VMEM(new_kv.shape, bf16),
            pltpu.VMEM(residual_in.shape, bf16),
            pltpu.VMEM(norm_gain.shape, f32),
            pltpu.VMEM((PAD, pages * page), f32),
            pltpu.VMEM((columns // HEAD // GROUP // sides, TALL, PAD), bf16),
            pltpu.VMEM((TALL, HEAD), f32),
            pltpu.VMEM((tiles, PAD, tiles * LIVE_CAP), bf16),
        ]
        scratch = [pltpu.VMEM(norm_gain.shape, bf16), pltpu.SemaphoreType.DMA((4,))]
    else:
        operands = [*before, kv_pool]
        in_specs = [vmem] * len(before) + [anywhere]
        scratch = []
    scratch += [
        pltpu.VMEM((pages, page, kv_pool.shape[2] // sides * 2), bf16),
        pltpu.SemaphoreType.DMA((2, POOL_CUTS)),
    ]
    outs = pl.pallas_call(
        functools.partial(attend_kernel, masks=masks, sides=sides, first=first),
        in_specs=in_specs,
        out_specs=[vmem] * len(out_shape),
        out_shape=out_shape,
        scratch_shapes=scratch,
        compiler_params=params(28),
        cost_estimate=cost(2e9, kv_pool.size),
        name="attend",
    )(*operands)
    n = len(masks)
    return outs[:n], outs[n : 2 * n], outs[2 * n], outs[2 * n + 1 :]


UP_TILE = 256
DOWN_TILE = 512


def tile_copy(w_ref, row, rows, column, buffer, sems, t, tile):
    at = pl.ds(pl.multiple_of(t * tile, tile), tile)
    source = w_ref.at[pl.ds(row, rows), pl.ds(pl.multiple_of(column + t * tile, tile), tile)]
    return pltpu.make_async_copy(source, buffer.at[:, at], sems.at[t])


def up_kernel(x_ref, w_ref, out_ref, buffer, sems, *, masks):
    side = lax.axis_index("side")
    depth, width = buffer.shape[1:]
    tiles = width // UP_TILE

    def copy_of(n, t):
        column = pl.multiple_of(((side ^ masks[n][0]) * 2 + masks[n][1]) * width, width)
        return tile_copy(w_ref, 0, depth, column, buffer.at[n], sems.at[n], t, UP_TILE)

    for n in range(len(masks)):
        for t in range(tiles):
            copy_of(n, t).start()

    @pl.loop(0, len(masks) * tiles)
    def _(job):
        n, t = lax.div(job, tiles), lax.rem(job, tiles)
        at = pl.ds(pl.multiple_of(t * UP_TILE, UP_TILE), UP_TILE)
        pltpu.make_async_copy(
            w_ref.at[:, pl.ds(0, UP_TILE)], buffer.at[n, :, at], sems.at[n, t]
        ).wait()
        out_ref[n, :, at] = jnp.dot(
            x_ref[: out_ref.shape[1], :], buffer[n, :, at], preferred_element_type=f32
        ).astype(out_ref.dtype)


def up(packed, w_up, rows, width, masks):
    depth = packed.shape[1]
    vmem = pl.BlockSpec(memory_space=pltpu.VMEM)
    return pl.pallas_call(
        functools.partial(up_kernel, masks=masks),
        in_specs=[vmem, pl.BlockSpec(memory_space=pl.ANY)],
        out_specs=vmem,
        out_shape=jax.ShapeDtypeStruct((len(masks), rows, width), bf16),
        scratch_shapes=[
            pltpu.VMEM((len(masks), depth, width), bf16),
            pltpu.SemaphoreType.DMA((len(masks), width // UP_TILE)),
        ],
        compiler_params=params(24),
        cost_estimate=cost(2 * rows * depth * width, depth * width * 2 * len(masks)),
        name="up",
    )(packed, w_up)


PIECES = ((0, 2), (1, 3))


def find_layout(gathered, layout, step_ref, limits):
    side, shard = lax.axis_index("side"), lax.axis_index("shard")
    pieces = gathered[0].shape[0] // TALL
    devices = len(gathered) * pieces
    counts, places = [None] * devices, [None] * devices
    number = lax.broadcasted_iota(i32, (LIVE_CAP, HEAD), 0) + 1
    for part in range(len(gathered)):
        marks = gathered[part][:, :HEAD].astype(f32)
        for piece, mask in enumerate(PIECES[part % 2]):
            rows = marks[piece * TALL : piece * TALL + LIVE_CAP]
            last = jnp.where(rows < EMPTY / 2, number, 0).astype(f32)
            place = part // 2 * 4 + mask
            counts[place] = jnp.max(last).astype(i32)
            places[place] = (side ^ mask) * 4 + (shard ^ (part // 2))
    total = jnp.int32(0)
    for one in range(devices):
        base = jnp.int32(0)
        for other in range(devices):
            base = base + jnp.where(places[other] < places[one], counts[other], 0)
        layout[one] = base
        layout[devices + one] = counts[one]
        total = total + counts[one]
    step = jnp.int32(0)
    for limit in limits:
        step = step + (total > limit).astype(i32)
    step_ref[0] = step


def pack_up_kernel(*refs, mask, limits):
    gathered, refs = refs[:-7], refs[-7:]
    w_ref, packed_ref, out_ref, layout, step_ref, buffer, sems = refs
    width = out_ref.shape[1]

    def copy_of(t):
        column = pl.multiple_of((lax.axis_index("side") ^ mask) * 2 * width, width)
        return tile_copy(w_ref, 0, buffer.shape[0], column, buffer, sems, t, UP_TILE)

    for t in range(width // UP_TILE):
        copy_of(t).start()
    find_layout(gathered, layout, step_ref, limits)
    rows, depth = packed_ref.shape
    per = gathered[0].shape[0]
    pieces = per // TALL
    devices = len(gathered) * pieces
    shape = (8, len(gathered) * per)
    lane = lax.broadcasted_iota(i32, shape, 1)
    row = lax.broadcasted_iota(i32, (rows, shape[1]), 0)
    for half in range(2):
        target = jnp.full(shape, -1, i32)
        for part in range(len(gathered)):
            for piece, other in enumerate(PIECES[part % 2]):
                place = part // 2 * 4 + other
                base, count = layout[place], layout[devices + place]
                inside = lane - (part * per + piece * TALL + half * LIVE_CAP)
                mine = jnp.logical_and(inside >= 0, inside < count)
                target = jnp.where(mine, base + inside, target)
        pick = (target[:1] == row).astype(f32).astype(bf16)

        @pl.loop(0, depth // 2 // DOWN_TILE)
        def _(t):
            at = pl.ds(pl.multiple_of(t * DOWN_TILE, DOWN_TILE), DOWN_TILE)
            to = pl.ds(pl.multiple_of(half * (depth // 2) + t * DOWN_TILE, DOWN_TILE), DOWN_TILE)
            found = jnp.concatenate([part[:, at] for part in gathered], axis=0)
            packed_ref[:, to] = jnp.dot(pick, found, preferred_element_type=f32).astype(bf16)

    @pl.loop(0, width // UP_TILE)
    def _(t):
        copy_of(t).wait()
        at = pl.ds(pl.multiple_of(t * UP_TILE, UP_TILE), UP_TILE)
        out_ref[:, at] = jnp.dot(
            packed_ref[...], buffer[:, at], preferred_element_type=f32
        ).astype(bf16)


def pack_up(gathered, w_up, rows, width, mask, limits):
    depth = w_up.shape[0]
    devices = len(gathered) * gathered[0].shape[0] // TALL
    vmem, smem = pl.BlockSpec(memory_space=pltpu.VMEM), pl.BlockSpec(memory_space=pltpu.SMEM)
    return pl.pallas_call(
        functools.partial(pack_up_kernel, mask=mask, limits=limits),
        in_specs=[vmem] * len(gathered) + [pl.BlockSpec(memory_space=pl.ANY)],
        out_specs=[vmem, vmem, smem, smem],
        out_shape=[
            jax.ShapeDtypeStruct((rows, depth), bf16),
            jax.ShapeDtypeStruct((rows, width), bf16),
            jax.ShapeDtypeStruct((2 * devices,), i32),
            jax.ShapeDtypeStruct((1,), i32),
        ],
        scratch_shapes=[
            pltpu.VMEM((depth, width), bf16),
            pltpu.SemaphoreType.DMA((width // UP_TILE,)),
        ],
        compiler_params=params(24),
        cost_estimate=cost(2 * rows * depth * width, depth * width * 2),
        name="pack_up",
    )(*gathered, w_up)


def down_kernel(*refs, first, mask, ahead):
    refs = list(refs)
    a_ref, w_ref = refs.pop(0), refs.pop(0)
    before_ref = None if first else refs.pop(0)
    out_ref = refs.pop(0)
    next_ref = refs.pop(0) if ahead is not None else None
    buffer, sems = refs.pop(0), refs.pop(0)
    depth, width = buffer.shape
    tiles = width // DOWN_TILE

    def copy_of(other, buffer, sems, t):
        row = pl.multiple_of((lax.axis_index("side") ^ other) * depth, depth)
        return tile_copy(w_ref, row, depth, 0, buffer, sems, t, DOWN_TILE)

    for t in range(tiles):
        copy_of(mask, buffer, sems, t).start()
    if ahead is not None:
        for t in range(tiles):
            copy_of(ahead, next_ref, refs[0], t).start()

    @pl.loop(0, tiles)
    def _(t):
        at = pl.ds(pl.multiple_of(t * DOWN_TILE, DOWN_TILE), DOWN_TILE)
        copy_of(mask, buffer, sems, t).wait()
        part = jnp.dot(a_ref[...], buffer[:, at], preferred_element_type=f32)
        out_ref[:, at] = part if first else before_ref[:, at] + part

    if ahead is not None:

        @pl.loop(0, tiles)
        def _(t):
            copy_of(ahead, next_ref, refs[0], t).wait()


def down(active, w_down, before, mask, ahead=None):
    rows, depth = active.shape
    width = w_down.shape[1]
    vmem = pl.BlockSpec(memory_space=pltpu.VMEM)
    out = jax.ShapeDtypeStruct((rows, width), f32)
    sems = pltpu.SemaphoreType.DMA((width // DOWN_TILE,))
    return pl.pallas_call(
        functools.partial(down_kernel, first=before is None, mask=mask, ahead=ahead),
        in_specs=[vmem, pl.BlockSpec(memory_space=pl.ANY)]
        + ([] if before is None else [vmem]),
        out_specs=vmem if ahead is None else [vmem, vmem],
        out_shape=out if ahead is None else [out, pltpu.VMEM((depth, width), bf16)],
        scratch_shapes=[pltpu.VMEM((depth, width), bf16), sems]
        + ([] if ahead is None else [sems]),
        compiler_params=params(24),
        cost_estimate=cost(2 * rows * depth * width, depth * width * 2),
        name="down",
    )(active, w_down, *([] if before is None else [before]))


BACK = ((2, 3), (0, 1))


def down_unpack_kernel(layout, a_ref, w_ref, before_ref, *refs):
    outs, wide = refs[:-1], refs[-1]
    rows = a_ref.shape[0]
    tiles, devices = wide.shape[:2]
    group = devices // len(outs)
    row = lax.broadcasted_iota(i32, (PAD, rows), 0)
    column = lax.broadcasted_iota(i32, (PAD, rows), 1)
    picks = []
    for core in (0, 1):
        for x in (2, 0):
            for masks in BACK:
                for mask in masks:
                    place = (x + core) * 4 + mask
                    base, count = layout[place], layout[devices + place]
                    picks.append(jnp.logical_and(column - row == base, row < count).astype(f32))
    pick = jnp.concatenate(picks, axis=0).astype(bf16)

    @pl.loop(0, tiles)
    def _(t):
        at = pl.ds(pl.multiple_of(t * DOWN_TILE, DOWN_TILE), DOWN_TILE)
        share = before_ref[:, at] + jnp.dot(a_ref[...], w_ref[:, at], preferred_element_type=f32)
        back = jnp.dot(pick, share.astype(bf16), preferred_element_type=f32)
        wide[t] = back.reshape(devices, PAD, DOWN_TILE)

    per = tiles * LIVE_CAP
    for n, out in enumerate(outs):

        @pl.loop(0, group)
        def _(device):
            here = [wide[t, n * group + device, :LIVE_CAP, :] for t in range(tiles)]
            rows = pl.ds(pl.multiple_of(device * per, per), per)
            out[rows, :] = jnp.concatenate(here, axis=0).astype(bf16)


def down_unpack(layout, active, weights, before):
    rows, depth = active.shape
    width = weights.shape[1]
    tiles, devices = width // DOWN_TILE, layout.shape[0] // 2
    vmem, smem = pl.BlockSpec(memory_space=pltpu.VMEM), pl.BlockSpec(memory_space=pltpu.SMEM)
    out = jax.ShapeDtypeStruct((devices // 2 * tiles * LIVE_CAP, DOWN_TILE), bf16)
    return pl.pallas_call(
        down_unpack_kernel,
        in_specs=[smem, vmem, vmem, vmem],
        out_specs=[vmem] * 2,
        out_shape=[out] * 2,
        scratch_shapes=[pltpu.VMEM((tiles, devices, PAD, DOWN_TILE), f32)],
        compiler_params=params(24),
        cost_estimate=cost(2 * rows * depth * width, rows * width * 4),
        name="down_unpack",
    )(layout, active, weights, before)


def finish_kernel(picks_ref, *refs):
    side = lax.axis_index("side")
    out_ref = refs[-1]
    sides = (len(refs) - 3) // 2
    mixed, squares, blocks = refs[:sides], refs[sides : sides + 2], refs[sides + 2 : -1]
    slots, width = out_ref.shape
    step = width // sides
    total = squares[0][...] + squares[1][...]
    root = lax.rsqrt(jnp.sum(total, axis=-1, keepdims=True) / width + epsilon)
    gain = root * root
    tiles = step // DOWN_TILE
    for shift in range(sides):
        base = (side ^ shift) * step
        block = blocks[shift][...]
        for t in range(tiles):
            back = jnp.dot(picks_ref[t], block, preferred_element_type=f32)[:slots]
            at = pl.multiple_of(base + t * DOWN_TILE, DOWN_TILE)
            here = mixed[shift][:, t * DOWN_TILE : (t + 1) * DOWN_TILE]
            out_ref[:, pl.ds(at, DOWN_TILE)] = (here + gain * back).astype(bf16)


def finish(picks, mixed, squares, blocks):
    vmem = pl.BlockSpec(memory_space=pltpu.VMEM)
    slots, width = mixed[0].shape[0], mixed[0].shape[1] * len(mixed)
    return pl.pallas_call(
        finish_kernel,
        in_specs=[vmem] * (2 * len(mixed) + 3),
        out_specs=vmem,
        out_shape=jax.ShapeDtypeStruct((slots, width), bf16),
        compiler_params=params(16),
        cost_estimate=cost(slots * width * 32, slots * width * 8),
        name="finish",
    )(picks, *mixed, *squares, *blocks)


def swap(x, axis, count, mask):
    return lax.ppermute(x, axis, [(j, j ^ mask) for j in range(count)])


def added(a, b):
    return (a.astype(f32) + b.astype(f32)).astype(bf16)


def tie(x, *others):
    return lax.optimization_barrier((x, *others))[0]


def squared_relu(*terms):
    lifted = sum(term.astype(f32) for term in terms)
    clipped = jnp.maximum(lifted, 0.0)
    return (clipped * clipped).astype(bf16)


def feed_forward(rows, layout, packed, other, w_up, w_down):
    half = w_up.shape[1] // 8
    across = lambda x: swap(x, "side", 4, 2)
    beside = lambda x: swap(x, "side", 4, 1)
    met_0 = beside(other[:rows])
    far = up(packed, w_up, rows, half, ((3, 1), (2, 0), (2, 1)))
    met_1 = beside(far[0])
    sum_0 = added(far[1], met_0)
    crossed_0 = across(sum_0)
    near = up(tie(packed, sum_0), w_up, rows, half, ((1, 0), (1, 1)))
    met_1, near = lax.optimization_barrier((met_1, near))
    sum_1 = added(far[2], met_1)
    crossed_1 = across(sum_1)
    near = beside(near)
    own = up(tie(packed, sum_1), w_up, rows, half, ((0, 0), (0, 1)))
    active = [squared_relu(own[n], near[n], crossed) for n, crossed in enumerate((crossed_0, crossed_1))]
    active = jnp.concatenate(active, axis=1)
    over, following = across(active), beside(active)
    total = down(active, w_down, None, 0)
    forward = beside(tie(over, total))
    total = down(following, w_down, total, 1)
    total, weights = down(over, w_down, total, 2, ahead=3)
    return down_unpack(layout, forward, weights, total)


ROW_STEPS = (112, 120, 128, 136, 144, 160, 192)


def line_shards(
    queries, new_kv, kv_pool, page_table, ctx_len, residual_in, norm_gain, w_up, w_down
):
    in_hbm = lambda x: pltpu.with_memory_space_constraint(x, pltpu.HBM)
    gain = norm_gain.reshape(-1, HEAD)
    inputs = queries, new_kv, kv_pool, page_table, ctx_len, residual_in, gain
    inputs, w_up, w_down = jax.tree.map(in_hbm, (inputs, w_up, w_down))
    (to_2, to_3), mixed_far, squares_far, copies = attend(inputs, 4, (2, 3), None)
    *copies, back_picks = copies
    met = swap(jnp.concatenate([to_2, to_3], axis=0), "side", 4, 2)
    (own, to_1), mixed_near, squares_near, _ = attend(inputs, 4, (0, 1), copies)
    first = jnp.concatenate([own, met[:TALL]], axis=0)
    second = swap(jnp.concatenate([to_1, met[TALL:]], axis=0), "side", 4, 1)
    gathered = []
    by_x = [swap(here, "shard", 4, 2) for here in (first, second)]
    by_core = [swap(here, "shard", 4, 1) for here in (first, second)]
    by_both = [swap(there, "shard", 4, 1) for there in by_x]
    gathered = [first, second, *by_core, *by_x, *by_both]
    packed, other, layout, step = pack_up(
        gathered, w_up, ROW_STEPS[-1], w_up.shape[1] // 8, 3, ROW_STEPS[:-1]
    )
    stay, leave = lax.switch(
        step[0],
        [functools.partial(feed_forward, rows) for rows in ROW_STEPS],
        layout, packed, other, w_up, w_down,
    )
    back = swap(leave, "shard", 4, 1)
    quarter = back.shape[0] // 4
    piece = quarter // 2
    cuts = [slice(at, at + quarter) for at in range(0, 4 * quarter, quarter)]
    sums = [added(stay[cut], back[cut]) for cut in cuts]
    far = added(sums[2], swap(sums[0], "shard", 4, 2))
    near = added(sums[3], swap(sums[1], "shard", 4, 2))
    home = near[:piece], near[piece:], far[:piece], far[piece:]
    blocks = [home[0]] + [swap(home[mask], "side", 4, mask) for mask in (1, 2, 3)]
    mixed = [*mixed_near, *mixed_far]
    return finish(back_picks, mixed, [squares_far, squares_near], blocks)


def attend_slots(queries, new_kv, pool_pages, page_rows, lengths):
    slot_count = queries.shape[0]
    positions = page_rows.shape[1] * pool_pages.shape[1]
    fetched = pool_pages[page_rows].reshape(slot_count, positions, 2, KV_HEADS, HEAD)
    fresh_kv = new_kv.reshape(slot_count, 2, KV_HEADS, HEAD)
    query_heads = queries.reshape(slot_count, KV_HEADS, GROUP, HEAD)
    score_scale = 1.0 / math.sqrt(HEAD)
    scores = (
        jnp.einsum("sgqd,slgd->sgql", query_heads, fetched[:, :, 0], preferred_element_type=f32)
        * score_scale
    )
    own_score = (
        jnp.einsum("sgqd,sgd->sgq", query_heads, fresh_kv[:, 0], preferred_element_type=f32)
        * score_scale
    )
    visible = (jnp.arange(positions, dtype=i32)[None, :] < lengths[:, None])[:, None, None, :]
    scores = jnp.where(visible, scores, -1e30)
    highest = jnp.maximum(jnp.max(scores, axis=-1), own_score)
    weights = jnp.where(visible, jnp.exp(scores - highest[..., None]), 0.0)
    own_weight = jnp.exp(own_score - highest)
    denominator = jnp.sum(weights, axis=-1) + own_weight
    probabilities = (weights / denominator[..., None]).astype(bf16)
    own_prob = (own_weight / denominator).astype(bf16).astype(f32)
    attended = jnp.einsum(
        "sgql,slgd->sgqd", probabilities, fetched[:, :, 1], preferred_element_type=f32
    )
    attended = attended + own_prob[..., None] * fresh_kv[:, 1].astype(f32)[:, :, None, :]
    return attended.reshape(slot_count, -1)


def any_shards(queries, new_kv, kv_pool, page_table, ctx_len, residual_in, norm_gain, w_up, w_down):
    attended = attend_slots(queries, new_kv, kv_pool, page_table, ctx_len)
    mixed_rows = residual_in.astype(f32) + attended
    mean_square = jnp.mean(mixed_rows * mixed_rows, axis=-1, keepdims=True)
    normed = (mixed_rows * lax.rsqrt(mean_square + epsilon) * norm_gain.astype(f32)).astype(bf16)
    live_mask = ctx_len > 0
    spread = lax.all_to_all(normed, "side", split_axis=1, concat_axis=0, tiled=True)
    up_partial = jnp.dot(
        lax.all_gather(spread, "shard", axis=0, tiled=True), w_up, preferred_element_type=f32
    )
    lifted = lax.psum(up_partial, "side")
    clipped = jnp.maximum(lifted, 0.0)
    active = (clipped * clipped).astype(bf16)
    down_share = lax.psum_scatter(
        jnp.dot(active, w_down, preferred_element_type=f32).astype(bf16),
        "shard",
        scatter_dimension=0,
        tiled=True,
    )
    returned = lax.all_to_all(down_share, "side", split_axis=0, concat_axis=1, tiled=True)
    returned = jnp.where(live_mask[:, None], returned.astype(f32), 0.0)
    return (mixed_rows + returned).astype(bf16)


def solution(mesh):
    rows = ("grp", "side", "shard")
    placed = (
        P(rows, None),
        P(rows, None),
        P(rows, None, None),
        P(rows, None),
        P(rows),
        P(rows, None),
        P(),
        P("side", "shard"),
        P("shard", "side"),
    )
    square = mesh.shape["side"] == 4 and mesh.shape["shard"] == 4
    return jax.shard_map(
        line_shards if square else any_shards,
        mesh=mesh,
        in_specs=placed,
        out_specs=P(rows, None),
        check_vma=False,
    )
```

```python
import functools
import math

import jax
import jax.numpy as jnp
from jax import lax
from jax.experimental import pallas as pl
from jax.experimental.pallas import tpu as pltpu
from jax.sharding import PartitionSpec as P

KV_HEADS = 8
HEAD = 128
GROUP = 8
LIVE_CAP = 12
PAD = 16
TALL = 2 * LIVE_CAP
EMPTY = 1e30

epsilon = 1e-05
bf16, f32, i32 = jnp.bfloat16, jnp.float32, jnp.int32
VMEM_MB = 1 << 20


def params(mb, **more):
    return pltpu.CompilerParams(vmem_limit_bytes=mb * VMEM_MB, **more)


def cost(flops, bytes_accessed):
    return pl.CostEstimate(
        flops=int(flops) // 64, bytes_accessed=int(bytes_accessed) // 64, transcendentals=0
    )


def pad_rows(x):
    rows = x.shape[0]
    if rows == PAD:
        return x
    return jnp.concatenate([x, jnp.zeros((PAD - rows,) + x.shape[1:], x.dtype)], axis=0)


def live_ranks(lengths, slots):
    live, rank, count = [], [], jnp.int32(0)
    for slot in range(slots):
        alive = lengths[slot] > 0
        live.append(alive)
        rank.append(count)
        count = count + alive.astype(i32)
    return live, rank


def token_bias(lengths, table, pages, page):
    slots, entries = table.shape
    tokens = pages * page
    lanes = 128 * ((pages + 127) // 128)
    row = lax.broadcasted_iota(i32, (PAD, lanes), 0)
    column = lax.broadcasted_iota(i32, (PAD, lanes), 1)
    reach = jnp.zeros((PAD, lanes), i32)
    for slot in range(slots):
        reach = jnp.where(row == slot, lengths[slot], reach)
    table = pad_rows(table)
    seen = jnp.zeros((PAD, lanes), i32)
    for entry in range(entries):
        here = jnp.minimum(jnp.maximum(reach - entry * page, 0), page)
        seen = seen + jnp.where(table[:, entry : entry + 1] == column, here, 0)
    spread = (
        lax.broadcasted_iota(i32, (lanes, tokens), 1) // page
        == lax.broadcasted_iota(i32, (lanes, tokens), 0)
    )
    seen_tokens = jnp.dot(
        seen.astype(f32).astype(bf16), spread.astype(f32).astype(bf16), preferred_element_type=f32
    )
    place = (lax.broadcasted_iota(i32, (PAD, tokens), 1) % page).astype(f32)
    return jnp.where(place < seen_tokens, 0.0, -1e30)


def live_pick(lengths, of_rank, of_slot, slots):
    live, rank = live_ranks(lengths, slots)
    pick = jnp.zeros(of_rank.shape, f32)
    for slot in range(slots):
        chosen = jnp.logical_and(of_rank == rank[slot], of_slot == slot)
        pick = jnp.where(jnp.logical_and(chosen, live[slot]), 1.0, pick)
    return pick.astype(bf16), rank[-1] + live[-1].astype(i32)


def back_rank(row, t, tiles):
    first, last = row - 8 * t, row - 8 * tiles - (LIVE_CAP - 8) * t
    rest = jnp.where(jnp.logical_and(last >= 0, last < LIVE_CAP - 8), last + 8, -1)
    return jnp.where(jnp.logical_and(first >= 0, first < 8), first, rest)


POOL_CUTS = 4


def attend_kernel(*refs, masks, sides, first):
    side = lax.axis_index("side")
    refs = list(refs)
    take = lambda n: [refs.pop(0) for _ in range(n)]
    if first:
        lengths, table_ref = take(2)
        sources = take(4)
    else:
        q_ref, new_ref, res_ref, gain_ref, bias_ref, picks_ref, empty_ref = take(7)
    pool_source = refs.pop(0)
    sends, mixed_refs = take(len(masks)), take(len(masks))
    square_ref = refs.pop(0)
    if first:
        q_ref, new_ref, res_ref, gain_ref, bias_ref, picks_ref, empty_ref, back_ref = take(8)
        gain_copy, sems = take(2)
    pool_ref, pool_sems = refs
    slots, step = mixed_refs[0].shape
    pages, page, width = pool_source.shape
    columns = width // 2 // sides
    heads = columns // HEAD
    tokens = pages * page
    scale = math.log2(math.e) / math.sqrt(HEAD)

    if first:
        small = [
            pltpu.make_async_copy(source, target, sems.at[n])
            for n, (source, target) in enumerate(
                zip(sources, (q_ref, new_ref, res_ref, gain_copy), strict=True)
            )
        ]
        for copy in small:
            copy.start()
    cut, half, pair = pages // POOL_CUTS, width // 2, columns * 2
    here = lax.div(side ^ masks[0], 2) * pair
    brought = []
    for n, at in enumerate((here, half + here)):
        columns_at = pl.ds(pl.multiple_of(at, pair), pair)
        target_at = pl.ds(n * pair, pair)
        brought.append([])
        for c in range(POOL_CUTS):
            rows = pl.ds(c * cut, cut)
            copy = pltpu.make_async_copy(
                pool_source.at[rows, :, columns_at], pool_ref.at[rows, :, target_at], pool_sems.at[n, c]
            )
            copy.start()
            brought[n].append(copy)
    if first:
        bias_ref[...] = token_bias(lengths, table_ref[...], pages, page)
        rank, slot = (lax.broadcasted_iota(i32, (TALL, PAD), n) for n in range(2))
        for head in range(heads):
            picks_ref[head], count = live_pick(lengths, rank - head * LIVE_CAP, slot, slots)
        rank = lax.broadcasted_iota(i32, empty_ref.shape, 0)
        rank = jnp.where(rank < LIVE_CAP, rank, rank - LIVE_CAP)
        empty_ref[...] = (rank >= count).astype(f32)
        slot, row = (lax.broadcasted_iota(i32, back_ref.shape[1:], n) for n in range(2))
        for t in range(back_ref.shape[0]):
            rank = back_rank(row, t, back_ref.shape[0])
            back_ref[t] = live_pick(lengths, rank, slot, slots)[0]
        for copy in small:
            copy.wait()
        gain_ref[...] = gain_copy[...].astype(f32)
    for copy in brought[0]:
        copy.wait()
    values_to_come = brought[1]

    squares = jnp.zeros((slots, HEAD), f32)
    bias = bias_ref[...][None]
    jobs = [(n, head) for n in range(len(masks)) for head in range(heads)]

    def places(job):
        block, base = side ^ masks[job[0]], job[1] * GROUP * HEAD
        new_at = pl.multiple_of(block * columns, columns) + job[1] * HEAD
        key_at = pl.multiple_of(lax.rem(block, 2) * columns, columns) + job[1] * HEAD
        return block, base, pl.multiple_of(block * step, step) + base, new_at, key_at

    def score(job):
        _, _, start, new_at, key_at = places(job)
        q = jnp.concatenate(
            [pad_rows(q_ref[:, pl.ds(start + g * HEAD, HEAD)]) for g in range(GROUP)], axis=0
        )
        keys = pool_ref[:, :, pl.ds(key_at, HEAD)].reshape(tokens, HEAD)
        new_key = pad_rows(new_ref[:, pl.ds(new_at, HEAD)]).astype(f32)
        scores = lax.dot_general(q, keys, (((1,), (1,)), ((), ())), preferred_element_type=f32)
        own = jnp.sum(
            q.astype(f32).reshape(GROUP, PAD, HEAD) * new_key[None], axis=-1, keepdims=True
        )
        return scores.reshape(GROUP, PAD, tokens), own * scale

    ready = score(jobs[0])
    for number, job in enumerate(jobs):
        block, base, start, new_at, key_at = places(job)
        scores, own = ready
        if number + 1 < len(jobs):
            ready = score(jobs[number + 1])
        scores = scores * scale + bias
        highest = jnp.maximum(jnp.max(scores, axis=-1, keepdims=True), own)
        weights = jnp.exp2(scores - highest)
        own_weight = jnp.exp2(own - highest)
        total = jnp.sum(weights, axis=-1, keepdims=True) + own_weight
        for copy in values_to_come:
            copy.wait()
        values_to_come = []
        values = pool_ref[:, :, pl.ds(pair + key_at, HEAD)].reshape(tokens, HEAD)
        new_value = pad_rows(new_ref[:, pl.ds(half + new_at, HEAD)]).astype(f32)
        summed = jnp.dot(
            weights.astype(bf16).reshape(GROUP * PAD, tokens), values, preferred_element_type=f32
        ).reshape(GROUP, PAD, HEAD)
        attended = (summed + own_weight * new_value[None]) / total
        for g in range(GROUP):
            at = slice(base + g * HEAD, base + (g + 1) * HEAD)
            residual = res_ref[:, pl.ds(start + g * HEAD, HEAD)].astype(f32)
            mixed = residual + attended[g][:slots]
            mixed_refs[job[0]][:, at] = mixed
            squares = squares + mixed * mixed
            gain = gain_ref[pl.ds(block * (step // HEAD) + job[1] * GROUP + g, 1), :]
            gained = pad_rows((mixed * gain).astype(bf16))
            rows = jnp.dot(picks_ref[job[1]], gained, preferred_element_type=f32)
            to = slice(g * HEAD, (g + 1) * HEAD)
            if job[1]:
                rows = rows + sends[job[0]][:, to].astype(f32)
                rows = jnp.where(empty_ref[...] > 0, EMPTY, rows)
            sends[job[0]][:, to] = rows.astype(bf16)
    square_ref[...] = squares


def attend(inputs, sides, masks, before):
    queries, new_kv, kv_pool, page_table, ctx_len, residual_in, norm_gain = inputs
    slots, columns = queries.shape
    pages, page, _ = kv_pool.shape
    step = columns // sides
    first = before is None
    vmem, anywhere = pl.BlockSpec(memory_space=pltpu.VMEM), pl.BlockSpec(memory_space=pl.ANY)
    smem = pl.BlockSpec(memory_space=pltpu.SMEM)
    out_shape = [jax.ShapeDtypeStruct((TALL, step // 2), bf16)] * len(masks)
    out_shape += [jax.ShapeDtypeStruct((slots, step), f32)] * len(masks)
    out_shape += [jax.ShapeDtypeStruct((slots, HEAD), f32)]
    if first:
        operands = [ctx_len, page_table, queries, new_kv, residual_in, norm_gain, kv_pool]
        in_specs = [smem, vmem] + [anywhere] * 5
        tiles = step // DOWN_TILE
        out_shape += [
            pltpu.VMEM(queries.shape, bf16),
            pltpu.VMEM(new_kv.shape, bf16),
            pltpu.VMEM(residual_in.shape, bf16),
            pltpu.VMEM(norm_gain.shape, f32),
            pltpu.VMEM((PAD, pages * page), f32),
            pltpu.VMEM((columns // HEAD // GROUP // sides, TALL, PAD), bf16),
            pltpu.VMEM((TALL, HEAD), f32),
            pltpu.VMEM((tiles, PAD, tiles * LIVE_CAP), bf16),
        ]
        scratch = [pltpu.VMEM(norm_gain.shape, bf16), pltpu.SemaphoreType.DMA((4,))]
    else:
        operands = [*before, kv_pool]
        in_specs = [vmem] * len(before) + [anywhere]
        scratch = []
    scratch += [
        pltpu.VMEM((pages, page, kv_pool.shape[2] // sides * 2), bf16),
        pltpu.SemaphoreType.DMA((2, POOL_CUTS)),
    ]
    outs = pl.pallas_call(
        functools.partial(attend_kernel, masks=masks, sides=sides, first=first),
        in_specs=in_specs,
        out_specs=[vmem] * len(out_shape),
        out_shape=out_shape,
        scratch_shapes=scratch,
        compiler_params=params(28),
        cost_estimate=cost(2e9, kv_pool.size),
        name="attend",
    )(*operands)
    n = len(masks)
    return outs[:n], outs[n : 2 * n], outs[2 * n], outs[2 * n + 1 :]


UP_TILE = 256
DOWN_TILE = 512


def tile_copy(w_ref, row, rows, column, buffer, sems, t, tile):
    at = pl.ds(pl.multiple_of(t * tile, tile), tile)
    source = w_ref.at[pl.ds(row, rows), pl.ds(pl.multiple_of(column + t * tile, tile), tile)]
    return pltpu.make_async_copy(source, buffer.at[:, at], sems.at[t])


def up_kernel(x_ref, w_ref, out_ref, buffer, sems, *, masks):
    side = lax.axis_index("side")
    depth, width = buffer.shape[1:]
    tiles = width // UP_TILE

    def copy_of(n, t):
        column = pl.multiple_of(((side ^ masks[n][0]) * 2 + masks[n][1]) * width, width)
        return tile_copy(w_ref, 0, depth, column, buffer.at[n], sems.at[n], t, UP_TILE)

    for n in range(len(masks)):
        for t in range(tiles):
            copy_of(n, t).start()

    @pl.loop(0, len(masks) * tiles)
    def _(job):
        n, t = lax.div(job, tiles), lax.rem(job, tiles)
        at = pl.ds(pl.multiple_of(t * UP_TILE, UP_TILE), UP_TILE)
        pltpu.make_async_copy(
            w_ref.at[:, pl.ds(0, UP_TILE)], buffer.at[n, :, at], sems.at[n, t]
        ).wait()
        out_ref[n, :, at] = jnp.dot(
            x_ref[: out_ref.shape[1], :], buffer[n, :, at], preferred_element_type=f32
        ).astype(out_ref.dtype)


def up(packed, w_up, rows, width, masks):
    depth = packed.shape[1]
    vmem = pl.BlockSpec(memory_space=pltpu.VMEM)
    return pl.pallas_call(
        functools.partial(up_kernel, masks=masks),
        in_specs=[vmem, pl.BlockSpec(memory_space=pl.ANY)],
        out_specs=vmem,
        out_shape=jax.ShapeDtypeStruct((len(masks), rows, width), bf16),
        scratch_shapes=[
            pltpu.VMEM((len(masks), depth, width), bf16),
            pltpu.SemaphoreType.DMA((len(masks), width // UP_TILE)),
        ],
        compiler_params=params(24),
        cost_estimate=cost(2 * rows * depth * width, depth * width * 2 * len(masks)),
        name="up",
    )(packed, w_up)


PIECES = ((0, 2), (1, 3))


def find_layout(gathered, layout, step_ref, limits):
    side, shard = lax.axis_index("side"), lax.axis_index("shard")
    pieces = gathered[0].shape[0] // TALL
    devices = len(gathered) * pieces
    counts, places = [None] * devices, [None] * devices
    number = lax.broadcasted_iota(i32, (LIVE_CAP, HEAD), 0) + 1
    for part in range(len(gathered)):
        marks = gathered[part][:, :HEAD].astype(f32)
        for piece, mask in enumerate(PIECES[part % 2]):
            rows = marks[piece * TALL : piece * TALL + LIVE_CAP]
            last = jnp.where(rows < EMPTY / 2, number, 0).astype(f32)
            place = part // 2 * 4 + mask
            counts[place] = jnp.max(last).astype(i32)
            places[place] = (side ^ mask) * 4 + (shard ^ (part // 2))
    total = jnp.int32(0)
    for one in range(devices):
        base = jnp.int32(0)
        for other in range(devices):
            base = base + jnp.where(places[other] < places[one], counts[other], 0)
        layout[one] = base
        layout[devices + one] = counts[one]
        total = total + counts[one]
    step = jnp.int32(0)
    for limit in limits:
        step = step + (total > limit).astype(i32)
    step_ref[0] = step


def pack_up_kernel(*refs, mask, limits):
    gathered, refs = refs[:-7], refs[-7:]
    w_ref, packed_ref, out_ref, layout, step_ref, buffer, sems = refs
    width = out_ref.shape[1]

    def copy_of(t):
        column = pl.multiple_of((lax.axis_index("side") ^ mask) * 2 * width, width)
        return tile_copy(w_ref, 0, buffer.shape[0], column, buffer, sems, t, UP_TILE)

    for t in range(width // UP_TILE):
        copy_of(t).start()
    find_layout(gathered, layout, step_ref, limits)
    rows, depth = packed_ref.shape
    per = gathered[0].shape[0]
    pieces = per // TALL
    devices = len(gathered) * pieces
    shape = (8, len(gathered) * per)
    lane = lax.broadcasted_iota(i32, shape, 1)
    row = lax.broadcasted_iota(i32, (rows, shape[1]), 0)
    for half in range(2):
        target = jnp.full(shape, -1, i32)
        for part in range(len(gathered)):
            for piece, other in enumerate(PIECES[part % 2]):
                place = part // 2 * 4 + other
                base, count = layout[place], layout[devices + place]
                inside = lane - (part * per + piece * TALL + half * LIVE_CAP)
                mine = jnp.logical_and(inside >= 0, inside < count)
                target = jnp.where(mine, base + inside, target)
        pick = (target[:1] == row).astype(f32).astype(bf16)

        @pl.loop(0, depth // 2 // DOWN_TILE)
        def _(t):
            at = pl.ds(pl.multiple_of(t * DOWN_TILE, DOWN_TILE), DOWN_TILE)
            to = pl.ds(pl.multiple_of(half * (depth // 2) + t * DOWN_TILE, DOWN_TILE), DOWN_TILE)
            found = jnp.concatenate([part[:, at] for part in gathered], axis=0)
            packed_ref[:, to] = jnp.dot(pick, found, preferred_element_type=f32).astype(bf16)

    @pl.loop(0, width // UP_TILE)
    def _(t):
        copy_of(t).wait()
        at = pl.ds(pl.multiple_of(t * UP_TILE, UP_TILE), UP_TILE)
        out_ref[:, at] = jnp.dot(
            packed_ref[...], buffer[:, at], preferred_element_type=f32
        ).astype(bf16)


def pack_up(gathered, w_up, rows, width, mask, limits):
    depth = w_up.shape[0]
    devices = len(gathered) * gathered[0].shape[0] // TALL
    vmem, smem = pl.BlockSpec(memory_space=pltpu.VMEM), pl.BlockSpec(memory_space=pltpu.SMEM)
    return pl.pallas_call(
        functools.partial(pack_up_kernel, mask=mask, limits=limits),
        in_specs=[vmem] * len(gathered) + [pl.BlockSpec(memory_space=pl.ANY)],
        out_specs=[vmem, vmem, smem, smem],
        out_shape=[
            jax.ShapeDtypeStruct((rows, depth), bf16),
            jax.ShapeDtypeStruct((rows, width), bf16),
            jax.ShapeDtypeStruct((2 * devices,), i32),
            jax.ShapeDtypeStruct((1,), i32),
        ],
        scratch_shapes=[
            pltpu.VMEM((depth, width), bf16),
            pltpu.SemaphoreType.DMA((width // UP_TILE,)),
        ],
        compiler_params=params(24),
        cost_estimate=cost(2 * rows * depth * width, depth * width * 2),
        name="pack_up",
    )(*gathered, w_up)


def down_kernel(*refs, first, mask, ahead):
    refs = list(refs)
    a_ref, w_ref = refs.pop(0), refs.pop(0)
    before_ref = None if first else refs.pop(0)
    out_ref = refs.pop(0)
    next_ref = refs.pop(0) if ahead is not None else None
    buffer, sems = refs.pop(0), refs.pop(0)
    depth, width = buffer.shape
    tiles = width // DOWN_TILE

    def copy_of(other, buffer, sems, t):
        row = pl.multiple_of((lax.axis_index("side") ^ other) * depth, depth)
        return tile_copy(w_ref, row, depth, 0, buffer, sems, t, DOWN_TILE)

    for t in range(tiles):
        copy_of(mask, buffer, sems, t).start()
    if ahead is not None:
        for t in range(tiles):
            copy_of(ahead, next_ref, refs[0], t).start()

    @pl.loop(0, tiles)
    def _(t):
        at = pl.ds(pl.multiple_of(t * DOWN_TILE, DOWN_TILE), DOWN_TILE)
        copy_of(mask, buffer, sems, t).wait()
        part = jnp.dot(a_ref[...], buffer[:, at], preferred_element_type=f32)
        out_ref[:, at] = part if first else before_ref[:, at] + part

    if ahead is not None:

        @pl.loop(0, tiles)
        def _(t):
            copy_of(ahead, next_ref, refs[0], t).wait()


def down(active, w_down, before, mask, ahead=None):
    rows, depth = active.shape
    width = w_down.shape[1]
    vmem = pl.BlockSpec(memory_space=pltpu.VMEM)
    out = jax.ShapeDtypeStruct((rows, width), f32)
    sems = pltpu.SemaphoreType.DMA((width // DOWN_TILE,))
    return pl.pallas_call(
        functools.partial(down_kernel, first=before is None, mask=mask, ahead=ahead),
        in_specs=[vmem, pl.BlockSpec(memory_space=pl.ANY)]
        + ([] if before is None else [vmem]),
        out_specs=vmem if ahead is None else [vmem, vmem],
        out_shape=out if ahead is None else [out, pltpu.VMEM((depth, width), bf16)],
        scratch_shapes=[pltpu.VMEM((depth, width), bf16), sems]
        + ([] if ahead is None else [sems]),
        compiler_params=params(24),
        cost_estimate=cost(2 * rows * depth * width, depth * width * 2),
        name="down",
    )(active, w_down, *([] if before is None else [before]))


BACK = ((2, 3), (0, 1))


def back_picks_kernel(layout, out):
    _, devices, _, rows = out.shape
    row = lax.broadcasted_iota(i32, (PAD, rows), 0)
    column = lax.broadcasted_iota(i32, (PAD, rows), 1)
    late = jnp.where(row < 8, row, jnp.where(row < LIVE_CAP, LIVE_CAP, row - (PAD - LIVE_CAP)))
    device = 0
    for core in (0, 1):
        for x in (2, 0):
            for masks in BACK:
                for mask in masks:
                    place = (x + core) * 4 + mask
                    base, count = layout[place], layout[devices + place]
                    for parity, rank in enumerate((row, late)):
                        mine = jnp.logical_and(column - rank == base, rank < count)
                        out[parity, device] = mine.astype(f32).astype(bf16)
                    device += 1


def back_picks(layout, rows):
    devices = layout.shape[0] // 2
    return pl.pallas_call(
        back_picks_kernel,
        in_specs=[pl.BlockSpec(memory_space=pltpu.SMEM)],
        out_specs=pl.BlockSpec(memory_space=pltpu.VMEM),
        out_shape=jax.ShapeDtypeStruct((2, devices, PAD, rows), bf16),
        compiler_params=params(16),
        name="back_picks",
    )(layout)


def down_unpack_kernel(picks_ref, a_ref, w_ref, before_ref, *refs):
    outs, wide = refs[:-1], refs[-1]
    rows = a_ref.shape[0]
    tiles, devices = wide.shape[:2]
    group = devices // len(outs)

    @pl.loop(0, tiles)
    def _(t):
        at = pl.ds(pl.multiple_of(t * DOWN_TILE, DOWN_TILE), DOWN_TILE)
        share = before_ref[:, at] + jnp.dot(a_ref[...], w_ref[:, at], preferred_element_type=f32)
        pick = picks_ref[lax.rem(t, 2)].reshape(devices * PAD, rows)
        back = jnp.dot(pick, share.astype(bf16), preferred_element_type=f32)
        wide[t] = back.reshape(devices, PAD, DOWN_TILE)

    per = tiles * LIVE_CAP
    for n, out in enumerate(outs):

        @pl.loop(0, group)
        def _(device):
            here = [wide[t, n * group + device] for t in range(tiles)]
            late = [here[t][8:] + here[t + 1][8:] for t in range(0, tiles, 2)]
            rows = pl.ds(pl.multiple_of(device * per, per), per)
            out[rows, :] = jnp.concatenate([h[:8] for h in here] + late, axis=0).astype(bf16)


def down_unpack(picks, active, weights, before):
    rows, depth = active.shape
    width = weights.shape[1]
    tiles, devices = width // DOWN_TILE, picks.shape[1]
    vmem = pl.BlockSpec(memory_space=pltpu.VMEM)
    out = jax.ShapeDtypeStruct((devices // 2 * tiles * LIVE_CAP, DOWN_TILE), bf16)
    return pl.pallas_call(
        down_unpack_kernel,
        in_specs=[vmem] * 4,
        out_specs=[vmem] * 2,
        out_shape=[out] * 2,
        scratch_shapes=[pltpu.VMEM((tiles, devices, PAD, DOWN_TILE), f32)],
        compiler_params=params(24),
        cost_estimate=cost(2 * rows * depth * width, rows * width * 4),
        name="down_unpack",
    )(picks, active, weights, before)


def finish_kernel(picks_ref, *refs):
    side = lax.axis_index("side")
    out_ref = refs[-1]
    sides = (len(refs) - 3) // 2
    mixed, squares, blocks = refs[:sides], refs[sides : sides + 2], refs[sides + 2 : -1]
    slots, width = out_ref.shape
    step = width // sides
    total = squares[0][...] + squares[1][...]
    root = lax.rsqrt(jnp.sum(total, axis=-1, keepdims=True) / width + epsilon)
    gain = root * root
    tiles = step // DOWN_TILE
    for shift in range(sides):
        base = (side ^ shift) * step
        block = blocks[shift][...]
        for t in range(tiles):
            back = jnp.dot(picks_ref[t], block, preferred_element_type=f32)[:slots]
            at = pl.multiple_of(base + t * DOWN_TILE, DOWN_TILE)
            here = mixed[shift][:, t * DOWN_TILE : (t + 1) * DOWN_TILE]
            out_ref[:, pl.ds(at, DOWN_TILE)] = (here + gain * back).astype(bf16)


def finish(picks, mixed, squares, blocks):
    vmem = pl.BlockSpec(memory_space=pltpu.VMEM)
    slots, width = mixed[0].shape[0], mixed[0].shape[1] * len(mixed)
    return pl.pallas_call(
        finish_kernel,
        in_specs=[vmem] * (2 * len(mixed) + 3),
        out_specs=vmem,
        out_shape=jax.ShapeDtypeStruct((slots, width), bf16),
        compiler_params=params(16),
        cost_estimate=cost(slots * width * 32, slots * width * 8),
        name="finish",
    )(picks, *mixed, *squares, *blocks)


def swap(x, axis, count, mask):
    return lax.ppermute(x, axis, [(j, j ^ mask) for j in range(count)])


def added(a, b):
    return (a.astype(f32) + b.astype(f32)).astype(bf16)


def tie(x, *others):
    return lax.optimization_barrier((x, *others))[0]


def squared_relu(*terms):
    lifted = sum(term.astype(f32) for term in terms)
    clipped = jnp.maximum(lifted, 0.0)
    return (clipped * clipped).astype(bf16)


def feed_forward(rows, layout, packed, other, w_up, w_down):
    half = w_up.shape[1] // 8
    across = lambda x: swap(x, "side", 4, 2)
    beside = lambda x: swap(x, "side", 4, 1)
    met_0 = beside(other[:rows])
    far = up(packed, w_up, rows, half, ((3, 1), (2, 0), (2, 1)))
    met_1 = beside(far[0])
    sum_0 = added(far[1], met_0)
    crossed_0 = across(sum_0)
    near = up(tie(packed, sum_0), w_up, rows, half, ((1, 0), (1, 1)))
    met_1, near = lax.optimization_barrier((met_1, near))
    sum_1 = added(far[2], met_1)
    crossed_1 = across(sum_1)
    near = beside(near)
    own = up(tie(packed, sum_1), w_up, rows, half, ((0, 0), (0, 1)))
    active = [squared_relu(own[n], near[n], crossed) for n, crossed in enumerate((crossed_0, crossed_1))]
    active = jnp.concatenate(active, axis=1)
    over, following = across(active), beside(active)
    total = down(active, w_down, None, 0)
    picks = back_picks(tie(layout, total), rows)
    forward = beside(tie(over, picks))
    total = down(following, w_down, total, 1)
    total, weights = down(over, w_down, total, 2, ahead=3)
    return down_unpack(picks, forward, weights, total)


ROW_STEPS = (112, 120, 128, 136, 144, 160, 192)


def line_shards(
    queries, new_kv, kv_pool, page_table, ctx_len, residual_in, norm_gain, w_up, w_down
):
    in_hbm = lambda x: pltpu.with_memory_space_constraint(x, pltpu.HBM)
    gain = norm_gain.reshape(-1, HEAD)
    inputs = queries, new_kv, kv_pool, page_table, ctx_len, residual_in, gain
    inputs, w_up, w_down = jax.tree.map(in_hbm, (inputs, w_up, w_down))
    (to_2, to_3), mixed_far, squares_far, copies = attend(inputs, 4, (2, 3), None)
    *copies, back_picks = copies
    met = swap(jnp.concatenate([to_2, to_3], axis=0), "side", 4, 2)
    (own, to_1), mixed_near, squares_near, _ = attend(inputs, 4, (0, 1), copies)
    first = jnp.concatenate([own, met[:TALL]], axis=0)
    second = swap(jnp.concatenate([to_1, met[TALL:]], axis=0), "side", 4, 1)
    gathered = []
    by_x = [swap(here, "shard", 4, 2) for here in (first, second)]
    by_core = [swap(here, "shard", 4, 1) for here in (first, second)]
    by_both = [swap(there, "shard", 4, 1) for there in by_x]
    gathered = [first, second, *by_core, *by_x, *by_both]
    packed, other, layout, step = pack_up(
        gathered, w_up, ROW_STEPS[-1], w_up.shape[1] // 8, 3, ROW_STEPS[:-1]
    )
    stay, leave = lax.switch(
        step[0],
        [functools.partial(feed_forward, rows) for rows in ROW_STEPS],
        layout, packed, other, w_up, w_down,
    )
    back = swap(leave, "shard", 4, 1)
    quarter = back.shape[0] // 4
    piece = quarter // 2
    cuts = [slice(at, at + quarter) for at in range(0, 4 * quarter, quarter)]
    sums = [added(stay[cut], back[cut]) for cut in cuts]
    far = added(sums[2], swap(sums[0], "shard", 4, 2))
    near = added(sums[3], swap(sums[1], "shard", 4, 2))
    home = near[:piece], near[piece:], far[:piece], far[piece:]
    blocks = [home[0]] + [swap(home[mask], "side", 4, mask) for mask in (1, 2, 3)]
    mixed = [*mixed_near, *mixed_far]
    return finish(back_picks, mixed, [squares_far, squares_near], blocks)


def attend_slots(queries, new_kv, pool_pages, page_rows, lengths):
    slot_count = queries.shape[0]
    positions = page_rows.shape[1] * pool_pages.shape[1]
    fetched = pool_pages[page_rows].reshape(slot_count, positions, 2, KV_HEADS, HEAD)
    fresh_kv = new_kv.reshape(slot_count, 2, KV_HEADS, HEAD)
    query_heads = queries.reshape(slot_count, KV_HEADS, GROUP, HEAD)
    score_scale = 1.0 / math.sqrt(HEAD)
    scores = (
        jnp.einsum("sgqd,slgd->sgql", query_heads, fetched[:, :, 0], preferred_element_type=f32)
        * score_scale
    )
    own_score = (
        jnp.einsum("sgqd,sgd->sgq", query_heads, fresh_kv[:, 0], preferred_element_type=f32)
        * score_scale
    )
    visible = (jnp.arange(positions, dtype=i32)[None, :] < lengths[:, None])[:, None, None, :]
    scores = jnp.where(visible, scores, -1e30)
    highest = jnp.maximum(jnp.max(scores, axis=-1), own_score)
    weights = jnp.where(visible, jnp.exp(scores - highest[..., None]), 0.0)
    own_weight = jnp.exp(own_score - highest)
    denominator = jnp.sum(weights, axis=-1) + own_weight
    probabilities = (weights / denominator[..., None]).astype(bf16)
    own_prob = (own_weight / denominator).astype(bf16).astype(f32)
    attended = jnp.einsum(
        "sgql,slgd->sgqd", probabilities, fetched[:, :, 1], preferred_element_type=f32
    )
    attended = attended + own_prob[..., None] * fresh_kv[:, 1].astype(f32)[:, :, None, :]
    return attended.reshape(slot_count, -1)


def any_shards(queries, new_kv, kv_pool, page_table, ctx_len, residual_in, norm_gain, w_up, w_down):
    attended = attend_slots(queries, new_kv, kv_pool, page_table, ctx_len)
    mixed_rows = residual_in.astype(f32) + attended
    mean_square = jnp.mean(mixed_rows * mixed_rows, axis=-1, keepdims=True)
    normed = (mixed_rows * lax.rsqrt(mean_square + epsilon) * norm_gain.astype(f32)).astype(bf16)
    live_mask = ctx_len > 0
    spread = lax.all_to_all(normed, "side", split_axis=1, concat_axis=0, tiled=True)
    up_partial = jnp.dot(
        lax.all_gather(spread, "shard", axis=0, tiled=True), w_up, preferred_element_type=f32
    )
    lifted = lax.psum(up_partial, "side")
    clipped = jnp.maximum(lifted, 0.0)
    active = (clipped * clipped).astype(bf16)
    down_share = lax.psum_scatter(
        jnp.dot(active, w_down, preferred_element_type=f32).astype(bf16),
        "shard",
        scatter_dimension=0,
        tiled=True,
    )
    returned = lax.all_to_all(down_share, "side", split_axis=0, concat_axis=1, tiled=True)
    returned = jnp.where(live_mask[:, None], returned.astype(f32), 0.0)
    return (mixed_rows + returned).astype(bf16)


def solution(mesh):
    rows = ("grp", "side", "shard")
    placed = (
        P(rows, None),
        P(rows, None),
        P(rows, None, None),
        P(rows, None),
        P(rows),
        P(rows, None),
        P(),
        P("side", "shard"),
        P("shard", "side"),
    )
    square = mesh.shape["side"] == 4 and mesh.shape["shard"] == 4
    return jax.shard_map(
        line_shards if square else any_shards,
        mesh=mesh,
        in_specs=placed,
        out_specs=P(rows, None),
        check_vma=False,
    )
```

```python
import functools
import math

import jax
import jax.numpy as jnp
from jax import lax
from jax.experimental import pallas as pl
from jax.experimental.pallas import tpu as pltpu
from jax.sharding import PartitionSpec as P

KV_HEADS = 8
HEAD = 128
GROUP = 8
LIVE_CAP = 12
PAD = 16
TALL = 2 * LIVE_CAP
EMPTY = 1e30

epsilon = 1e-05
bf16, f32, i32 = jnp.bfloat16, jnp.float32, jnp.int32
VMEM_MB = 1 << 20


def params(mb, **more):
    return pltpu.CompilerParams(vmem_limit_bytes=mb * VMEM_MB, **more)


def cost(flops, bytes_accessed):
    return pl.CostEstimate(
        flops=int(flops) // 64, bytes_accessed=int(bytes_accessed) // 64, transcendentals=0
    )


def pad_rows(x):
    rows = x.shape[0]
    if rows == PAD:
        return x
    return jnp.concatenate([x, jnp.zeros((PAD - rows,) + x.shape[1:], x.dtype)], axis=0)


def live_ranks(lengths, slots):
    live, rank, count = [], [], jnp.int32(0)
    for slot in range(slots):
        alive = lengths[slot] > 0
        live.append(alive)
        rank.append(count)
        count = count + alive.astype(i32)
    return live, rank


def token_bias(lengths, table, pages, page):
    slots, entries = table.shape
    tokens = pages * page
    lanes = 128 * ((pages + 127) // 128)
    row = lax.broadcasted_iota(i32, (PAD, lanes), 0)
    column = lax.broadcasted_iota(i32, (PAD, lanes), 1)
    reach = jnp.zeros((PAD, lanes), i32)
    for slot in range(slots):
        reach = jnp.where(row == slot, lengths[slot], reach)
    table = pad_rows(table)
    seen = jnp.zeros((PAD, lanes), i32)
    for entry in range(entries):
        here = jnp.minimum(jnp.maximum(reach - entry * page, 0), page)
        seen = seen + jnp.where(table[:, entry : entry + 1] == column, here, 0)
    spread = (
        lax.broadcasted_iota(i32, (lanes, tokens), 1) // page
        == lax.broadcasted_iota(i32, (lanes, tokens), 0)
    )
    seen_tokens = jnp.dot(
        seen.astype(f32).astype(bf16), spread.astype(f32).astype(bf16), preferred_element_type=f32
    )
    place = (lax.broadcasted_iota(i32, (PAD, tokens), 1) % page).astype(f32)
    return jnp.where(place < seen_tokens, 0.0, -1e30)


def live_pick(lengths, of_rank, of_slot, slots):
    live, rank = live_ranks(lengths, slots)
    pick = jnp.zeros(of_rank.shape, f32)
    for slot in range(slots):
        chosen = jnp.logical_and(of_rank == rank[slot], of_slot == slot)
        pick = jnp.where(jnp.logical_and(chosen, live[slot]), 1.0, pick)
    return pick.astype(bf16), rank[-1] + live[-1].astype(i32)


def back_rank(row, t, tiles):
    first, last = row - 8 * t, row - 8 * tiles - (LIVE_CAP - 8) * t
    rest = jnp.where(jnp.logical_and(last >= 0, last < LIVE_CAP - 8), last + 8, -1)
    return jnp.where(jnp.logical_and(first >= 0, first < 8), first, rest)


POOL_CUTS = 4


def attend_kernel(*refs, masks, sides, first):
    side = lax.axis_index("side")
    refs = list(refs)
    take = lambda n: [refs.pop(0) for _ in range(n)]
    if first:
        lengths, table_ref = take(2)
        sources = take(4)
    else:
        q_ref, new_ref, res_ref, gain_ref, bias_ref, picks_ref, empty_ref = take(7)
    pool_source = refs.pop(0)
    sends, mixed_refs = take(len(masks)), take(len(masks))
    square_ref = refs.pop(0)
    if first:
        q_ref, new_ref, res_ref, gain_ref, bias_ref, picks_ref, empty_ref, back_ref = take(8)
        gain_copy, sems = take(2)
    pool_ref, pool_sems = refs
    slots, step = mixed_refs[0].shape
    pages, page, width = pool_source.shape
    columns = width // 2 // sides
    heads = columns // HEAD
    tokens = pages * page
    scale = math.log2(math.e) / math.sqrt(HEAD)

    if first:
        small = [
            pltpu.make_async_copy(source, target, sems.at[n])
            for n, (source, target) in enumerate(
                zip(sources, (q_ref, new_ref, res_ref, gain_copy), strict=True)
            )
        ]
        for copy in small:
            copy.start()
    cut, half, pair = pages // POOL_CUTS, width // 2, columns * 2
    here = lax.div(side ^ masks[0], 2) * pair
    brought = []
    for n, at in enumerate((here, half + here)):
        columns_at = pl.ds(pl.multiple_of(at, pair), pair)
        target_at = pl.ds(n * pair, pair)
        brought.append([])
        for c in range(POOL_CUTS):
            rows = pl.ds(c * cut, cut)
            copy = pltpu.make_async_copy(
                pool_source.at[rows, :, columns_at], pool_ref.at[rows, :, target_at], pool_sems.at[n, c]
            )
            copy.start()
            brought[n].append(copy)
    if first:
        bias_ref[...] = token_bias(lengths, table_ref[...], pages, page)
        rank, slot = (lax.broadcasted_iota(i32, (TALL, PAD), n) for n in range(2))
        for head in range(heads):
            picks_ref[head], count = live_pick(lengths, rank - head * LIVE_CAP, slot, slots)
        rank = lax.broadcasted_iota(i32, empty_ref.shape, 0)
        rank = jnp.where(rank < LIVE_CAP, rank, rank - LIVE_CAP)
        empty_ref[...] = (rank >= count).astype(f32)
        slot, row = (lax.broadcasted_iota(i32, back_ref.shape[1:], n) for n in range(2))
        for t in range(back_ref.shape[0]):
            rank = back_rank(row, t, back_ref.shape[0])
            back_ref[t] = live_pick(lengths, rank, slot, slots)[0]
        for copy in small:
            copy.wait()
        gain_ref[...] = gain_copy[...].astype(f32)
    for copy in brought[0]:
        copy.wait()
    values_to_come = brought[1]

    squares = jnp.zeros((slots, HEAD), f32)
    bias = bias_ref[...][None]
    jobs = [(n, head) for n in range(len(masks)) for head in range(heads)]

    def places(job):
        block, base = side ^ masks[job[0]], job[1] * GROUP * HEAD
        new_at = pl.multiple_of(block * columns, columns) + job[1] * HEAD
        key_at = pl.multiple_of(lax.rem(block, 2) * columns, columns) + job[1] * HEAD
        return block, base, pl.multiple_of(block * step, step) + base, new_at, key_at

    def score(job):
        _, _, start, new_at, key_at = places(job)
        q = jnp.concatenate(
            [pad_rows(q_ref[:, pl.ds(start + g * HEAD, HEAD)]) for g in range(GROUP)], axis=0
        )
        keys = pool_ref[:, :, pl.ds(key_at, HEAD)].reshape(tokens, HEAD)
        new_key = pad_rows(new_ref[:, pl.ds(new_at, HEAD)]).astype(f32)
        scores = lax.dot_general(q, keys, (((1,), (1,)), ((), ())), preferred_element_type=f32)
        own = jnp.sum(
            q.astype(f32).reshape(GROUP, PAD, HEAD) * new_key[None], axis=-1, keepdims=True
        )
        return scores.reshape(GROUP, PAD, tokens), own * scale

    ready = score(jobs[0])
    for number, job in enumerate(jobs):
        block, base, start, new_at, key_at = places(job)
        scores, own = ready
        if number + 1 < len(jobs):
            ready = score(jobs[number + 1])
        scores = scores * scale + bias
        highest = jnp.maximum(jnp.max(scores, axis=-1, keepdims=True), own)
        weights = jnp.exp2(scores - highest)
        own_weight = jnp.exp2(own - highest)
        total = jnp.sum(weights, axis=-1, keepdims=True) + own_weight
        for copy in values_to_come:
            copy.wait()
        values_to_come = []
        values = pool_ref[:, :, pl.ds(pair + key_at, HEAD)].reshape(tokens, HEAD)
        new_value = pad_rows(new_ref[:, pl.ds(half + new_at, HEAD)]).astype(f32)
        summed = jnp.dot(
            weights.astype(bf16).reshape(GROUP * PAD, tokens), values, preferred_element_type=f32
        ).reshape(GROUP, PAD, HEAD)
        attended = (summed + own_weight * new_value[None]) / total
        for g in range(GROUP):
            at = slice(base + g * HEAD, base + (g + 1) * HEAD)
            residual = res_ref[:, pl.ds(start + g * HEAD, HEAD)].astype(f32)
            mixed = residual + attended[g][:slots]
            mixed_refs[job[0]][:, at] = mixed
            squares = squares + mixed * mixed
            gain = gain_ref[pl.ds(block * (step // HEAD) + job[1] * GROUP + g, 1), :]
            gained = pad_rows((mixed * gain).astype(bf16))
            rows = jnp.dot(picks_ref[job[1]], gained, preferred_element_type=f32)
            to = slice(g * HEAD, (g + 1) * HEAD)
            if job[1]:
                rows = rows + sends[job[0]][:, to].astype(f32)
                rows = jnp.where(empty_ref[...] > 0, EMPTY, rows)
            sends[job[0]][:, to] = rows.astype(bf16)
    square_ref[...] = squares


def attend(inputs, sides, masks, before):
    queries, new_kv, kv_pool, page_table, ctx_len, residual_in, norm_gain = inputs
    slots, columns = queries.shape
    pages, page, _ = kv_pool.shape
    step = columns // sides
    first = before is None
    vmem, anywhere = pl.BlockSpec(memory_space=pltpu.VMEM), pl.BlockSpec(memory_space=pl.ANY)
    smem = pl.BlockSpec(memory_space=pltpu.SMEM)
    out_shape = [jax.ShapeDtypeStruct((TALL, step // 2), bf16)] * len(masks)
    out_shape += [jax.ShapeDtypeStruct((slots, step), f32)] * len(masks)
    out_shape += [jax.ShapeDtypeStruct((slots, HEAD), f32)]
    if first:
        operands = [ctx_len, page_table, queries, new_kv, residual_in, norm_gain, kv_pool]
        in_specs = [smem, vmem] + [anywhere] * 5
        tiles = step // DOWN_TILE
        out_shape += [
            pltpu.VMEM(queries.shape, bf16),
            pltpu.VMEM(new_kv.shape, bf16),
            pltpu.VMEM(residual_in.shape, bf16),
            pltpu.VMEM(norm_gain.shape, f32),
            pltpu.VMEM((PAD, pages * page), f32),
            pltpu.VMEM((columns // HEAD // GROUP // sides, TALL, PAD), bf16),
            pltpu.VMEM((TALL, HEAD), f32),
            pltpu.VMEM((tiles, PAD, tiles * LIVE_CAP), bf16),
        ]
        scratch = [pltpu.VMEM(norm_gain.shape, bf16), pltpu.SemaphoreType.DMA((4,))]
    else:
        operands = [*before, kv_pool]
        in_specs = [vmem] * len(before) + [anywhere]
        scratch = []
    scratch += [
        pltpu.VMEM((pages, page, kv_pool.shape[2] // sides * 2), bf16),
        pltpu.SemaphoreType.DMA((2, POOL_CUTS)),
    ]
    outs = pl.pallas_call(
        functools.partial(attend_kernel, masks=masks, sides=sides, first=first),
        in_specs=in_specs,
        out_specs=[vmem] * len(out_shape),
        out_shape=out_shape,
        scratch_shapes=scratch,
        compiler_params=params(28),
        cost_estimate=cost(2e9, kv_pool.size),
        name="attend",
    )(*operands)
    n = len(masks)
    return outs[:n], outs[n : 2 * n], outs[2 * n], outs[2 * n + 1 :]


UP_TILE = 256
DOWN_TILE = 512


def tile_copy(w_ref, row, rows, column, buffer, sems, t, tile):
    at = pl.ds(pl.multiple_of(t * tile, tile), tile)
    source = w_ref.at[pl.ds(row, rows), pl.ds(pl.multiple_of(column + t * tile, tile), tile)]
    return pltpu.make_async_copy(source, buffer.at[:, at], sems.at[t])


def up_kernel(x_ref, w_ref, *refs, masks, ahead):
    if ahead is None:
        out_ref, buffer, sems = refs
    else:
        down_ref, out_ref, next_ref, buffer, sems, next_sems = refs
    side = lax.axis_index("side")
    depth, width = buffer.shape[1:]
    tiles = width // UP_TILE

    def copy_of(n, t):
        column = pl.multiple_of(((side ^ masks[n][0]) * 2 + masks[n][1]) * width, width)
        return tile_copy(w_ref, 0, depth, column, buffer.at[n], sems.at[n], t, UP_TILE)

    for n in range(len(masks)):
        for t in range(tiles):
            copy_of(n, t).start()
    if ahead is not None:
        row = pl.multiple_of((side ^ ahead) * next_ref.shape[0], next_ref.shape[0])
        later = [
            tile_copy(down_ref, row, next_ref.shape[0], 0, next_ref, next_sems, t, DOWN_TILE)
            for t in range(next_ref.shape[1] // DOWN_TILE)
        ]
        for copy in later:
            copy.start()

    @pl.loop(0, len(masks) * tiles)
    def _(job):
        n, t = lax.div(job, tiles), lax.rem(job, tiles)
        at = pl.ds(pl.multiple_of(t * UP_TILE, UP_TILE), UP_TILE)
        pltpu.make_async_copy(
            w_ref.at[:, pl.ds(0, UP_TILE)], buffer.at[n, :, at], sems.at[n, t]
        ).wait()
        out_ref[n, :, at] = jnp.dot(
            x_ref[: out_ref.shape[1], :], buffer[n, :, at], preferred_element_type=f32
        ).astype(out_ref.dtype)

    if ahead is not None:
        for copy in later:
            copy.wait()


def up(packed, w_up, rows, width, masks, w_down=None, ahead=None):
    depth = w_up.shape[0]
    vmem, anywhere = pl.BlockSpec(memory_space=pltpu.VMEM), pl.BlockSpec(memory_space=pl.ANY)
    out = jax.ShapeDtypeStruct((len(masks), rows, width), bf16)
    scratch = [
        pltpu.VMEM((len(masks), depth, width), bf16),
        pltpu.SemaphoreType.DMA((len(masks), width // UP_TILE)),
    ]
    extra = ahead is not None
    if extra:
        out = [out, pltpu.VMEM((2 * width, w_down.shape[1]), bf16)]
        scratch.append(pltpu.SemaphoreType.DMA((w_down.shape[1] // DOWN_TILE,)))
    return pl.pallas_call(
        functools.partial(up_kernel, masks=masks, ahead=ahead),
        in_specs=[vmem, anywhere] + [anywhere] * extra,
        out_specs=[vmem, vmem] if extra else vmem,
        out_shape=out,
        scratch_shapes=scratch,
        compiler_params=params(24),
        cost_estimate=cost(2 * rows * depth * width, depth * width * 2 * len(masks)),
        name="up",
    )(packed, w_up, *([w_down] if extra else []))


PIECES = ((0, 2), (1, 3))


def find_layout(gathered, layout, step_ref, limits):
    side, shard = lax.axis_index("side"), lax.axis_index("shard")
    pieces = gathered[0].shape[0] // TALL
    devices = len(gathered) * pieces
    counts, places = [None] * devices, [None] * devices
    number = lax.broadcasted_iota(i32, (LIVE_CAP, HEAD), 0) + 1
    for part in range(len(gathered)):
        marks = gathered[part][:, :HEAD].astype(f32)
        for piece, mask in enumerate(PIECES[part % 2]):
            rows = marks[piece * TALL : piece * TALL + LIVE_CAP]
            last = jnp.where(rows < EMPTY / 2, number, 0).astype(f32)
            place = part // 2 * 4 + mask
            counts[place] = jnp.max(last).astype(i32)
            places[place] = (side ^ mask) * 4 + (shard ^ (part // 2))
    total = jnp.int32(0)
    for one in range(devices):
        base = jnp.int32(0)
        for other in range(devices):
            base = base + jnp.where(places[other] < places[one], counts[other], 0)
        layout[one] = base
        layout[devices + one] = counts[one]
        total = total + counts[one]
    step = jnp.int32(0)
    for limit in limits:
        step = step + (total > limit).astype(i32)
    step_ref[0] = step


def pack_up_kernel(*refs, mask, limits):
    gathered, refs = refs[:-7], refs[-7:]
    w_ref, packed_ref, out_ref, layout, step_ref, buffer, sems = refs
    width = out_ref.shape[1]

    def copy_of(t):
        column = pl.multiple_of((lax.axis_index("side") ^ mask) * 2 * width, width)
        return tile_copy(w_ref, 0, buffer.shape[0], column, buffer, sems, t, UP_TILE)

    for t in range(width // UP_TILE):
        copy_of(t).start()
    find_layout(gathered, layout, step_ref, limits)
    rows, depth = packed_ref.shape
    per = gathered[0].shape[0]
    pieces = per // TALL
    devices = len(gathered) * pieces
    shape = (8, len(gathered) * per)
    lane = lax.broadcasted_iota(i32, shape, 1)
    row = lax.broadcasted_iota(i32, (rows, shape[1]), 0)
    for half in range(2):
        target = jnp.full(shape, -1, i32)
        for part in range(len(gathered)):
            for piece, other in enumerate(PIECES[part % 2]):
                place = part // 2 * 4 + other
                base, count = layout[place], layout[devices + place]
                inside = lane - (part * per + piece * TALL + half * LIVE_CAP)
                mine = jnp.logical_and(inside >= 0, inside < count)
                target = jnp.where(mine, base + inside, target)
        pick = (target[:1] == row).astype(f32).astype(bf16)

        @pl.loop(0, depth // 2 // DOWN_TILE)
        def _(t):
            at = pl.ds(pl.multiple_of(t * DOWN_TILE, DOWN_TILE), DOWN_TILE)
            to = pl.ds(pl.multiple_of(half * (depth // 2) + t * DOWN_TILE, DOWN_TILE), DOWN_TILE)
            found = jnp.concatenate([part[:, at] for part in gathered], axis=0)
            packed_ref[:, to] = jnp.dot(pick, found, preferred_element_type=f32).astype(bf16)

    @pl.loop(0, width // UP_TILE)
    def _(t):
        copy_of(t).wait()
        at = pl.ds(pl.multiple_of(t * UP_TILE, UP_TILE), UP_TILE)
        out_ref[:, at] = jnp.dot(
            packed_ref[...], buffer[:, at], preferred_element_type=f32
        ).astype(bf16)


def pack_up(gathered, w_up, rows, width, mask, limits):
    depth = w_up.shape[0]
    devices = len(gathered) * gathered[0].shape[0] // TALL
    vmem, smem = pl.BlockSpec(memory_space=pltpu.VMEM), pl.BlockSpec(memory_space=pltpu.SMEM)
    return pl.pallas_call(
        functools.partial(pack_up_kernel, mask=mask, limits=limits),
        in_specs=[vmem] * len(gathered) + [pl.BlockSpec(memory_space=pl.ANY)],
        out_specs=[vmem, vmem, smem, smem],
        out_shape=[
            jax.ShapeDtypeStruct((rows, depth), bf16),
            jax.ShapeDtypeStruct((rows, width), bf16),
            jax.ShapeDtypeStruct((2 * devices,), i32),
            jax.ShapeDtypeStruct((1,), i32),
        ],
        scratch_shapes=[
            pltpu.VMEM((depth, width), bf16),
            pltpu.SemaphoreType.DMA((width // UP_TILE,)),
        ],
        compiler_params=params(24),
        cost_estimate=cost(2 * rows * depth * width, depth * width * 2),
        name="pack_up",
    )(*gathered, w_up)


def down_kernel(*refs, first, mask, ahead):
    refs = list(refs)
    a_ref, w_ref = refs.pop(0), refs.pop(0)
    before_ref = None if first else refs.pop(0)
    out_ref = refs.pop(0)
    next_ref = refs.pop(0) if ahead is not None else None
    buffer, sems = refs.pop(0), refs.pop(0)
    depth, width = buffer.shape
    tiles = width // DOWN_TILE

    def copy_of(other, buffer, sems, t):
        row = pl.multiple_of((lax.axis_index("side") ^ other) * depth, depth)
        return tile_copy(w_ref, row, depth, 0, buffer, sems, t, DOWN_TILE)

    for t in range(tiles):
        copy_of(mask, buffer, sems, t).start()
    if ahead is not None:
        for t in range(tiles):
            copy_of(ahead, next_ref, refs[0], t).start()

    @pl.loop(0, tiles)
    def _(t):
        at = pl.ds(pl.multiple_of(t * DOWN_TILE, DOWN_TILE), DOWN_TILE)
        copy_of(mask, buffer, sems, t).wait()
        part = jnp.dot(a_ref[...], buffer[:, at], preferred_element_type=f32)
        out_ref[:, at] = part if first else before_ref[:, at] + part

    if ahead is not None:

        @pl.loop(0, tiles)
        def _(t):
            copy_of(ahead, next_ref, refs[0], t).wait()


def down(active, w_down, before, mask, ahead=None):
    rows, depth = active.shape
    width = w_down.shape[1]
    vmem = pl.BlockSpec(memory_space=pltpu.VMEM)
    out = jax.ShapeDtypeStruct((rows, width), f32)
    sems = pltpu.SemaphoreType.DMA((width // DOWN_TILE,))
    return pl.pallas_call(
        functools.partial(down_kernel, first=before is None, mask=mask, ahead=ahead),
        in_specs=[vmem, pl.BlockSpec(memory_space=pl.ANY)]
        + ([] if before is None else [vmem]),
        out_specs=vmem if ahead is None else [vmem, vmem],
        out_shape=out if ahead is None else [out, pltpu.VMEM((depth, width), bf16)],
        scratch_shapes=[pltpu.VMEM((depth, width), bf16), sems]
        + ([] if ahead is None else [sems]),
        compiler_params=params(24),
        cost_estimate=cost(2 * rows * depth * width, depth * width * 2),
        name="down",
    )(active, w_down, *([] if before is None else [before]))


BACK = ((2, 3), (0, 1))


def back_picks_kernel(layout, out):
    _, devices, _, rows = out.shape
    row = lax.broadcasted_iota(i32, (PAD, rows), 0)
    column = lax.broadcasted_iota(i32, (PAD, rows), 1)
    late = jnp.where(row < 8, row, jnp.where(row < LIVE_CAP, LIVE_CAP, row - (PAD - LIVE_CAP)))
    device = 0
    for core in (0, 1):
        for x in (2, 0):
            for masks in BACK:
                for mask in masks:
                    place = (x + core) * 4 + mask
                    base, count = layout[place], layout[devices + place]
                    for parity, rank in enumerate((row, late)):
                        mine = jnp.logical_and(column - rank == base, rank < count)
                        out[parity, device] = mine.astype(f32).astype(bf16)
                    device += 1


def back_picks(layout, rows):
    devices = layout.shape[0] // 2
    return pl.pallas_call(
        back_picks_kernel,
        in_specs=[pl.BlockSpec(memory_space=pltpu.SMEM)],
        out_specs=pl.BlockSpec(memory_space=pltpu.VMEM),
        out_shape=jax.ShapeDtypeStruct((2, devices, PAD, rows), bf16),
        compiler_params=params(16),
        name="back_picks",
    )(layout)


def down_unpack_kernel(picks_ref, a_ref, w_ref, before_ref, *refs):
    outs, wide = refs[:-1], refs[-1]
    rows = a_ref.shape[0]
    tiles, devices = wide.shape[:2]
    group = devices // len(outs)

    @pl.loop(0, tiles)
    def _(t):
        at = pl.ds(pl.multiple_of(t * DOWN_TILE, DOWN_TILE), DOWN_TILE)
        share = before_ref[:, at] + jnp.dot(a_ref[...], w_ref[:, at], preferred_element_type=f32)
        pick = picks_ref[lax.rem(t, 2)].reshape(devices * PAD, rows)
        back = jnp.dot(pick, share.astype(bf16), preferred_element_type=f32)
        wide[t] = back.reshape(devices, PAD, DOWN_TILE)

    per = tiles * LIVE_CAP
    for n, out in enumerate(outs):

        @pl.loop(0, group)
        def _(device):
            here = [wide[t, n * group + device] for t in range(tiles)]
            late = [here[t][8:] + here[t + 1][8:] for t in range(0, tiles, 2)]
            rows = pl.ds(pl.multiple_of(device * per, per), per)
            out[rows, :] = jnp.concatenate([h[:8] for h in here] + late, axis=0).astype(bf16)


def down_unpack(picks, active, weights, before):
    rows, depth = active.shape
    width = weights.shape[1]
    tiles, devices = width // DOWN_TILE, picks.shape[1]
    vmem = pl.BlockSpec(memory_space=pltpu.VMEM)
    out = jax.ShapeDtypeStruct((devices // 2 * tiles * LIVE_CAP, DOWN_TILE), bf16)
    return pl.pallas_call(
        down_unpack_kernel,
        in_specs=[vmem] * 4,
        out_specs=[vmem] * 2,
        out_shape=[out] * 2,
        scratch_shapes=[pltpu.VMEM((tiles, devices, PAD, DOWN_TILE), f32)],
        compiler_params=params(24),
        cost_estimate=cost(2 * rows * depth * width, rows * width * 4),
        name="down_unpack",
    )(picks, active, weights, before)


def finish_kernel(picks_ref, *refs):
    side = lax.axis_index("side")
    out_ref = refs[-1]
    sides = (len(refs) - 3) // 2
    mixed, squares, blocks = refs[:sides], refs[sides : sides + 2], refs[sides + 2 : -1]
    slots, width = out_ref.shape
    step = width // sides
    total = squares[0][...] + squares[1][...]
    root = lax.rsqrt(jnp.sum(total, axis=-1, keepdims=True) / width + epsilon)
    gain = root * root
    tiles = step // DOWN_TILE
    for shift in range(sides):
        base = (side ^ shift) * step
        block = blocks[shift][...]
        for t in range(tiles):
            back = jnp.dot(picks_ref[t], block, preferred_element_type=f32)[:slots]
            at = pl.multiple_of(base + t * DOWN_TILE, DOWN_TILE)
            here = mixed[shift][:, t * DOWN_TILE : (t + 1) * DOWN_TILE]
            out_ref[:, pl.ds(at, DOWN_TILE)] = (here + gain * back).astype(bf16)


def finish(picks, mixed, squares, blocks):
    vmem = pl.BlockSpec(memory_space=pltpu.VMEM)
    slots, width = mixed[0].shape[0], mixed[0].shape[1] * len(mixed)
    return pl.pallas_call(
        finish_kernel,
        in_specs=[vmem] * (2 * len(mixed) + 3),
        out_specs=vmem,
        out_shape=jax.ShapeDtypeStruct((slots, width), bf16),
        compiler_params=params(16),
        cost_estimate=cost(slots * width * 32, slots * width * 8),
        name="finish",
    )(picks, *mixed, *squares, *blocks)


def swap(x, axis, count, mask):
    return lax.ppermute(x, axis, [(j, j ^ mask) for j in range(count)])


def added(a, b):
    return (a.astype(f32) + b.astype(f32)).astype(bf16)


def tie(x, *others):
    return lax.optimization_barrier((x, *others))[0]


def squared_relu(*terms):
    lifted = sum(term.astype(f32) for term in terms)
    clipped = jnp.maximum(lifted, 0.0)
    return (clipped * clipped).astype(bf16)


def feed_forward(rows, layout, packed, other, w_up, w_down):
    half = w_up.shape[1] // 8
    across = lambda x: swap(x, "side", 4, 2)
    beside = lambda x: swap(x, "side", 4, 1)
    met_0 = beside(other[:rows])
    far = up(packed, w_up, rows, half, ((3, 1), (2, 0), (2, 1)))
    met_1 = beside(far[0])
    sum_0 = added(far[1], met_0)
    crossed_0 = across(sum_0)
    near = up(tie(packed, sum_0), w_up, rows, half, ((1, 0), (1, 1)))
    met_1, near = lax.optimization_barrier((met_1, near))
    sum_1 = added(far[2], met_1)
    crossed_1 = across(sum_1)
    near = beside(near)
    own, weights = up(tie(packed, sum_1), w_up, rows, half, ((0, 0), (0, 1)), w_down, ahead=3)
    active = [squared_relu(own[n], near[n], crossed) for n, crossed in enumerate((crossed_0, crossed_1))]
    active = jnp.concatenate(active, axis=1)
    over, following = across(active), beside(active)
    total = down(active, w_down, None, 0)
    picks = back_picks(tie(layout, total), rows)
    forward = beside(tie(over, picks))
    total = down(following, w_down, total, 1)
    total = down(over, w_down, total, 2)
    return down_unpack(picks, forward, weights, total)


ROW_STEPS = (112, 120, 128, 136, 144, 160, 192)


def line_shards(
    queries, new_kv, kv_pool, page_table, ctx_len, residual_in, norm_gain, w_up, w_down
):
    in_hbm = lambda x: pltpu.with_memory_space_constraint(x, pltpu.HBM)
    gain = norm_gain.reshape(-1, HEAD)
    inputs = queries, new_kv, kv_pool, page_table, ctx_len, residual_in, gain
    inputs, w_up, w_down = jax.tree.map(in_hbm, (inputs, w_up, w_down))
    (to_2, to_3), mixed_far, squares_far, copies = attend(inputs, 4, (2, 3), None)
    *copies, back_picks = copies
    met = swap(jnp.concatenate([to_2, to_3], axis=0), "side", 4, 2)
    (own, to_1), mixed_near, squares_near, _ = attend(inputs, 4, (0, 1), copies)
    first = jnp.concatenate([own, met[:TALL]], axis=0)
    second = swap(jnp.concatenate([to_1, met[TALL:]], axis=0), "side", 4, 1)
    gathered = []
    by_x = [swap(here, "shard", 4, 2) for here in (first, second)]
    by_core = [swap(here, "shard", 4, 1) for here in (first, second)]
    by_both = [swap(there, "shard", 4, 1) for there in by_x]
    gathered = [first, second, *by_core, *by_x, *by_both]
    packed, other, layout, step = pack_up(
        gathered, w_up, ROW_STEPS[-1], w_up.shape[1] // 8, 3, ROW_STEPS[:-1]
    )
    stay, leave = lax.switch(
        step[0],
        [functools.partial(feed_forward, rows) for rows in ROW_STEPS],
        layout, packed, other, w_up, w_down,
    )
    back = swap(leave, "shard", 4, 1)
    quarter = back.shape[0] // 4
    piece = quarter // 2
    cuts = [slice(at, at + quarter) for at in range(0, 4 * quarter, quarter)]
    sums = [added(stay[cut], back[cut]) for cut in cuts]
    far = added(sums[2], swap(sums[0], "shard", 4, 2))
    near = added(sums[3], swap(sums[1], "shard", 4, 2))
    home = near[:piece], near[piece:], far[:piece], far[piece:]
    blocks = [home[0]] + [swap(home[mask], "side", 4, mask) for mask in (1, 2, 3)]
    mixed = [*mixed_near, *mixed_far]
    return finish(back_picks, mixed, [squares_far, squares_near], blocks)


def attend_slots(queries, new_kv, pool_pages, page_rows, lengths):
    slot_count = queries.shape[0]
    positions = page_rows.shape[1] * pool_pages.shape[1]
    fetched = pool_pages[page_rows].reshape(slot_count, positions, 2, KV_HEADS, HEAD)
    fresh_kv = new_kv.reshape(slot_count, 2, KV_HEADS, HEAD)
    query_heads = queries.reshape(slot_count, KV_HEADS, GROUP, HEAD)
    score_scale = 1.0 / math.sqrt(HEAD)
    scores = (
        jnp.einsum("sgqd,slgd->sgql", query_heads, fetched[:, :, 0], preferred_element_type=f32)
        * score_scale
    )
    own_score = (
        jnp.einsum("sgqd,sgd->sgq", query_heads, fresh_kv[:, 0], preferred_element_type=f32)
        * score_scale
    )
    visible = (jnp.arange(positions, dtype=i32)[None, :] < lengths[:, None])[:, None, None, :]
    scores = jnp.where(visible, scores, -1e30)
    highest = jnp.maximum(jnp.max(scores, axis=-1), own_score)
    weights = jnp.where(visible, jnp.exp(scores - highest[..., None]), 0.0)
    own_weight = jnp.exp(own_score - highest)
    denominator = jnp.sum(weights, axis=-1) + own_weight
    probabilities = (weights / denominator[..., None]).astype(bf16)
    own_prob = (own_weight / denominator).astype(bf16).astype(f32)
    attended = jnp.einsum(
        "sgql,slgd->sgqd", probabilities, fetched[:, :, 1], preferred_element_type=f32
    )
    attended = attended + own_prob[..., None] * fresh_kv[:, 1].astype(f32)[:, :, None, :]
    return attended.reshape(slot_count, -1)


def any_shards(queries, new_kv, kv_pool, page_table, ctx_len, residual_in, norm_gain, w_up, w_down):
    attended = attend_slots(queries, new_kv, kv_pool, page_table, ctx_len)
    mixed_rows = residual_in.astype(f32) + attended
    mean_square = jnp.mean(mixed_rows * mixed_rows, axis=-1, keepdims=True)
    normed = (mixed_rows * lax.rsqrt(mean_square + epsilon) * norm_gain.astype(f32)).astype(bf16)
    live_mask = ctx_len > 0
    spread = lax.all_to_all(normed, "side", split_axis=1, concat_axis=0, tiled=True)
    up_partial = jnp.dot(
        lax.all_gather(spread, "shard", axis=0, tiled=True), w_up, preferred_element_type=f32
    )
    lifted = lax.psum(up_partial, "side")
    clipped = jnp.maximum(lifted, 0.0)
    active = (clipped * clipped).astype(bf16)
    down_share = lax.psum_scatter(
        jnp.dot(active, w_down, preferred_element_type=f32).astype(bf16),
        "shard",
        scatter_dimension=0,
        tiled=True,
    )
    returned = lax.all_to_all(down_share, "side", split_axis=0, concat_axis=1, tiled=True)
    returned = jnp.where(live_mask[:, None], returned.astype(f32), 0.0)
    return (mixed_rows + returned).astype(bf16)


def solution(mesh):
    rows = ("grp", "side", "shard")
    placed = (
        P(rows, None),
        P(rows, None),
        P(rows, None, None),
        P(rows, None),
        P(rows),
        P(rows, None),
        P(),
        P("side", "shard"),
        P("shard", "side"),
    )
    square = mesh.shape["side"] == 4 and mesh.shape["shard"] == 4
    return jax.shard_map(
        line_shards if square else any_shards,
        mesh=mesh,
        in_specs=placed,
        out_specs=P(rows, None),
        check_vma=False,
    )
```

```python
import functools
import math

import jax
import jax.numpy as jnp
from jax import lax
from jax.experimental import pallas as pl
from jax.experimental.pallas import tpu as pltpu
from jax.sharding import PartitionSpec as P

KV_HEADS = 8
HEAD = 128
GROUP = 8
LIVE_CAP = 12
PAD = 16
TALL = 2 * LIVE_CAP
EMPTY = 1e30

epsilon = 1e-05
bf16, f32, i32 = jnp.bfloat16, jnp.float32, jnp.int32
VMEM_MB = 1 << 20


def params(mb, **more):
    return pltpu.CompilerParams(vmem_limit_bytes=mb * VMEM_MB, **more)


def cost(flops, bytes_accessed):
    return pl.CostEstimate(
        flops=int(flops) // 64, bytes_accessed=int(bytes_accessed) // 64, transcendentals=0
    )


def pad_rows(x):
    rows = x.shape[0]
    if rows == PAD:
        return x
    return jnp.concatenate([x, jnp.zeros((PAD - rows,) + x.shape[1:], x.dtype)], axis=0)


def live_ranks(lengths, slots):
    live, rank, count = [], [], jnp.int32(0)
    for slot in range(slots):
        alive = lengths[slot] > 0
        live.append(alive)
        rank.append(count)
        count = count + alive.astype(i32)
    return live, rank


def token_bias(lengths, table, pages, page):
    slots, entries = table.shape
    tokens = pages * page
    lanes = 128 * ((pages + 127) // 128)
    row = lax.broadcasted_iota(i32, (PAD, lanes), 0)
    column = lax.broadcasted_iota(i32, (PAD, lanes), 1)
    reach = jnp.zeros((PAD, lanes), i32)
    for slot in range(slots):
        reach = jnp.where(row == slot, lengths[slot], reach)
    table = pad_rows(table)
    seen = jnp.zeros((PAD, lanes), i32)
    for entry in range(entries):
        here = jnp.minimum(jnp.maximum(reach - entry * page, 0), page)
        seen = seen + jnp.where(table[:, entry : entry + 1] == column, here, 0)
    spread = (
        lax.broadcasted_iota(i32, (lanes, tokens), 1) // page
        == lax.broadcasted_iota(i32, (lanes, tokens), 0)
    )
    seen_tokens = jnp.dot(
        seen.astype(f32).astype(bf16), spread.astype(f32).astype(bf16), preferred_element_type=f32
    )
    place = (lax.broadcasted_iota(i32, (PAD, tokens), 1) % page).astype(f32)
    return jnp.where(place < seen_tokens, 0.0, -1e30)


def live_pick(lengths, of_rank, of_slot, slots):
    live, rank = live_ranks(lengths, slots)
    pick = jnp.zeros(of_rank.shape, f32)
    for slot in range(slots):
        chosen = jnp.logical_and(of_rank == rank[slot], of_slot == slot)
        pick = jnp.where(jnp.logical_and(chosen, live[slot]), 1.0, pick)
    return pick.astype(bf16), rank[-1] + live[-1].astype(i32)


def back_rank(row, t, tiles):
    first, last = row - 8 * t, row - 8 * tiles - (LIVE_CAP - 8) * t
    rest = jnp.where(jnp.logical_and(last >= 0, last < LIVE_CAP - 8), last + 8, -1)
    return jnp.where(jnp.logical_and(first >= 0, first < 8), first, rest)


POOL_CUTS = 4


def attend_kernel(*refs, masks, sides, first):
    side = lax.axis_index("side")
    refs = list(refs)
    take = lambda n: [refs.pop(0) for _ in range(n)]
    if first:
        lengths, table_ref = take(2)
        sources = take(4)
    else:
        q_ref, new_ref, res_ref, gain_ref, bias_ref, picks_ref, empty_ref = take(7)
    pool_source = refs.pop(0)
    w_ref = None if first else refs.pop(0)
    sends, mixed_refs = take(len(masks)), take(len(masks))
    square_ref = refs.pop(0)
    weights_ref = None if first else refs.pop(0)
    if first:
        q_ref, new_ref, res_ref, gain_ref, bias_ref, picks_ref, empty_ref, back_ref = take(8)
        gain_copy, sems = take(2)
    pool_ref, pool_sems = take(2)
    fetched = []
    if not first:
        rows, across = weights_ref.shape
        column = pl.multiple_of((side ^ FIRST_BLOCK) * 2 * across, across)
        for t in range(across // UP_TILE):
            fetched.append(tile_copy(w_ref, 0, rows, column, weights_ref, refs[0], t, UP_TILE))
    slots, step = mixed_refs[0].shape
    pages, page, width = pool_source.shape
    columns = width // 2 // sides
    heads = columns // HEAD
    tokens = pages * page
    scale = math.log2(math.e) / math.sqrt(HEAD)

    if first:
        small = [
            pltpu.make_async_copy(source, target, sems.at[n])
            for n, (source, target) in enumerate(
                zip(sources, (q_ref, new_ref, res_ref, gain_copy), strict=True)
            )
        ]
        for copy in small:
            copy.start()
    cut, half, pair = pages // POOL_CUTS, width // 2, columns * 2
    here = lax.div(side ^ masks[0], 2) * pair
    brought = []
    for n, at in enumerate((here, half + here)):
        columns_at = pl.ds(pl.multiple_of(at, pair), pair)
        target_at = pl.ds(n * pair, pair)
        brought.append([])
        for c in range(POOL_CUTS):
            rows = pl.ds(c * cut, cut)
            copy = pltpu.make_async_copy(
                pool_source.at[rows, :, columns_at], pool_ref.at[rows, :, target_at], pool_sems.at[n, c]
            )
            copy.start()
            brought[n].append(copy)
    if first:
        bias_ref[...] = token_bias(lengths, table_ref[...], pages, page)
        rank, slot = (lax.broadcasted_iota(i32, (TALL, PAD), n) for n in range(2))
        for head in range(heads):
            picks_ref[head], count = live_pick(lengths, rank - head * LIVE_CAP, slot, slots)
        rank = lax.broadcasted_iota(i32, empty_ref.shape, 0)
        rank = jnp.where(rank < LIVE_CAP, rank, rank - LIVE_CAP)
        empty_ref[...] = (rank >= count).astype(f32)
        slot, row = (lax.broadcasted_iota(i32, back_ref.shape[1:], n) for n in range(2))
        for t in range(back_ref.shape[0]):
            rank = back_rank(row, t, back_ref.shape[0])
            back_ref[t] = live_pick(lengths, rank, slot, slots)[0]
        for copy in small:
            copy.wait()
        gain_ref[...] = gain_copy[...].astype(f32)
    for copy in brought[0]:
        copy.wait()
    values_to_come = brought[1]
    for copy in fetched:
        copy.start()

    squares = jnp.zeros((slots, HEAD), f32)
    bias = bias_ref[...][None]
    jobs = [(n, head) for n in range(len(masks)) for head in range(heads)]

    def places(job):
        block, base = side ^ masks[job[0]], job[1] * GROUP * HEAD
        new_at = pl.multiple_of(block * columns, columns) + job[1] * HEAD
        key_at = pl.multiple_of(lax.rem(block, 2) * columns, columns) + job[1] * HEAD
        return block, base, pl.multiple_of(block * step, step) + base, new_at, key_at

    def score(job):
        _, _, start, new_at, key_at = places(job)
        q = jnp.concatenate(
            [pad_rows(q_ref[:, pl.ds(start + g * HEAD, HEAD)]) for g in range(GROUP)], axis=0
        )
        keys = pool_ref[:, :, pl.ds(key_at, HEAD)].reshape(tokens, HEAD)
        new_key = pad_rows(new_ref[:, pl.ds(new_at, HEAD)]).astype(f32)
        scores = lax.dot_general(q, keys, (((1,), (1,)), ((), ())), preferred_element_type=f32)
        own = jnp.sum(
            q.astype(f32).reshape(GROUP, PAD, HEAD) * new_key[None], axis=-1, keepdims=True
        )
        return scores.reshape(GROUP, PAD, tokens), own * scale

    ready = score(jobs[0])
    for number, job in enumerate(jobs):
        block, base, start, new_at, key_at = places(job)
        scores, own = ready
        if number + 1 < len(jobs):
            ready = score(jobs[number + 1])
        scores = scores * scale + bias
        highest = jnp.maximum(jnp.max(scores, axis=-1, keepdims=True), own)
        weights = jnp.exp2(scores - highest)
        own_weight = jnp.exp2(own - highest)
        total = jnp.sum(weights, axis=-1, keepdims=True) + own_weight
        for copy in values_to_come:
            copy.wait()
        values_to_come = []
        values = pool_ref[:, :, pl.ds(pair + key_at, HEAD)].reshape(tokens, HEAD)
        new_value = pad_rows(new_ref[:, pl.ds(half + new_at, HEAD)]).astype(f32)
        summed = jnp.dot(
            weights.astype(bf16).reshape(GROUP * PAD, tokens), values, preferred_element_type=f32
        ).reshape(GROUP, PAD, HEAD)
        attended = (summed + own_weight * new_value[None]) / total
        for g in range(GROUP):
            at = slice(base + g * HEAD, base + (g + 1) * HEAD)
            residual = res_ref[:, pl.ds(start + g * HEAD, HEAD)].astype(f32)
            mixed = residual + attended[g][:slots]
            mixed_refs[job[0]][:, at] = mixed
            squares = squares + mixed * mixed
            gain = gain_ref[pl.ds(block * (step // HEAD) + job[1] * GROUP + g, 1), :]
            gained = pad_rows((mixed * gain).astype(bf16))
            rows = jnp.dot(picks_ref[job[1]], gained, preferred_element_type=f32)
            to = slice(g * HEAD, (g + 1) * HEAD)
            if job[1]:
                rows = rows + sends[job[0]][:, to].astype(f32)
                rows = jnp.where(empty_ref[...] > 0, EMPTY, rows)
            sends[job[0]][:, to] = rows.astype(bf16)
    square_ref[...] = squares
    for copy in fetched:
        copy.wait()


FIRST_BLOCK = 3


def attend(inputs, sides, masks, before, w_up):
    queries, new_kv, kv_pool, page_table, ctx_len, residual_in, norm_gain = inputs
    slots, columns = queries.shape
    pages, page, _ = kv_pool.shape
    step = columns // sides
    first = before is None
    vmem, anywhere = pl.BlockSpec(memory_space=pltpu.VMEM), pl.BlockSpec(memory_space=pl.ANY)
    smem = pl.BlockSpec(memory_space=pltpu.SMEM)
    out_shape = [jax.ShapeDtypeStruct((TALL, step // 2), bf16)] * len(masks)
    out_shape += [jax.ShapeDtypeStruct((slots, step), f32)] * len(masks)
    out_shape += [jax.ShapeDtypeStruct((slots, HEAD), f32)]
    if first:
        operands = [ctx_len, page_table, queries, new_kv, residual_in, norm_gain, kv_pool]
        in_specs = [smem, vmem] + [anywhere] * 5
        tiles = step // DOWN_TILE
        out_shape += [
            pltpu.VMEM(queries.shape, bf16),
            pltpu.VMEM(new_kv.shape, bf16),
            pltpu.VMEM(residual_in.shape, bf16),
            pltpu.VMEM(norm_gain.shape, f32),
            pltpu.VMEM((PAD, pages * page), f32),
            pltpu.VMEM((columns // HEAD // GROUP // sides, TALL, PAD), bf16),
            pltpu.VMEM((TALL, HEAD), f32),
            pltpu.VMEM((tiles, PAD, tiles * LIVE_CAP), bf16),
        ]
        scratch = [pltpu.VMEM(norm_gain.shape, bf16), pltpu.SemaphoreType.DMA((4,))]
    else:
        operands = [*before, kv_pool, w_up]
        in_specs = [vmem] * len(before) + [anywhere] * 2
        half = w_up.shape[1] // 8
        out_shape.append(pltpu.VMEM((w_up.shape[0], half), bf16))
        scratch = []
    scratch += [
        pltpu.VMEM((pages, page, kv_pool.shape[2] // sides * 2), bf16),
        pltpu.SemaphoreType.DMA((2, POOL_CUTS)),
    ]
    if not first:
        scratch.append(pltpu.SemaphoreType.DMA((half // UP_TILE,)))
    outs = pl.pallas_call(
        functools.partial(attend_kernel, masks=masks, sides=sides, first=first),
        in_specs=in_specs,
        out_specs=[vmem] * len(out_shape),
        out_shape=out_shape,
        scratch_shapes=scratch,
        compiler_params=params(28),
        cost_estimate=cost(2e9, kv_pool.size),
        name="attend",
    )(*operands)
    n = len(masks)
    return outs[:n], outs[n : 2 * n], outs[2 * n], outs[2 * n + 1 :]


UP_TILE = 256
DOWN_TILE = 512


def tile_copy(w_ref, row, rows, column, buffer, sems, t, tile):
    at = pl.ds(pl.multiple_of(t * tile, tile), tile)
    source = w_ref.at[pl.ds(row, rows), pl.ds(pl.multiple_of(column + t * tile, tile), tile)]
    return pltpu.make_async_copy(source, buffer.at[:, at], sems.at[t])


def up_kernel(x_ref, w_ref, *refs, masks, ahead):
    if ahead is None:
        out_ref, buffer, sems = refs
    else:
        down_ref, out_ref, next_ref, buffer, sems, next_sems = refs
    side = lax.axis_index("side")
    depth, width = buffer.shape[1:]
    tiles = width // UP_TILE

    def copy_of(n, t):
        column = pl.multiple_of(((side ^ masks[n][0]) * 2 + masks[n][1]) * width, width)
        return tile_copy(w_ref, 0, depth, column, buffer.at[n], sems.at[n], t, UP_TILE)

    for n in range(len(masks)):
        for t in range(tiles):
            copy_of(n, t).start()
    if ahead is not None:
        row = pl.multiple_of((side ^ ahead) * next_ref.shape[0], next_ref.shape[0])
        later = [
            tile_copy(down_ref, row, next_ref.shape[0], 0, next_ref, next_sems, t, DOWN_TILE)
            for t in range(next_ref.shape[1] // DOWN_TILE)
        ]
        for copy in later:
            copy.start()

    @pl.loop(0, len(masks) * tiles)
    def _(job):
        n, t = lax.div(job, tiles), lax.rem(job, tiles)
        at = pl.ds(pl.multiple_of(t * UP_TILE, UP_TILE), UP_TILE)
        pltpu.make_async_copy(
            w_ref.at[:, pl.ds(0, UP_TILE)], buffer.at[n, :, at], sems.at[n, t]
        ).wait()
        out_ref[n, :, at] = jnp.dot(
            x_ref[: out_ref.shape[1], :], buffer[n, :, at], preferred_element_type=f32
        ).astype(out_ref.dtype)

    if ahead is not None:
        for copy in later:
            copy.wait()


def up(packed, w_up, rows, width, masks, w_down=None, ahead=None):
    depth = w_up.shape[0]
    vmem, anywhere = pl.BlockSpec(memory_space=pltpu.VMEM), pl.BlockSpec(memory_space=pl.ANY)
    out = jax.ShapeDtypeStruct((len(masks), rows, width), bf16)
    scratch = [
        pltpu.VMEM((len(masks), depth, width), bf16),
        pltpu.SemaphoreType.DMA((len(masks), width // UP_TILE)),
    ]
    extra = ahead is not None
    if extra:
        out = [out, pltpu.VMEM((2 * width, w_down.shape[1]), bf16)]
        scratch.append(pltpu.SemaphoreType.DMA((w_down.shape[1] // DOWN_TILE,)))
    return pl.pallas_call(
        functools.partial(up_kernel, masks=masks, ahead=ahead),
        in_specs=[vmem, anywhere] + [anywhere] * extra,
        out_specs=[vmem, vmem] if extra else vmem,
        out_shape=out,
        scratch_shapes=scratch,
        compiler_params=params(24),
        cost_estimate=cost(2 * rows * depth * width, depth * width * 2 * len(masks)),
        name="up",
    )(packed, w_up, *([w_down] if extra else []))


PIECES = ((0, 2), (1, 3))


def find_layout(gathered, layout, step_ref, limits):
    side, shard = lax.axis_index("side"), lax.axis_index("shard")
    pieces = gathered[0].shape[0] // TALL
    devices = len(gathered) * pieces
    counts, places = [None] * devices, [None] * devices
    number = lax.broadcasted_iota(i32, (LIVE_CAP, HEAD), 0) + 1
    for part in range(len(gathered)):
        marks = gathered[part][:, :HEAD].astype(f32)
        for piece, mask in enumerate(PIECES[part % 2]):
            rows = marks[piece * TALL : piece * TALL + LIVE_CAP]
            last = jnp.where(rows < EMPTY / 2, number, 0).astype(f32)
            place = part // 2 * 4 + mask
            counts[place] = jnp.max(last).astype(i32)
            places[place] = (side ^ mask) * 4 + (shard ^ (part // 2))
    total = jnp.int32(0)
    for one in range(devices):
        base = jnp.int32(0)
        for other in range(devices):
            base = base + jnp.where(places[other] < places[one], counts[other], 0)
        layout[one] = base
        layout[devices + one] = counts[one]
        total = total + counts[one]
    step = jnp.int32(0)
    for limit in limits:
        step = step + (total > limit).astype(i32)
    step_ref[0] = step


def pack_up_kernel(*refs, limits):
    gathered, (w_ref, packed_ref, out_ref, layout, step_ref) = refs[:-5], refs[-5:]
    width = out_ref.shape[1]
    find_layout(gathered, layout, step_ref, limits)
    rows, depth = packed_ref.shape
    per = gathered[0].shape[0]
    pieces = per // TALL
    devices = len(gathered) * pieces
    shape = (8, len(gathered) * per)
    lane = lax.broadcasted_iota(i32, shape, 1)
    row = lax.broadcasted_iota(i32, (rows, shape[1]), 0)
    for half in range(2):
        target = jnp.full(shape, -1, i32)
        for part in range(len(gathered)):
            for piece, other in enumerate(PIECES[part % 2]):
                place = part // 2 * 4 + other
                base, count = layout[place], layout[devices + place]
                inside = lane - (part * per + piece * TALL + half * LIVE_CAP)
                mine = jnp.logical_and(inside >= 0, inside < count)
                target = jnp.where(mine, base + inside, target)
        pick = (target[:1] == row).astype(f32).astype(bf16)

        @pl.loop(0, depth // 2 // DOWN_TILE)
        def _(t):
            at = pl.ds(pl.multiple_of(t * DOWN_TILE, DOWN_TILE), DOWN_TILE)
            to = pl.ds(pl.multiple_of(half * (depth // 2) + t * DOWN_TILE, DOWN_TILE), DOWN_TILE)
            found = jnp.concatenate([part[:, at] for part in gathered], axis=0)
            packed_ref[:, to] = jnp.dot(pick, found, preferred_element_type=f32).astype(bf16)

    @pl.loop(0, width // UP_TILE)
    def _(t):
        at = pl.ds(pl.multiple_of(t * UP_TILE, UP_TILE), UP_TILE)
        out_ref[:, at] = jnp.dot(
            packed_ref[...], w_ref[:, at], preferred_element_type=f32
        ).astype(bf16)


def pack_up(gathered, weights, rows, limits):
    depth, width = weights.shape
    devices = len(gathered) * gathered[0].shape[0] // TALL
    vmem, smem = pl.BlockSpec(memory_space=pltpu.VMEM), pl.BlockSpec(memory_space=pltpu.SMEM)
    return pl.pallas_call(
        functools.partial(pack_up_kernel, limits=limits),
        in_specs=[vmem] * (len(gathered) + 1),
        out_specs=[vmem, vmem, smem, smem],
        out_shape=[
            jax.ShapeDtypeStruct((rows, depth), bf16),
            jax.ShapeDtypeStruct((rows, width), bf16),
            jax.ShapeDtypeStruct((2 * devices,), i32),
            jax.ShapeDtypeStruct((1,), i32),
        ],
        compiler_params=params(24),
        cost_estimate=cost(2 * rows * depth * width, depth * width * 2),
        name="pack_up",
    )(*gathered, weights)


def down_kernel(*refs, first, mask, ahead):
    refs = list(refs)
    a_ref, w_ref = refs.pop(0), refs.pop(0)
    before_ref = None if first else refs.pop(0)
    out_ref = refs.pop(0)
    next_ref = refs.pop(0) if ahead is not None else None
    buffer, sems = refs.pop(0), refs.pop(0)
    depth, width = buffer.shape
    tiles = width // DOWN_TILE

    def copy_of(other, buffer, sems, t):
        row = pl.multiple_of((lax.axis_index("side") ^ other) * depth, depth)
        return tile_copy(w_ref, row, depth, 0, buffer, sems, t, DOWN_TILE)

    for t in range(tiles):
        copy_of(mask, buffer, sems, t).start()
    if ahead is not None:
        for t in range(tiles):
            copy_of(ahead, next_ref, refs[0], t).start()

    @pl.loop(0, tiles)
    def _(t):
        at = pl.ds(pl.multiple_of(t * DOWN_TILE, DOWN_TILE), DOWN_TILE)
        copy_of(mask, buffer, sems, t).wait()
        part = jnp.dot(a_ref[...], buffer[:, at], preferred_element_type=f32)
        out_ref[:, at] = part if first else before_ref[:, at] + part

    if ahead is not None:

        @pl.loop(0, tiles)
        def _(t):
            copy_of(ahead, next_ref, refs[0], t).wait()


def down(active, w_down, before, mask, ahead=None):
    rows, depth = active.shape
    width = w_down.shape[1]
    vmem = pl.BlockSpec(memory_space=pltpu.VMEM)
    out = jax.ShapeDtypeStruct((rows, width), f32)
    sems = pltpu.SemaphoreType.DMA((width // DOWN_TILE,))
    return pl.pallas_call(
        functools.partial(down_kernel, first=before is None, mask=mask, ahead=ahead),
        in_specs=[vmem, pl.BlockSpec(memory_space=pl.ANY)]
        + ([] if before is None else [vmem]),
        out_specs=vmem if ahead is None else [vmem, vmem],
        out_shape=out if ahead is None else [out, pltpu.VMEM((depth, width), bf16)],
        scratch_shapes=[pltpu.VMEM((depth, width), bf16), sems]
        + ([] if ahead is None else [sems]),
        compiler_params=params(24),
        cost_estimate=cost(2 * rows * depth * width, depth * width * 2),
        name="down",
    )(active, w_down, *([] if before is None else [before]))


BACK = ((2, 3), (0, 1))


def back_picks_kernel(layout, out):
    _, devices, _, rows = out.shape
    row = lax.broadcasted_iota(i32, (PAD, rows), 0)
    column = lax.broadcasted_iota(i32, (PAD, rows), 1)
    late = jnp.where(row < 8, row, jnp.where(row < LIVE_CAP, LIVE_CAP, row - (PAD - LIVE_CAP)))
    device = 0
    for core in (0, 1):
        for x in (2, 0):
            for masks in BACK:
                for mask in masks:
                    place = (x + core) * 4 + mask
                    base, count = layout[place], layout[devices + place]
                    for parity, rank in enumerate((row, late)):
                        mine = jnp.logical_and(column - rank == base, rank < count)
                        out[parity, device] = mine.astype(f32).astype(bf16)
                    device += 1


def back_picks(layout, rows):
    devices = layout.shape[0] // 2
    return pl.pallas_call(
        back_picks_kernel,
        in_specs=[pl.BlockSpec(memory_space=pltpu.SMEM)],
        out_specs=pl.BlockSpec(memory_space=pltpu.VMEM),
        out_shape=jax.ShapeDtypeStruct((2, devices, PAD, rows), bf16),
        compiler_params=params(16),
        name="back_picks",
    )(layout)


def down_unpack_kernel(picks_ref, a_ref, w_ref, before_ref, *refs):
    outs, wide = refs[:-1], refs[-1]
    rows = a_ref.shape[0]
    tiles, devices = wide.shape[:2]
    group = devices // len(outs)

    @pl.loop(0, tiles)
    def _(t):
        at = pl.ds(pl.multiple_of(t * DOWN_TILE, DOWN_TILE), DOWN_TILE)
        share = before_ref[:, at] + jnp.dot(a_ref[...], w_ref[:, at], preferred_element_type=f32)
        pick = picks_ref[lax.rem(t, 2)].reshape(devices * PAD, rows)
        back = jnp.dot(pick, share.astype(bf16), preferred_element_type=f32)
        wide[t] = back.reshape(devices, PAD, DOWN_TILE)

    per = tiles * LIVE_CAP
    for n, out in enumerate(outs):

        @pl.loop(0, group)
        def _(device):
            here = [wide[t, n * group + device] for t in range(tiles)]
            late = [here[t][8:] + here[t + 1][8:] for t in range(0, tiles, 2)]
            rows = pl.ds(pl.multiple_of(device * per, per), per)
            out[rows, :] = jnp.concatenate([h[:8] for h in here] + late, axis=0).astype(bf16)


def down_unpack(picks, active, weights, before):
    rows, depth = active.shape
    width = weights.shape[1]
    tiles, devices = width // DOWN_TILE, picks.shape[1]
    vmem = pl.BlockSpec(memory_space=pltpu.VMEM)
    out = jax.ShapeDtypeStruct((devices // 2 * tiles * LIVE_CAP, DOWN_TILE), bf16)
    return pl.pallas_call(
        down_unpack_kernel,
        in_specs=[vmem] * 4,
        out_specs=[vmem] * 2,
        out_shape=[out] * 2,
        scratch_shapes=[pltpu.VMEM((tiles, devices, PAD, DOWN_TILE), f32)],
        compiler_params=params(24),
        cost_estimate=cost(2 * rows * depth * width, rows * width * 4),
        name="down_unpack",
    )(picks, active, weights, before)


def finish_kernel(picks_ref, *refs):
    side = lax.axis_index("side")
    out_ref = refs[-1]
    sides = (len(refs) - 3) // 2
    mixed, squares, blocks = refs[:sides], refs[sides : sides + 2], refs[sides + 2 : -1]
    slots, width = out_ref.shape
    step = width // sides
    total = squares[0][...] + squares[1][...]
    root = lax.rsqrt(jnp.sum(total, axis=-1, keepdims=True) / width + epsilon)
    gain = root * root
    tiles = step // DOWN_TILE
    for shift in range(sides):
        base = (side ^ shift) * step
        block = blocks[shift][...]
        for t in range(tiles):
            back = jnp.dot(picks_ref[t], block, preferred_element_type=f32)[:slots]
            at = pl.multiple_of(base + t * DOWN_TILE, DOWN_TILE)
            here = mixed[shift][:, t * DOWN_TILE : (t + 1) * DOWN_TILE]
            out_ref[:, pl.ds(at, DOWN_TILE)] = (here + gain * back).astype(bf16)


def finish(picks, mixed, squares, blocks):
    vmem = pl.BlockSpec(memory_space=pltpu.VMEM)
    slots, width = mixed[0].shape[0], mixed[0].shape[1] * len(mixed)
    return pl.pallas_call(
        finish_kernel,
        in_specs=[vmem] * (2 * len(mixed) + 3),
        out_specs=vmem,
        out_shape=jax.ShapeDtypeStruct((slots, width), bf16),
        compiler_params=params(16),
        cost_estimate=cost(slots * width * 32, slots * width * 8),
        name="finish",
    )(picks, *mixed, *squares, *blocks)


def swap(x, axis, count, mask):
    return lax.ppermute(x, axis, [(j, j ^ mask) for j in range(count)])


def added(a, b):
    return (a.astype(f32) + b.astype(f32)).astype(bf16)


def tie(x, *others):
    return lax.optimization_barrier((x, *others))[0]


def squared_relu(*terms):
    lifted = sum(term.astype(f32) for term in terms)
    clipped = jnp.maximum(lifted, 0.0)
    return (clipped * clipped).astype(bf16)


def feed_forward(rows, layout, packed, other, w_up, w_down):
    half = w_up.shape[1] // 8
    across = lambda x: swap(x, "side", 4, 2)
    beside = lambda x: swap(x, "side", 4, 1)
    met_0 = beside(other[:rows])
    far = up(packed, w_up, rows, half, ((3, 1), (2, 0), (2, 1)))
    met_1 = beside(far[0])
    sum_0 = added(far[1], met_0)
    crossed_0 = across(sum_0)
    near = up(tie(packed, sum_0), w_up, rows, half, ((1, 0), (1, 1)))
    met_1, near = lax.optimization_barrier((met_1, near))
    sum_1 = added(far[2], met_1)
    crossed_1 = across(sum_1)
    near = beside(near)
    own, weights = up(tie(packed, sum_1), w_up, rows, half, ((0, 0), (0, 1)), w_down, ahead=3)
    active = [squared_relu(own[n], near[n], crossed) for n, crossed in enumerate((crossed_0, crossed_1))]
    active = jnp.concatenate(active, axis=1)
    over, following = across(active), beside(active)
    total = down(active, w_down, None, 0)
    picks = back_picks(tie(layout, total), rows)
    forward = beside(tie(over, picks))
    total = down(following, w_down, total, 1)
    total = down(over, w_down, total, 2)
    return down_unpack(picks, forward, weights, total)


ROW_STEPS = (112, 120, 128, 136, 144, 160, 192)


def line_shards(
    queries, new_kv, kv_pool, page_table, ctx_len, residual_in, norm_gain, w_up, w_down
):
    in_hbm = lambda x: pltpu.with_memory_space_constraint(x, pltpu.HBM)
    gain = norm_gain.reshape(-1, HEAD)
    inputs = queries, new_kv, kv_pool, page_table, ctx_len, residual_in, gain
    inputs, w_up, w_down = jax.tree.map(in_hbm, (inputs, w_up, w_down))
    (to_2, to_3), mixed_far, squares_far, copies = attend(inputs, 4, (2, 3), None, w_up)
    *copies, back_picks = copies
    met = swap(jnp.concatenate([to_2, to_3], axis=0), "side", 4, 2)
    (own, to_1), mixed_near, squares_near, (weights,) = attend(inputs, 4, (0, 1), copies, w_up)
    first = jnp.concatenate([own, met[:TALL]], axis=0)
    second = swap(jnp.concatenate([to_1, met[TALL:]], axis=0), "side", 4, 1)
    gathered = []
    by_x = [swap(here, "shard", 4, 2) for here in (first, second)]
    by_core = [swap(here, "shard", 4, 1) for here in (first, second)]
    by_both = [swap(there, "shard", 4, 1) for there in by_x]
    gathered = [first, second, *by_core, *by_x, *by_both]
    packed, other, layout, step = pack_up(
        gathered, weights, ROW_STEPS[-1], ROW_STEPS[:-1]
    )
    stay, leave = lax.switch(
        step[0],
        [functools.partial(feed_forward, rows) for rows in ROW_STEPS],
        layout, packed, other, w_up, w_down,
    )
    back = swap(leave, "shard", 4, 1)
    quarter = back.shape[0] // 4
    piece = quarter // 2
    cuts = [slice(at, at + quarter) for at in range(0, 4 * quarter, quarter)]
    sums = [added(stay[cut], back[cut]) for cut in cuts]
    far = added(sums[2], swap(sums[0], "shard", 4, 2))
    near = added(sums[3], swap(sums[1], "shard", 4, 2))
    home = near[:piece], near[piece:], far[:piece], far[piece:]
    blocks = [home[0]] + [swap(home[mask], "side", 4, mask) for mask in (1, 2, 3)]
    mixed = [*mixed_near, *mixed_far]
    return finish(back_picks, mixed, [squares_far, squares_near], blocks)


def attend_slots(queries, new_kv, pool_pages, page_rows, lengths):
    slot_count = queries.shape[0]
    positions = page_rows.shape[1] * pool_pages.shape[1]
    fetched = pool_pages[page_rows].reshape(slot_count, positions, 2, KV_HEADS, HEAD)
    fresh_kv = new_kv.reshape(slot_count, 2, KV_HEADS, HEAD)
    query_heads = queries.reshape(slot_count, KV_HEADS, GROUP, HEAD)
    score_scale = 1.0 / math.sqrt(HEAD)
    scores = (
        jnp.einsum("sgqd,slgd->sgql", query_heads, fetched[:, :, 0], preferred_element_type=f32)
        * score_scale
    )
    own_score = (
        jnp.einsum("sgqd,sgd->sgq", query_heads, fresh_kv[:, 0], preferred_element_type=f32)
        * score_scale
    )
    visible = (jnp.arange(positions, dtype=i32)[None, :] < lengths[:, None])[:, None, None, :]
    scores = jnp.where(visible, scores, -1e30)
    highest = jnp.maximum(jnp.max(scores, axis=-1), own_score)
    weights = jnp.where(visible, jnp.exp(scores - highest[..., None]), 0.0)
    own_weight = jnp.exp(own_score - highest)
    denominator = jnp.sum(weights, axis=-1) + own_weight
    probabilities = (weights / denominator[..., None]).astype(bf16)
    own_prob = (own_weight / denominator).astype(bf16).astype(f32)
    attended = jnp.einsum(
        "sgql,slgd->sgqd", probabilities, fetched[:, :, 1], preferred_element_type=f32
    )
    attended = attended + own_prob[..., None] * fresh_kv[:, 1].astype(f32)[:, :, None, :]
    return attended.reshape(slot_count, -1)


def any_shards(queries, new_kv, kv_pool, page_table, ctx_len, residual_in, norm_gain, w_up, w_down):
    attended = attend_slots(queries, new_kv, kv_pool, page_table, ctx_len)
    mixed_rows = residual_in.astype(f32) + attended
    mean_square = jnp.mean(mixed_rows * mixed_rows, axis=-1, keepdims=True)
    normed = (mixed_rows * lax.rsqrt(mean_square + epsilon) * norm_gain.astype(f32)).astype(bf16)
    live_mask = ctx_len > 0
    spread = lax.all_to_all(normed, "side", split_axis=1, concat_axis=0, tiled=True)
    up_partial = jnp.dot(
        lax.all_gather(spread, "shard", axis=0, tiled=True), w_up, preferred_element_type=f32
    )
    lifted = lax.psum(up_partial, "side")
    clipped = jnp.maximum(lifted, 0.0)
    active = (clipped * clipped).astype(bf16)
    down_share = lax.psum_scatter(
        jnp.dot(active, w_down, preferred_element_type=f32).astype(bf16),
        "shard",
        scatter_dimension=0,
        tiled=True,
    )
    returned = lax.all_to_all(down_share, "side", split_axis=0, concat_axis=1, tiled=True)
    returned = jnp.where(live_mask[:, None], returned.astype(f32), 0.0)
    return (mixed_rows + returned).astype(bf16)


def solution(mesh):
    rows = ("grp", "side", "shard")
    placed = (
        P(rows, None),
        P(rows, None),
        P(rows, None, None),
        P(rows, None),
        P(rows),
        P(rows, None),
        P(),
        P("side", "shard"),
        P("shard", "side"),
    )
    square = mesh.shape["side"] == 4 and mesh.shape["shard"] == 4
    return jax.shard_map(
        line_shards if square else any_shards,
        mesh=mesh,
        in_specs=placed,
        out_specs=P(rows, None),
        check_vma=False,
    )
```
